128 devices in a mesh: grp: 4 (over y), gy: 32 (over x, z, core).
Axes of the slice: x: 4, y: 4, z: 4, core: 2. Of those that a mesh axis runs over, the one named last changes fastest.
Arguments:
- right_side: float32 [5, 4, 1024, 512], P(None, None, 'gy', 'grp'), may hold values from -7 to 7
- potential: float32 [4, 1024, 512], P(None, 'gy', 'grp'), may hold values from -3 to 3
- capacity: float32 [4, 1024, 512], P(None, 'gy', 'grp'), may hold values from 0.05 to 0.5
- diffusivity: float32 [5, 4], replicated, may hold values from 0.2 to 2
- material: int32 [4, 1024, 512], P(None, 'gy', 'grp'), may hold values from 0 to 3
- coarse_map: int32 [32, 4, 4], P('gy', 'grp'), may hold values from 0 to 511
- coarse_inverse: float32 [512, 5, 5], P(('grp', 'gy')), as said below
Outputs:
- solution_field: float32 [5, 4, 1024, 512], P(None, None, 'gy', 'grp')
- residual: float32 [5, 4, 1024, 512], P(None, None, 'gy', 'grp')
- smoothed: float32 [5, 4, 1024, 512], P(None, None, 'gy', 'grp')
The draws below stay inside these ranges and needn't reach their ends.
Inputs may be any that keep to these rules, and one draw needn't show every extreme that they name: `coarse_inverse`: each 5 x 5 block is symmetric, with a positive diagonal entry larger than the sum of the magnitudes of the other entries of its row.
All inputs are finite; a program needn't handle non-finite values.
Results may differ from the reference program's by a relative error of at most 0.0003.
Values sent between devices are 32-bit elements; how exact they have to be, the bound alone decides.
No kernel may reach another device: no remote copies, remote signals or barrier semaphores. Data moves between devices by JAX's collectives and lax.ppermute only.
A program may use at most 64 MiB of HBM per device.

```python
import math
import jax
import jax.numpy as jnp
from jax import lax

S = 5
L = 4
MATS = 4
SWEEPS = 4
ITERS = 2
CX = 128
CY = 32
NX = 512
NY = 1024
NC = 512
N_GRP = 4
N_GY = 32


def draw_right_side(key, part):
    key = jax.random.fold_in(key, 11)
    jitter_key, offset_key = jax.random.split(key)
    extent = (S, L, NY, NX)
    row_frac = jnp.arange(NY, dtype=jnp.float32)[:, None] / NY
    col_frac = jnp.arange(NX, dtype=jnp.float32)[None, :] / NX
    profile = 1.0 + 0.5 * jnp.sin(2.0 * math.pi * (2.0 * row_frac + 3.0 * col_frac))
    jitter = jnp.clip(jax.random.normal(jitter_key, extent, jnp.float32), -5.0, 5.0)
    offset = jax.random.uniform(offset_key, (S, L, 1, 1), jnp.float32, -1.0, 1.0)
    return jitter + offset * profile


def draw_coarse_inverse(key, part):
    key = jax.random.fold_in(key, 23)
    lead_key, cross_key = jax.random.split(key)
    leading = jax.random.uniform(lead_key, (NC, S), jnp.float32, 1.0, 2.0)
    cross = jax.random.uniform(cross_key, (NC, S, S), jnp.float32, -1.0, 1.0)
    identity = jnp.eye(S, dtype=jnp.float32)
    cross = 0.1 * (cross + jnp.swapaxes(cross, 1, 2)) * (1.0 - identity)
    blocks = cross + leading[:, :, None] * identity
    return blocks * (MATS / (L * CY * CX))


def touch_ends(values, stream_key, least, top_value):
    longest = values.shape.index(max(values.shape))
    spots = []
    for shift in (0, 1):
        where = [jax.random.randint(jax.random.fold_in(stream_key, axis), (), 0, length) for axis, length in enumerate(values.shape)]
        where[longest] = (where[longest] + shift) % values.shape[longest]
        spots.append(tuple(where))
    return values.at[spots[0]].set(least).at[spots[1]].set(top_value)


def steps_of(own_key, shape, cuts, least, high):
    def one(dim, parts):
        heights = jax.random.uniform(jax.random.fold_in(jax.random.fold_in(own_key, 6), dim), (parts,), jnp.float32, least / len(cuts), high / len(cuts))
        return jnp.repeat(jnp.exp(heights), shape[dim] // parts).reshape((-1,) + (1,) * (len(shape) - dim - 1))

    level = one(*cuts[0])
    for cut in cuts[1:]:
        level = level * one(*cut)
    return level


def scatter_about(key, shape, spread, most, cuts=(), held_as=jnp.bfloat16):
    result = jax.random.normal(key, shape, jnp.float32) * spread
    if len(cuts) > 0:
        result = steps_of(key, shape, cuts, -0.22, 0.18) * result
    return jnp.clip(result, min=-most, max=most).astype(held_as)


def setup_inputs(seed: int = 0) -> dict:
    key_of = jax.random.split(jax.random.key(seed), 8)
    right_side = draw_right_side(jax.random.fold_in(key_of[7], 71), 0)
    potential = scatter_about(key_of[1], (L, NY, NX), 1.0, 3.0, ((1, 32), (2, 4)), jnp.float32)
    capacity = jnp.clip(jnp.exp(math.log(0.5) - 2.3025851 * jax.random.uniform(key_of[2], (L, NY, NX), jnp.float32) ** steps_of(key_of[2], (L, NY, NX), ((1, 32), (2, 4)), -0.2, 0.2)), 0.05, 0.5)
    diffusivity = jnp.clip(jnp.exp(jax.random.uniform(key_of[3], (S, MATS), jnp.float32, math.log(0.2), math.log(2.0))), 0.2, 2.0)
    material = touch_ends(jax.random.randint(key_of[4], (L, NY, NX), 0, MATS), jax.random.fold_in(key_of[4], 1), 0, MATS - 1).astype(jnp.int32)
    coarse_map = touch_ends(jax.random.randint(key_of[5], (N_GY, N_GRP, MATS), 0, NC), jax.random.fold_in(key_of[5], 1), 0, NC - 1).astype(jnp.int32)
    coarse_inverse = draw_coarse_inverse(jax.random.fold_in(key_of[7], 71), 0)
    return {"right_side": right_side, "potential": potential, "capacity": capacity, "diffusivity": diffusivity, "material": material, "coarse_map": coarse_map, "coarse_inverse": coarse_inverse}


VALENCE = (1.0, -1.0, 2.0, -2.0, 1.0)
VERTICAL = 0.5
DAMPING = 2.0 / 3.0


def harmonic(lower_w, upper_w):
    return 2.0 * lower_w * upper_w / (lower_w + upper_w)


def cell_weights(diffusivity, material, potential):
    weights = jnp.zeros((diffusivity.shape[0],) + material.shape, diffusivity.dtype)
    for mat_id in range(MATS):
        weights = weights + jnp.where(material[None] == mat_id, diffusivity[:, mat_id][:, None, None, None], 0.0)
    charge = jnp.asarray(VALENCE, diffusivity.dtype)[:, None, None, None]
    return weights * jnp.exp(-0.5 * charge * potential[None])


def pad_last(array, before, after):
    return jnp.pad(array, ((0, 0), (0, 0), (0, 0), (before, after)))


def pad_layer(array, before, after):
    return jnp.pad(array, ((0, 0), (before, after), (0, 0), (0, 0)))


def build_operator(weights, capacity):
    gy_edge = harmonic(weights, jnp.roll(weights, -1, axis=2))
    gx_edge = harmonic(weights[..., :-1], weights[..., 1:])
    gz_edge = VERTICAL * harmonic(weights[:, :-1], weights[:, 1:])
    diagonal = capacity[None] + gy_edge + jnp.roll(gy_edge, 1, axis=2)
    diagonal = diagonal + pad_last(gx_edge, 0, 1) + pad_last(gx_edge, 1, 0)
    diagonal = diagonal + pad_layer(gz_edge, 0, 1) + pad_layer(gz_edge, 1, 0)
    return gy_edge, gx_edge, gz_edge, diagonal


def apply_operator(field, tables):
    gy_edge, gx_edge, gz_edge, diagonal = tables
    beside_y = gy_edge * jnp.roll(field, -1, axis=2) + jnp.roll(gy_edge * field, 1, axis=2)
    beside_x = pad_last(gx_edge * field[..., 1:], 0, 1) + pad_last(gx_edge * field[..., :-1], 1, 0)
    beside_z = pad_layer(gz_edge * field[:, 1:], 0, 1) + pad_layer(gz_edge * field[:, :-1], 1, 0)
    return diagonal * field - (beside_y + beside_x + beside_z)


def coarse_field(resid, material, coarse_map, coarse_inverse):
    species = resid.shape[0]
    blocked_r = resid.reshape(species, L, N_GY, CY, N_GRP, CX)
    blocked_m = material.reshape(L, N_GY, CY, N_GRP, CX)
    sums = jnp.stack([jnp.sum(jnp.where(blocked_m[None] == mat_id, blocked_r, 0.0), axis=(1, 3, 5)) for mat_id in range(MATS)])
    sums = jnp.transpose(sums, (2, 3, 0, 1)).reshape(-1, species)
    flat_map = coarse_map.reshape(-1).astype(jnp.int32)
    coarse_res = jnp.zeros((NC, species), resid.dtype).at[flat_map].add(sums)
    coarse_sol = jnp.einsum("qst,qt->qs", coarse_inverse, coarse_res, precision=lax.Precision.HIGHEST)
    picked = coarse_sol[flat_map].reshape(N_GY, N_GRP, MATS, species)
    field = jnp.zeros_like(blocked_r)
    for mat_id in range(MATS):
        values = jnp.transpose(picked[:, :, mat_id, :], (2, 0, 1))[:, None, :, None, :, None]
        field = field + jnp.where(blocked_m[None] == mat_id, values, 0.0)
    return field.reshape(resid.shape)


def precondition(resid, tables, material, coarse_map, coarse_inverse):
    diagonal = tables[3]
    smooth = DAMPING * resid / diagonal
    for sweep_no in range(1, SWEEPS):
        smooth = smooth + DAMPING * (resid - apply_operator(smooth, tables)) / diagonal
    return smooth + coarse_field(resid, material, coarse_map, coarse_inverse)


def reference(right_side, potential, capacity, diffusivity, material, coarse_map, coarse_inverse):
    weights = cell_weights(diffusivity, material, potential)
    tables = build_operator(weights, capacity)
    solution_field = jnp.zeros_like(right_side)
    residual = right_side
    smoothed = precondition(residual, tables, material, coarse_map, coarse_inverse)
    direction = smoothed
    inner_now = jnp.sum(residual * smoothed)
    for step_no in range(ITERS):
        image = apply_operator(direction, tables)
        alpha = inner_now / jnp.sum(direction * image)
        solution_field = solution_field + alpha * direction
        residual = residual - alpha * image
        smoothed = precondition(residual, tables, material, coarse_map, coarse_inverse)
        if step_no + 1 < ITERS:
            inner_next = jnp.sum(residual * smoothed)
            direction = smoothed + (inner_next / inner_now) * direction
            inner_now = inner_next
    return solution_field, residual, smoothed
```

```python
import jax
import jax.numpy as jnp
from jax import lax
from jax.sharding import PartitionSpec as P

MATS = 4
SWEEPS = 4
VALENCE = (1.0, -1.0, 2.0, -2.0, 1.0)
VERTICAL = 0.5
DAMPING = 2.0 / 3.0
HALO = 12
BOTH = ("grp", "gy")
HIGH = lax.Precision.HIGHEST


def with_halo(block, sides, width):
    for axis, dim in sides:
        count = lax.axis_size(axis)
        forward = [(i, (i + 1) % count) for i in range(count)]
        backward = [(target, source) for source, target in forward]
        low = lax.ppermute(
            lax.slice_in_dim(block, block.shape[dim] - width, None, axis=dim), axis, forward
        )
        high = lax.ppermute(lax.slice_in_dim(block, 0, width, axis=dim), axis, backward)
        block = jnp.concatenate([low, block, high], axis=dim)
    return block


def harmonic(lower_w, upper_w):
    return 2.0 * lower_w * upper_w / (lower_w + upper_w)


def to_all(row):
    count = lax.axis_size("grp") * lax.axis_size("gy")
    return lax.all_to_all(jnp.broadcast_to(row[None], (count,) + row.shape), BOTH, 0, 0, tiled=True)


def body(right_side, potential, capacity, diffusivity, material, coarse_map, coarse_inverse):
    species, layers, rows, cols = right_side.shape
    n_grp, n_gy = lax.axis_size("grp"), lax.axis_size("gy")
    total = n_grp * n_gy
    grid_cols = cols * n_grp
    own_masks = jnp.stack([(material == m).astype(jnp.float32) for m in range(MATS)])

    def by_material(field):
        return jnp.stack([jnp.sum(own_masks[m][None] * field, axis=(1, 2, 3)) for m in range(MATS)])

    first = jnp.concatenate(
        [
            by_material(right_side).reshape(-1),
            coarse_map.reshape(-1).astype(jnp.float32),
            coarse_inverse.reshape(-1),
        ]
    )
    planes = jnp.concatenate(
        [
            right_side.reshape(species * layers, rows, cols),
            potential,
            capacity,
            material.astype(jnp.float32),
        ]
    )
    wide = with_halo(planes, (("grp", 2), ("gy", 1)), HALO)
    got = to_all(first)
    n_b = species * layers
    b = wide[:n_b].reshape((species, layers) + wide.shape[1:])
    pot = wide[n_b : n_b + layers]
    cap = wide[n_b + layers : n_b + 2 * layers]
    mat = wide[n_b + 2 * layers :]

    sums_b = got[:, :20].reshape(total, MATS, species)
    maps = got[:, 20:24].astype(jnp.int32)
    inverse = got[:, 24:124].reshape(total * 4, species, species)
    count = inverse.shape[0]
    onehot = (maps.reshape(-1)[:, None] == jnp.arange(count)[None]).astype(jnp.float32)

    def coarse(sums):
        res = jnp.einsum("uq,us->qs", onehot, sums.reshape(-1, species), precision=HIGH)
        sol = jnp.einsum("qst,qt->qs", inverse, res, precision=HIGH)
        return jnp.einsum("uq,qs->us", onehot, sol, precision=HIGH).reshape(total, MATS, species)

    me_x, me_y = lax.axis_index("grp"), lax.axis_index("gy")

    wide_masks = [(mat == m) for m in range(MATS)]
    weights = jnp.zeros(b.shape, jnp.float32)
    for m in range(MATS):
        weights = weights + jnp.where(wide_masks[m][None], diffusivity[:, m][:, None, None, None], 0.0)
    charge = jnp.asarray(VALENCE, jnp.float32)[:, None, None, None]
    weights = weights * jnp.exp(-0.5 * charge * pot[None])
    gy = harmonic(weights[:, :, :-1], weights[:, :, 1:])
    gx = harmonic(weights[..., :-1], weights[..., 1:])
    left_cell = me_x * cols - HALO + jnp.arange(gx.shape[-1])
    gx = jnp.where((left_cell >= 0) & (left_cell <= grid_cols - 2), gx, 0.0)
    gz = VERTICAL * harmonic(weights[:, :-1], weights[:, 1:])

    def pads(edge, axis):
        before = [(0, 0)] * 4
        after = [(0, 0)] * 4
        before[axis], after[axis] = (1, 0), (0, 1)
        return jnp.pad(edge, after), jnp.pad(edge, before)

    diagonal = cap[None] + sum(p for a, e in ((2, gy), (3, gx), (1, gz)) for p in pads(e, a))
    scale = DAMPING / diagonal

    def apply(u):
        out = cap[None] * u
        for axis, edge in ((2, gy), (3, gx), (1, gz)):
            lo = lax.slice_in_dim(u, 0, u.shape[axis] - 1, axis=axis)
            hi = lax.slice_in_dim(u, 1, None, axis=axis)
            after, before = pads(edge * (lo - hi), axis)
            out = out + after - before
        return out

    def smooth(r):
        z = scale * r
        for _ in range(1, SWEEPS):
            z = z + scale * (r - apply(z))
        return z

    def own(u):
        return u[..., HALO : HALO + rows, HALO : HALO + cols]

    def spread(c):
        grid = c.reshape(n_grp, n_gy, MATS, species)
        ys = []
        for dy in (-1, 0, 1):
            xs = []
            for dx in (-1, 0, 1):
                v = grid[jnp.clip(me_x + dx, 0, n_grp - 1), (me_y + dy) % n_gy]
                xs.append(jnp.broadcast_to(v[..., None], v.shape + ((cols if dx == 0 else HALO),)))
            line = jnp.concatenate(xs, axis=-1)
            ys.append(jnp.broadcast_to(line[:, :, None], line.shape[:2] + ((rows if dy == 0 else HALO),) + line.shape[2:]))
        v = jnp.concatenate(ys, axis=2)
        field = jnp.zeros(b.shape, jnp.float32)
        for m in range(MATS):
            field = field + jnp.where(wide_masks[m][None], v[m][:, None], 0.0)
        return field

    c0 = coarse(sums_b)
    z0 = smooth(b) + spread(c0)
    w0 = apply(z0)
    u = smooth(w0)
    au = apply(u)

    row_id = jnp.arange(b.shape[2])[:, None]
    col_id = jnp.arange(b.shape[3])[None]
    in_rows = (row_id >= HALO) & (row_id < HALO + rows)
    in_cols = (col_id >= HALO) & (col_id < HALO + cols)
    blocks = []
    for m in range(MATS):
        h = apply(jnp.broadcast_to((wide_masks[m] & in_rows & in_cols)[None].astype(jnp.float32), b.shape))
        for region in (
            in_rows & in_cols,
            (row_id >= HALO + rows) & in_cols,
            in_rows & (col_id >= HALO + cols),
        ):
            for other in range(MATS):
                blocks.append(jnp.sum(jnp.where((wide_masks[other] & region)[None], h, 0.0), axis=(1, 2, 3)))
    blocks = jnp.stack(blocks)
    moments = jnp.stack(
        [jnp.sum(own(p) * own(q)) for p, q in ((b, z0), (z0, w0), (w0, u), (u, au))]
    )
    second = jnp.concatenate(
        [by_material(own(w0)).reshape(-1), by_material(own(au)).reshape(-1), blocks.reshape(-1), moments]
    )
    got2 = to_all(second)
    sums_w = got2[:, :20].reshape(total, MATS, species)
    sums_au = got2[:, 20:40].reshape(total, MATS, species)
    mats = got2[:, 40:280].reshape(n_grp, n_gy, MATS, 3, MATS, species)
    moments = jnp.sum(got2[:, 280:284], axis=0)
    c1 = coarse(sums_w)
    cg = c1.reshape(n_grp, n_gy, MATS, species)
    b_self, b_y, b_x = mats[:, :, :, 0], mats[:, :, :, 1], mats[:, :, :, 2]

    def times(mat4, vec):
        return jnp.sum(mat4 * vec[:, :, None], axis=3)

    def times_t(mat4, vec):
        return jnp.sum(mat4 * vec[:, :, :, None], axis=2)

    bc = (
        times(b_self, cg)
        + times(b_y, jnp.roll(cg, -1, axis=1))
        + jnp.roll(times_t(b_y, cg), 1, axis=1)
        + times(b_x, jnp.roll(cg, -1, axis=0))
        + jnp.roll(times_t(b_x, cg), 1, axis=0)
    ).reshape(total, MATS, species)
    c2 = coarse(sums_au + bc)
    m0 = moments[0]
    m1 = moments[1]
    m2 = moments[2] + jnp.sum(sums_w * c1)
    m3 = moments[3] + 2.0 * jnp.sum(sums_au * c1) + jnp.sum(bc * c1)
    a0 = m0 / m1
    rz1 = m0 - 2.0 * a0 * m1 + a0 * a0 * m2
    beta = rz1 / m0
    g = 1.0 + beta
    a1 = rz1 / (g * g * m1 - 2.0 * a0 * g * m2 + a0 * a0 * m3)

    v1 = u + spread(c1)
    w1 = apply(v1)
    v2 = smooth(w1) + spread(c2)
    z0, w0, v1, w1, v2 = own(z0), own(w0), own(v1), own(w1), own(v2)
    ca = a0 + a1 * g
    cb = a1 * a0
    solution_field = ca * z0 - cb * v1
    residual = right_side - ca * w0 + cb * w1
    smoothed = z0 - ca * v1 + cb * v2
    return (solution_field, residual, smoothed)


def solution(mesh):
    placed = (
        P(None, None, "gy", "grp"),
        P(None, "gy", "grp"),
        P(None, "gy", "grp"),
        P(),
        P(None, "gy", "grp"),
        P("gy", "grp", None),
        P(("grp", "gy"), None, None),
    )
    return jax.shard_map(
        body,
        mesh=mesh,
        in_specs=placed,
        out_specs=(P(None, None, "gy", "grp"),) * 3,
        check_vma=False,
    )
```

```python
import functools

import jax
import jax.numpy as jnp
from jax import lax
from jax.experimental import pallas as pl
from jax.experimental.pallas import tpu as pltpu
from jax.sharding import PartitionSpec as P

SPECIES = 5
LAYERS = 4
MATS = 4
FIELDS = SPECIES * LAYERS
PLANES = FIELDS + 3 * LAYERS
ROWS = 32
COLS = 128
N_GRP = 4
N_GY = 32
TOTAL = N_GRP * N_GY
NC = 512
DAMPING = 2.0 / 3.0
BOTH = ("grp", "gy")

HALO = 12
PER = 10
GROUPS = -(-PLANES // PER)
RHALO = 16
PAD = 8
WIDE = 2 * COLS
TALL = ROWS + 2 * RHALO + 2 * PAD
TOP = PAD + RHALO
F32 = jnp.float32

G_RW, G_RAU, G_S, G_CY, G_CX, G_MOM = 0, 4, 8, 14, 30, 46
ROW_CAP = 250
MAP_LANE = 20
INV_LANE = 24


def lanes(shape):
    return lax.broadcasted_iota(jnp.int32, shape, 1)


def subs(shape):
    return lax.broadcasted_iota(jnp.int32, shape, 0)


def pack_kernel(b, pot, cap, mat, to_low, to_high):
    lane = lanes((ROWS, COLS))
    for g in range(GROUPS):
        low = jnp.zeros((ROWS, COLS), F32)
        high = jnp.zeros((ROWS, COLS), F32)
        for j in range(min(PER, PLANES - g * PER)):
            v = plane_of(b, pot, cap, mat, g * PER + j)
            inside = (lane >= HALO * j) & (lane < HALO * (j + 1))
            low = jnp.where(inside, turn(v, HALO * j), low)
            high = jnp.where(inside, turn(v, HALO * j + HALO), high)
        to_low[g] = low
        to_high[g] = high


def turn(v, shift):
    shift = shift % v.shape[1]
    return v if shift == 0 else pltpu.roll(v, shift, 1)


def plane_of(b, pot, cap, mat, k):
    if k < FIELDS:
        return b[k]
    which, layer = divmod(k - FIELDS, LAYERS)
    return (pot, cap, mat)[which][layer].astype(F32)


def place(rows):
    n = rows.shape[0]
    total = jnp.sum(rows, axis=1, keepdims=True)
    spread = jnp.where(lanes((n, COLS)) == subs((n, COLS)), total, 0.0)
    return jnp.sum(spread, axis=0, keepdims=True)


def fold(v):
    return jnp.sum(v, axis=0, keepdims=True)


def sums_kernel(b, mat, tail, out, acc):
    acc[...] = jnp.zeros(acc.shape, F32)
    for s in range(SPECIES):
        for m in range(MATS):
            total = jnp.zeros((ROWS, COLS), F32)
            for l in range(LAYERS):
                total = total + jnp.where(mat[l] == m, b[s * LAYERS + l], 0.0)
            acc[m * SPECIES + s : m * SPECIES + s + 1, :] = fold(total)
    row = place(acc[...]) + tail[...]
    out[...] = jnp.broadcast_to(row, (TOTAL, COLS))


def rows_kernel(b, pot, cap, mat, from_low, from_high, to_low, to_high):
    for k in range(PLANES):
        v = plane_of(b, pot, cap, mat, k)
        to_low[k] = v[:RHALO]
        to_high[k] = v[ROWS - RHALO :]
    for g in range(GROUPS):
        for i, part in enumerate((from_low, from_high)):
            k = PLANES + i * GROUPS + g
            to_low[k] = part[g, :RHALO]
            to_high[k] = part[g, ROWS - RHALO :]


def unpack_halo(low, high, j, fill):
    shape = low.shape
    lane = lanes(shape)
    right = turn(high, -HALO * j)
    left = turn(low, -HALO * (j + 1))
    return jnp.where(lane < HALO, right, jnp.where(lane >= COLS - HALO, left, fill))


def a_tile(src, cap, gy, gx, gz, s, row):
    base = s * LAYERS
    here = pl.ds(row, 8)
    below = pl.ds(row - 1, 8)
    above = pl.ds(row + 1, 8)
    us, outs = [], []
    flux_z = None
    for l in range(LAYERS):
        k = base + l
        u = src[k, here, :]
        if l == 0:
            nxt = u
        u = nxt
        flux_x = gx[k, here, :] * (u - pltpu.roll(u, WIDE - 1, 1))
        out = cap[l, here, :] * u + (flux_x - pltpu.roll(flux_x, 1, 1))
        out = out + gy[k, here, :] * (u - src[k, above, :])
        out = out + gy[k, below, :] * (u - src[k, below, :])
        if flux_z is not None:
            out = out - flux_z
        if l + 1 < LAYERS:
            nxt = src[k + 1, here, :]
            flux_z = gz[k, here, :] * (u - nxt)
            out = out + flux_z
        us.append(u)
        outs.append(out)
    return us, outs


def tile_rows(first, last):
    return [PAD + 8 * t for t in range(first, last + 1)]


def sweep(src, resid, dst, ops, tiles):
    cap, gy, gx, gz, scale = ops

    @pl.loop(0, SPECIES)
    def _(s):
        for row in tiles:
            us, outs = a_tile(src, cap, gy, gx, gz, s, row)
            for l in range(LAYERS):
                k = s * LAYERS + l
                here = pl.ds(row, 8)
                dst[k, here, :] = us[l] + scale[k, here, :] * (resid[k, here, :] - outs[l])


def image(src, dst, ops, tiles):
    cap, gy, gx, gz, _ = ops

    @pl.loop(0, SPECIES)
    def _(s):
        for row in tiles:
            _, outs = a_tile(src, cap, gy, gx, gz, s, row)
            for l in range(LAYERS):
                dst[s * LAYERS + l, pl.ds(row, 8), :] = outs[l]


def start_sweep(resid, dst, scale, tiles):
    @pl.loop(0, SPECIES)
    def _(s):
        for row in tiles:
            for l in range(LAYERS):
                k = s * LAYERS + l
                here = pl.ds(row, 8)
                dst[k, here, :] = scale[k, here, :] * resid[k, here, :]


def split3(x):
    hi = x.astype(jnp.bfloat16)
    rest = x - hi.astype(F32)
    mid = rest.astype(jnp.bfloat16)
    lo = (rest - mid.astype(F32)).astype(jnp.bfloat16)
    return jnp.concatenate([hi, mid, lo], axis=0)


def exact_dot(x, onehot):
    n = x.shape[0]
    y = jnp.dot(
        jnp.concatenate([split3(x)], axis=0), onehot, preferred_element_type=F32
    )
    return y[:n] + y[n : 2 * n] + y[2 * n :]


def build_scatter(got, onehot):
    for m in range(MATS):
        col = jnp.broadcast_to(got[:, MAP_LANE + m : MAP_LANE + m + 1], (TOTAL, COLS))
        for k in range(4):
            target = (lanes((TOTAL, COLS)) + k * COLS).astype(F32)
            onehot[m * TOTAL : (m + 1) * TOTAL, k * COLS : (k + 1) * COLS] = jnp.where(
                col == target, 1.0, 0.0
            ).astype(jnp.bfloat16)


def build_gather(turned, onehot):
    for m in range(MATS):
        row = jnp.broadcast_to(turned[MAP_LANE + m : MAP_LANE + m + 1, :], (COLS, TOTAL))
        for k in range(4):
            target = (subs((COLS, TOTAL)) + k * COLS).astype(F32)
            onehot[k * COLS : (k + 1) * COLS, m * TOTAL : (m + 1) * TOTAL] = jnp.where(
                row == target, 1.0, 0.0
            ).astype(jnp.bfloat16)


def build_near(got, onehot):
    gx, gy = lax.axis_index("grp"), lax.axis_index("gy")
    lane = lanes((1, COLS))
    row = jnp.full((1, COLS), -1.0, F32)
    for iy in range(3):
        y = lax.rem(gy + (N_GY - 1 + iy), N_GY)
        for ix in range(3):
            x = jnp.clip(gx + (ix - 1), 0, N_GRP - 1)
            region = iy * 3 + ix
            here = got[pl.ds(x * N_GY + y, 1), :]
            inside = (lane >= region * MATS) & (lane < (region + 1) * MATS)
            row = jnp.where(inside, turn(here, region * MATS - MAP_LANE), row)
    for k in range(4):
        target = (subs((COLS, COLS)) + k * COLS).astype(F32)
        onehot[k * COLS : (k + 1) * COLS, :] = jnp.where(
            jnp.broadcast_to(row, (COLS, COLS)) == target, 1.0, 0.0
        ).astype(jnp.bfloat16)


def coarse_solve(sums, turned, scatter):
    res = exact_dot(sums, scatter[...])
    parts = []
    for k in range(4):
        total = None
        for t in range(SPECIES):
            start = INV_LANE + k * SPECIES * SPECIES + t * SPECIES
            term = turned[start : start + 8, :] * res[t : t + 1, k * COLS : (k + 1) * COLS]
            total = term if total is None else total + term
        parts.append(total)
    sol = jnp.concatenate(parts, axis=1)
    return jnp.where(subs(sol.shape) < SPECIES, sol, 0.0)


def local_sums(turned, group):
    x = jnp.concatenate(
        [turned[(group + m) * SPECIES : (group + m) * SPECIES + 8, :] for m in range(MATS)], axis=1
    )
    return jnp.where(subs(x.shape) < SPECIES, x, 0.0)


def spread_values(near, values):
    lane = lanes((8, COLS))
    for iy in range(3):
        for m in range(MATS):
            cols = [
                jnp.broadcast_to(
                    near[:, (iy * 3 + ix) * MATS + m : (iy * 3 + ix) * MATS + m + 1], (8, COLS)
                )
                for ix in range(3)
            ]
            values[iy * MATS + m, :, 0:COLS] = cols[1]
            values[iy * MATS + m, :, COLS:WIDE] = jnp.where(lane < COLS // 2, cols[2], cols[0])


def region_of(row):
    return 0 if row < TOP else (1 if row < TOP + ROWS else 2)


def coarse_at(values, mat_tile, s, row):
    iy = region_of(row)
    v = [
        jnp.broadcast_to(values[iy * MATS + m, pl.ds(s, 1), :], mat_tile.shape) for m in range(MATS)
    ]
    out = jnp.where(mat_tile == 1.0, v[1], v[0])
    out = jnp.where(mat_tile == 2.0, v[2], out)
    return jnp.where(mat_tile == 3.0, v[3], out)


def fill_plane(dst, index, k, own, x_low, x_high, y_low, y_high, fill):
    g, j = divmod(k, PER)
    dst[index, PAD : PAD + RHALO, 0:COLS] = y_low[k]
    dst[index, TOP : TOP + ROWS, 0:COLS] = own
    dst[index, TOP + ROWS : TOP + ROWS + RHALO, 0:COLS] = y_high[k]
    dst[index, PAD : PAD + RHALO, COLS:WIDE] = unpack_halo(
        y_low[PLANES + g], y_low[PLANES + GROUPS + g], j, fill
    )
    dst[index, TOP : TOP + ROWS, COLS:WIDE] = unpack_halo(x_low[g], x_high[g], j, fill)
    dst[index, TOP + ROWS : TOP + ROWS + RHALO, COLS:WIDE] = unpack_halo(
        y_high[PLANES + g], y_high[PLANES + GROUPS + g], j, fill
    )


def harmonic(a, b):
    return 2.0 * a * b / (a + b)


def first_kernel(
    diff, b, pot, cap, mat, x_low, x_high, y_low, y_high, got,
    second, cap_w, mat_w, gy, gx, gz, scale, z0_out, w0_out, u_out,
    b_w, w, za, zb, w0, scatter, near_hot, turned, values, acc,
):
    halves = (x_low, x_high, y_low, y_high)
    for k in range(FIELDS):
        fill_plane(b_w, k, k, b[k], *halves, 0.0)
    for l in range(LAYERS):
        fill_plane(za, l, FIELDS + l, pot[l], *halves, 0.0)
        fill_plane(cap_w, l, FIELDS + LAYERS + l, cap[l], *halves, 1.0)
        fill_plane(mat_w, l, FIELDS + 2 * LAYERS + l, mat[l].astype(F32), *halves, 0.0)

    for row in tile_rows(0, 7):
        for l in range(LAYERS):
            here = pl.ds(row, 8)
            m = mat_w[l, here, :]
            is1, is2, is3 = m == 1.0, m == 2.0, m == 3.0
            down = jnp.exp(-0.5 * za[l, here, :])
            up = jnp.exp(0.5 * za[l, here, :])
            drift = (down, up, down * down, up * up, down)
            for s in range(SPECIES):
                d = jnp.where(is1, diff[s, 1], diff[s, 0])
                d = jnp.where(is2, diff[s, 2], d)
                d = jnp.where(is3, diff[s, 3], d)
                w[s * LAYERS + l, here, :] = d * drift[s]

    me_x = lax.axis_index("grp")
    lane = lanes((8, WIDE))
    closed = ((lane == COLS - 1) & (me_x == N_GRP - 1)) | ((lane == WIDE - 1) & (me_x == 0))

    @pl.loop(0, SPECIES)
    def _(s):
        for row in tile_rows(0, 7):
            here, above = pl.ds(row, 8), pl.ds(row + 1, 8)
            for l in range(LAYERS):
                k = s * LAYERS + l
                c = w[k, here, :]
                gy[k, here, :] = harmonic(c, w[k, above, :])
                gx[k, here, :] = jnp.where(closed, 0.0, harmonic(c, pltpu.roll(c, WIDE - 1, 1)))
                if l + 1 < LAYERS:
                    gz[k, here, :] = 0.5 * harmonic(c, w[k + 1, here, :])
        for row in tile_rows(0, 7):
            here, below = pl.ds(row, 8), pl.ds(row - 1, 8)
            for l in range(LAYERS):
                k = s * LAYERS + l
                ex = gx[k, here, :]
                d = cap_w[l, here, :] + gy[k, here, :] + gy[k, below, :] + ex + pltpu.roll(ex, 1, 1)
                if l + 1 < LAYERS:
                    d = d + gz[k, here, :]
                if l > 0:
                    d = d + gz[k - 1, here, :]
                scale[k, here, :] = DAMPING / d

    ops = (cap_w, gy, gx, gz, scale)
    all_tiles, mid, own = tile_rows(0, 7), tile_rows(1, 6), tile_rows(2, 5)

    turned[...] = got[...].T
    build_scatter(got, scatter)
    build_near(got, near_hot)
    sol = coarse_solve(local_sums(turned, 0), turned, scatter)
    spread_values(exact_dot(sol, near_hot[...]), values)

    start_sweep(b_w, za, scale, all_tiles)
    sweep(za, b_w, zb, ops, all_tiles)
    sweep(zb, b_w, za, ops, all_tiles)

    cap_o, gy_o, gx_o, gz_o, scale_o = ops

    @pl.loop(0, SPECIES)
    def _(s):
        for row in mid:
            here = pl.ds(row, 8)
            us, outs = a_tile(za, cap_o, gy_o, gx_o, gz_o, s, row)
            for l in range(LAYERS):
                k = s * LAYERS + l
                smooth = us[l] + scale[k, here, :] * (b_w[k, here, :] - outs[l])
                zb[k, here, :] = smooth + coarse_at(values, mat_w[l, here, :], s, row)

    for k in range(FIELDS):
        z0_out[k] = zb[k, TOP : TOP + ROWS, 0:COLS]
    image(zb, w0, ops, mid)
    for k in range(FIELDS):
        w0_out[k] = w0[k, TOP : TOP + ROWS, 0:COLS]
    start_sweep(w0, za, scale, mid)
    sweep(za, w0, zb, ops, mid)
    sweep(zb, w0, za, ops, mid)
    sweep(za, w0, u_out, ops, mid)

    acc[...] = jnp.zeros(acc.shape, F32)
    own_lane = lanes((8, COLS))
    sub = subs((8, COLS))

    @pl.loop(0, SPECIES)
    def _(s):
        def keep(group, v):
            acc[pl.ds(group * SPECIES + s, 1), :] = fold(v)

        zero = jnp.zeros((8, COLS), F32)
        rw, rau, mom = [zero] * MATS, [zero] * MATS, [zero] * 4
        pairs, cy, cx = [zero] * 6, [zero] * 16, [zero] * 16
        codes = (3.0, 5.0, 9.0, 6.0, 10.0, 12.0)

        def power(m):
            p = jnp.where(m == 1.0, 2.0, 1.0)
            p = jnp.where(m == 2.0, 4.0, p)
            return jnp.where(m == 3.0, 8.0, p)

        for row in own:
            here = pl.ds(row, 8)
            above = pl.ds(row + 1, 8)
            us, outs = a_tile(u_out, cap_o, gy_o, gx_o, gz_o, s, row)
            side_g, side_c = zero, zero - 1.0
            for l in range(LAYERS):
                k = s * LAYERS + l
                m_wide = mat_w[l, here, :]
                m = m_wide[:, :COLS]
                u, au = us[l][:, :COLS], outs[l][:, :COLS]
                wv, zv, bv = w0_out[k, row - TOP : row - TOP + 8, :], z0_out[k, row - TOP : row - TOP + 8, :], b[k, row - TOP : row - TOP + 8, :]
                mom[0] = mom[0] + bv * zv
                mom[1] = mom[1] + zv * wv
                mom[2] = mom[2] + wv * u
                mom[3] = mom[3] + u * au
                for i in range(MATS):
                    is_i = m == float(i)
                    rw[i] = rw[i] + jnp.where(is_i, wv, 0.0)
                    rau[i] = rau[i] + jnp.where(is_i, au, 0.0)
                m_y = mat_w[l, above, 0:COLS]
                m_x = pltpu.roll(m_wide, WIDE - 1, 1)[:, :COLS]
                ey, ex = gy[k, here, 0:COLS], gx[k, here, 0:COLS]
                p = power(m)
                last = row == own[-1]
                code = p + power(m_y)
                if last:
                    code = jnp.where(sub == 7, 0.0, code)
                kinds = [(code, ey), (jnp.where(own_lane == COLS - 1, 0.0, p + power(m_x)), ex)]
                if l + 1 < LAYERS:
                    kinds.append((p + power(mat_w[l + 1, here, 0:COLS]), gz[k, here, 0:COLS]))
                for code, edge in kinds:
                    for i in range(6):
                        pairs[i] = pairs[i] + jnp.where(code == codes[i], edge, 0.0)
                if last:
                    code = jnp.where(sub == 7, m * 4.0 + m_y, -1.0)
                    for i in range(16):
                        cy[i] = cy[i] + jnp.where(code == float(i), ey, 0.0)
                at_end = own_lane == COLS - 1 - l
                side_g = jnp.where(at_end, turn(ex, -l), side_g)
                side_c = jnp.where(at_end, turn(m * 4.0 + m_x, -l), side_c)
            for i in range(16):
                cx[i] = cx[i] + jnp.where(side_c == float(i), side_g, 0.0)
        for i in range(MATS):
            keep(G_RW + i, rw[i])
            keep(G_RAU + i, rau[i])
            keep(G_MOM + i, mom[i])
        for i in range(6):
            keep(G_S + i, pairs[i])
        for i in range(16):
            keep(G_CY + i, cy[i])
            keep(G_CX + i, cx[i])

    for i in range(MATS):
        total = jnp.zeros((ROWS, COLS), F32)
        for l in range(LAYERS):
            total = total + jnp.where(mat[l] == i, cap[l], 0.0)
        acc[ROW_CAP + i : ROW_CAP + i + 1, :] = fold(total)
    second[:, 0:COLS] = jnp.broadcast_to(place(acc[0:COLS, :]), (TOTAL, COLS))
    second[:, COLS:WIDE] = jnp.broadcast_to(place(acc[COLS:WIDE, :]), (TOTAL, COLS))


def next_y(x):
    y = lax.rem(lanes(x.shape), N_GY)
    return jnp.where(y == N_GY - 1, turn(x, N_GY - 1), turn(x, -1))


def prev_y(x):
    y = lax.rem(lanes(x.shape), N_GY)
    return jnp.where(y == 0, turn(x, -(N_GY - 1)), turn(x, 1))


def total_of(x):
    return jnp.sum(jnp.sum(x, axis=0, keepdims=True), axis=1, keepdims=True)


def second_kernel(
    b, got, got2, cap, mat, gy, gx, gz, scale, z0, w0, u,
    out_x, out_r, out_z,
    v1, w1, za, zb, scatter, gather, near_hot, turned, turned2, values, values2,
):
    turned[...] = got[...].T
    turned2[0:COLS, :] = got2[:, 0:COLS].T
    turned2[COLS:WIDE, :] = got2[:, COLS:WIDE].T
    build_scatter(got, scatter)
    build_gather(turned, gather)
    build_near(got, near_hot)

    sums_w = local_sums(turned2, G_RW)
    sol = coarse_solve(sums_w, turned, scatter)
    spread_values(exact_dot(sol, near_hot[...]), values)
    c_all = exact_dot(sol, gather[...])
    c = [c_all[:, m * TOTAL : (m + 1) * TOTAL] for m in range(MATS)]

    def rows5(group):
        return turned2[group * SPECIES : group * SPECIES + 8, :]

    live = subs((8, TOTAL)) < SPECIES
    bc = [turned2[ROW_CAP + m : ROW_CAP + m + 1, :] * c[m] for m in range(MATS)]
    n = 0
    for i in range(MATS):
        for j in range(i + 1, MATS):
            f = rows5(G_S + n) * (c[i] - c[j])
            bc[i] = bc[i] + f
            bc[j] = bc[j] - f
            n += 1
    c_y = [next_y(v) for v in c]
    c_x = [turn(v, -N_GY) for v in c]
    back_y = [jnp.zeros((8, TOTAL), F32)] * MATS
    back_x = [jnp.zeros((8, TOTAL), F32)] * MATS
    for i in range(MATS):
        for j in range(MATS):
            f = rows5(G_CY + 4 * i + j) * (c[i] - c_y[j])
            bc[i] = bc[i] + f
            back_y[j] = back_y[j] + f
            f = rows5(G_CX + 4 * i + j) * (c[i] - c_x[j])
            bc[i] = bc[i] + f
            back_x[j] = back_x[j] + f
    for j in range(MATS):
        bc[j] = jnp.where(live, bc[j] - prev_y(back_y[j]) - turn(back_x[j], N_GY), 0.0)
    bc_all = jnp.concatenate(bc, axis=1)
    sums_au = local_sums(turned2, G_RAU)
    sol2 = coarse_solve(sums_au + bc_all, turned, scatter)
    spread_values(exact_dot(sol2, near_hot[...]), values2)

    def moment(i):
        return total_of(jnp.where(live, rows5(G_MOM + i), 0.0))

    m0, m1 = moment(0), moment(1)
    m2 = moment(2) + total_of(sums_w * c_all)
    m3 = moment(3) + total_of((2.0 * sums_au + bc_all) * c_all)
    a0 = m0 / m1
    rz1 = m0 - 2.0 * a0 * m1 + a0 * a0 * m2
    g = 1.0 + rz1 / m0
    a1 = rz1 / (g * g * m1 - 2.0 * a0 * g * m2 + a0 * a0 * m3)
    ca = jnp.broadcast_to(a0 + a1 * g, (8, COLS))
    cb = jnp.broadcast_to(a1 * a0, (8, COLS))

    ops = (cap, gy, gx, gz, scale)
    mid, own = tile_rows(1, 6), tile_rows(2, 5)

    @pl.loop(0, SPECIES)
    def _(s):
        for row in mid:
            here = pl.ds(row, 8)
            for l in range(LAYERS):
                k = s * LAYERS + l
                v1[k, here, :] = u[k, here, :] + coarse_at(values, mat[l, here, :], s, row)

    image(v1, w1, ops, mid)
    start_sweep(w1, za, scale, mid)
    sweep(za, w1, zb, ops, mid)
    sweep(zb, w1, za, ops, mid)

    @pl.loop(0, SPECIES)
    def _(s):
        for row in own:
            here = pl.ds(row, 8)
            us, outs = a_tile(za, cap, gy, gx, gz, s, row)
            for l in range(LAYERS):
                k = s * LAYERS + l
                w1v = w1[k, here, :]
                v2 = us[l] + scale[k, here, :] * (w1v - outs[l])
                v2 = (v2 + coarse_at(values2, mat[l, here, :], s, row))[:, :COLS]
                w1v = w1v[:, :COLS]
                v1v = v1[k, here, 0:COLS]
                rows = pl.ds(row - TOP, 8)
                z0v, w0v = z0[k, rows, :], w0[k, rows, :]
                out_x[k, rows, :] = ca * z0v - cb * v1v
                out_r[k, rows, :] = b[k, rows, :] - ca * w0v + cb * w1v
                out_z[k, rows, :] = z0v - ca * v1v + cb * v2


def shape(*dims):
    return jax.ShapeDtypeStruct(dims, F32)


VMEM = pl.BlockSpec(memory_space=pltpu.VMEM)
SMEM = pl.BlockSpec(memory_space=pltpu.SMEM)
PARAMS = pltpu.CompilerParams(vmem_limit_bytes=56 * 1024 * 1024)


def run(kernel, outs, scratch, in_specs, *args):
    return pl.pallas_call(
        kernel,
        out_shape=outs,
        in_specs=in_specs,
        out_specs=jax.tree.map(lambda _: VMEM, outs),
        scratch_shapes=scratch,
        compiler_params=PARAMS,
    )(*args)


def shifts(axis, count):
    forward = [(i, (i + 1) % count) for i in range(count)]
    backward = [(target, source) for source, target in forward]
    return (functools.partial(lax.ppermute, axis_name=axis, perm=p) for p in (forward, backward))


def to_all(rows):
    width = rows.shape[1]
    got = lax.all_to_all(rows.reshape(TOTAL, 1, width), BOTH, 0, 0, tiled=True)
    return got.reshape(TOTAL, width)


def body(right_side, potential, capacity, diffusivity, material, coarse_map, coarse_inverse):
    b = right_side.reshape(FIELDS, ROWS, COLS)
    own = (b, potential, capacity, material)
    right, left = shifts("grp", N_GRP)
    down, up = shifts("gy", N_GY)

    packed = shape(GROUPS, ROWS, COLS)
    to_low, to_high = run(pack_kernel, (packed, packed), [], [VMEM] * 4, *own)
    x_low, x_high = right(to_high), left(to_low)

    q = coarse_map.reshape(-1)
    tail = jnp.concatenate(
        [
            jnp.zeros((MAP_LANE,), F32),
            ((q & 3) * TOTAL + (q >> 2)).astype(F32),
            coarse_inverse.reshape(-1),
            jnp.zeros((COLS - INV_LANE - 100,), F32),
        ]
    ).reshape(1, COLS)
    first = run(
        sums_kernel, shape(TOTAL, COLS), [pltpu.VMEM((24, COLS), F32)], [VMEM] * 3, b, material, tail
    )

    strips = shape(PLANES + 2 * GROUPS, RHALO, COLS)
    to_low, to_high = run(rows_kernel, (strips, strips), [], [VMEM] * 6, *own, x_low, x_high)
    first, to_low, to_high = lax.optimization_barrier((first, to_low, to_high))
    y_low, y_high = down(to_high), up(to_low)
    got = to_all(first)

    wide = shape(FIELDS, TALL, WIDE)
    thin = shape(LAYERS, TALL, WIDE)
    field = shape(FIELDS, ROWS, COLS)
    big = pltpu.VMEM((FIELDS, TALL, WIDE), F32)
    hot = pltpu.VMEM((NC, MATS * TOTAL), jnp.bfloat16)
    near = pltpu.VMEM((NC, COLS), jnp.bfloat16)
    square = pltpu.VMEM((COLS + 8, COLS), F32)
    values = pltpu.VMEM((3 * MATS, 8, WIDE), F32)
    second, cap_w, mat_w, gy, gx, gz, scale, z0, w0, u = run(
        first_kernel,
        (shape(TOTAL, WIDE), thin, thin, wide, wide, wide, wide, field, field, wide),
        [big] * 5 + [hot, near, pltpu.VMEM((COLS, COLS), F32), values, pltpu.VMEM((WIDE, COLS), F32)],
        [SMEM] + [VMEM] * 9,
        diffusivity, *own, x_low, x_high, y_low, y_high, got,
    )
    got2 = to_all(second)
    out = run(
        second_kernel,
        (field, field, field),
        [big] * 4
        + [hot, hot, near, pltpu.VMEM((COLS, COLS), F32), pltpu.VMEM((WIDE, COLS), F32), values, values],
        [VMEM] * 12,
        b, got, got2, cap_w, mat_w, gy, gx, gz, scale, z0, w0, u,
    )
    return tuple(o.reshape(right_side.shape) for o in out)


def solution(mesh):
    placed = (
        P(None, None, "gy", "grp"),
        P(None, "gy", "grp"),
        P(None, "gy", "grp"),
        P(),
        P(None, "gy", "grp"),
        P("gy", "grp", None),
        P(("grp", "gy"), None, None),
    )
    return jax.shard_map(
        body,
        mesh=mesh,
        in_specs=placed,
        out_specs=(P(None, None, "gy", "grp"),) * 3,
        check_vma=False,
    )
```

```python
import functools

import jax
import jax.numpy as jnp
from jax import lax
from jax.experimental import pallas as pl
from jax.experimental.pallas import tpu as pltpu
from jax.sharding import PartitionSpec as P

SPECIES = 5
LAYERS = 4
MATS = 4
FIELDS = SPECIES * LAYERS
PLANES = FIELDS + 3 * LAYERS
ROWS = 32
COLS = 128
N_GRP = 4
N_GY = 32
TOTAL = N_GRP * N_GY
NC = 512
DAMPING = 2.0 / 3.0
BOTH = ("grp", "gy")

HALO = 12
PER = 10
GROUPS = -(-PLANES // PER)
RHALO = 16
PAD = 8
WIDE = 2 * COLS
TALL = ROWS + 2 * RHALO + 2 * PAD
TOP = PAD + RHALO
F32 = jnp.float32

G_RW, G_RAU, G_S, G_CY, G_CX, G_MOM = 0, 4, 8, 14, 30, 46
ROW_CAP = 250
MAP_LANE = 20
INV_LANE = 24


def lanes(shape):
    return lax.broadcasted_iota(jnp.int32, shape, 1)


def subs(shape):
    return lax.broadcasted_iota(jnp.int32, shape, 0)


def pack_kernel(b, pot, cap, mat, to_low, to_high):
    lane = lanes((ROWS, COLS))
    for g in range(GROUPS):
        low = jnp.zeros((ROWS, COLS), F32)
        high = jnp.zeros((ROWS, COLS), F32)
        for j in range(min(PER, PLANES - g * PER)):
            v = plane_of(b, pot, cap, mat, g * PER + j)
            inside = (lane >= HALO * j) & (lane < HALO * (j + 1))
            low = jnp.where(inside, turn(v, HALO * j), low)
            high = jnp.where(inside, turn(v, HALO * j + HALO), high)
        to_low[g] = low
        to_high[g] = high


def turn(v, shift):
    shift = shift % v.shape[1]
    return v if shift == 0 else pltpu.roll(v, shift, 1)


def plane_of(b, pot, cap, mat, k):
    if k < FIELDS:
        return b[k]
    which, layer = divmod(k - FIELDS, LAYERS)
    return (pot, cap, mat)[which][layer].astype(F32)


def place(rows):
    n = rows.shape[0]
    total = jnp.sum(rows, axis=1, keepdims=True)
    spread = jnp.where(lanes((n, COLS)) == subs((n, COLS)), total, 0.0)
    return jnp.sum(spread, axis=0, keepdims=True)


def fold(v):
    return jnp.sum(v, axis=0, keepdims=True)


def sums_kernel(b, mat, cmap, inverse, out, acc, ids):
    acc[...] = jnp.zeros(acc.shape, F32)
    row = jnp.zeros((1, COLS), F32)
    for s in range(SPECIES):
        acc[0:4, 0:SPECIES] = inverse[s]
        for k in range(4):
            row = row + turn(acc[k : k + 1, :], INV_LANE + (k * SPECIES + s) * SPECIES)
    acc[0:4, :] = jnp.zeros((4, COLS), F32)
    ids[...] = jnp.zeros(ids.shape, jnp.int32)
    ids[0:1, 0:MATS] = cmap[0]
    q = ids[0:1, :]
    row = row + turn(((q & 3) * TOTAL + (q >> 2)).astype(F32), MAP_LANE)
    for s in range(SPECIES):
        for m in range(MATS):
            total = jnp.zeros((ROWS, COLS), F32)
            for l in range(LAYERS):
                total = total + jnp.where(mat[l] == m, b[s * LAYERS + l], 0.0)
            acc[m * SPECIES + s : m * SPECIES + s + 1, :] = fold(total)
    row = row + place(acc[...])
    out[...] = jnp.broadcast_to(row, (TOTAL, COLS))


def rows_kernel(b, pot, cap, mat, from_low, from_high, to_low, to_high):
    for k in range(PLANES):
        v = plane_of(b, pot, cap, mat, k)
        to_low[k] = v[:RHALO]
        to_high[k] = v[ROWS - RHALO :]
    for g in range(GROUPS):
        for i, part in enumerate((from_low, from_high)):
            k = PLANES + i * GROUPS + g
            to_low[k] = part[g, :RHALO]
            to_high[k] = part[g, ROWS - RHALO :]


def unpack_halo(low, high, j, fill):
    shape = low.shape
    lane = lanes(shape)
    right = turn(high, -HALO * j)
    left = turn(low, -HALO * (j + 1))
    return jnp.where(lane < HALO, right, jnp.where(lane >= COLS - HALO, left, fill))


def a_tile(src, cap, gy, gx, gz, s, row):
    base = s * LAYERS
    here = pl.ds(row, 8)
    below = pl.ds(row - 1, 8)
    above = pl.ds(row + 1, 8)
    us, outs = [], []
    flux_z = None
    for l in range(LAYERS):
        k = base + l
        u = src[k, here, :]
        if l == 0:
            nxt = u
        u = nxt
        flux_x = gx[k, here, :] * (u - pltpu.roll(u, WIDE - 1, 1))
        out = cap[l, here, :] * u + (flux_x - pltpu.roll(flux_x, 1, 1))
        out = out + gy[k, here, :] * (u - src[k, above, :])
        out = out + gy[k, below, :] * (u - src[k, below, :])
        if flux_z is not None:
            out = out - flux_z
        if l + 1 < LAYERS:
            nxt = src[k + 1, here, :]
            flux_z = gz[k, here, :] * (u - nxt)
            out = out + flux_z
        us.append(u)
        outs.append(out)
    return us, outs


def tile_rows(first, last):
    return [PAD + 8 * t for t in range(first, last + 1)]


def sweep(src, resid, dst, ops, tiles):
    cap, gy, gx, gz, scale = ops

    @pl.loop(0, SPECIES)
    def _(s):
        for row in tiles:
            us, outs = a_tile(src, cap, gy, gx, gz, s, row)
            for l in range(LAYERS):
                k = s * LAYERS + l
                here = pl.ds(row, 8)
                dst[k, here, :] = us[l] + scale[k, here, :] * (resid[k, here, :] - outs[l])


def image(src, dst, ops, tiles):
    cap, gy, gx, gz, _ = ops

    @pl.loop(0, SPECIES)
    def _(s):
        for row in tiles:
            _, outs = a_tile(src, cap, gy, gx, gz, s, row)
            for l in range(LAYERS):
                dst[s * LAYERS + l, pl.ds(row, 8), :] = outs[l]


def start_sweep(resid, dst, scale, tiles):
    @pl.loop(0, SPECIES)
    def _(s):
        for row in tiles:
            for l in range(LAYERS):
                k = s * LAYERS + l
                here = pl.ds(row, 8)
                dst[k, here, :] = scale[k, here, :] * resid[k, here, :]


def split3(x):
    hi = x.astype(jnp.bfloat16)
    rest = x - hi.astype(F32)
    mid = rest.astype(jnp.bfloat16)
    lo = (rest - mid.astype(F32)).astype(jnp.bfloat16)
    return jnp.concatenate([hi, mid, lo], axis=0)


def exact_dot(x, onehot):
    n = x.shape[0]
    y = jnp.dot(
        jnp.concatenate([split3(x)], axis=0), onehot, preferred_element_type=F32
    )
    return y[:n] + y[n : 2 * n] + y[2 * n :]


def build_scatter(got, onehot):
    for m in range(MATS):
        col = jnp.broadcast_to(got[:, MAP_LANE + m : MAP_LANE + m + 1], (TOTAL, COLS))
        for k in range(4):
            target = (lanes((TOTAL, COLS)) + k * COLS).astype(F32)
            onehot[m * TOTAL : (m + 1) * TOTAL, k * COLS : (k + 1) * COLS] = jnp.where(
                col == target, 1.0, 0.0
            ).astype(jnp.bfloat16)


def build_gather(turned, onehot):
    for m in range(MATS):
        row = jnp.broadcast_to(turned[MAP_LANE + m : MAP_LANE + m + 1, :], (COLS, TOTAL))
        for k in range(4):
            target = (subs((COLS, TOTAL)) + k * COLS).astype(F32)
            onehot[k * COLS : (k + 1) * COLS, m * TOTAL : (m + 1) * TOTAL] = jnp.where(
                row == target, 1.0, 0.0
            ).astype(jnp.bfloat16)


def build_near(got, onehot):
    gx, gy = lax.axis_index("grp"), lax.axis_index("gy")
    lane = lanes((1, COLS))
    row = jnp.full((1, COLS), -1.0, F32)
    for iy in range(3):
        y = lax.rem(gy + (N_GY - 1 + iy), N_GY)
        for ix in range(3):
            x = jnp.clip(gx + (ix - 1), 0, N_GRP - 1)
            region = iy * 3 + ix
            here = got[pl.ds(x * N_GY + y, 1), :]
            inside = (lane >= region * MATS) & (lane < (region + 1) * MATS)
            row = jnp.where(inside, turn(here, region * MATS - MAP_LANE), row)
    for k in range(4):
        target = (subs((COLS, COLS)) + k * COLS).astype(F32)
        onehot[k * COLS : (k + 1) * COLS, :] = jnp.where(
            jnp.broadcast_to(row, (COLS, COLS)) == target, 1.0, 0.0
        ).astype(jnp.bfloat16)


def coarse_solve(sums, turned, scatter):
    res = exact_dot(sums, scatter[...])
    parts = []
    for k in range(4):
        total = None
        for t in range(SPECIES):
            start = INV_LANE + k * SPECIES * SPECIES + t * SPECIES
            term = turned[start : start + 8, :] * res[t : t + 1, k * COLS : (k + 1) * COLS]
            total = term if total is None else total + term
        parts.append(total)
    sol = jnp.concatenate(parts, axis=1)
    return jnp.where(subs(sol.shape) < SPECIES, sol, 0.0)


def local_sums(turned, group):
    x = jnp.concatenate(
        [turned[(group + m) * SPECIES : (group + m) * SPECIES + 8, :] for m in range(MATS)], axis=1
    )
    return jnp.where(subs(x.shape) < SPECIES, x, 0.0)


def spread_values(near, values):
    lane = lanes((8, COLS))
    for iy in range(3):
        for m in range(MATS):
            cols = [
                jnp.broadcast_to(
                    near[:, (iy * 3 + ix) * MATS + m : (iy * 3 + ix) * MATS + m + 1], (8, COLS)
                )
                for ix in range(3)
            ]
            values[iy * MATS + m, :, 0:COLS] = cols[1]
            values[iy * MATS + m, :, COLS:WIDE] = jnp.where(lane < COLS // 2, cols[2], cols[0])


def region_of(row):
    return 0 if row < TOP else (1 if row < TOP + ROWS else 2)


def coarse_at(values, mat_tile, s, row):
    iy = region_of(row)
    v = [
        jnp.broadcast_to(values[iy * MATS + m, pl.ds(s, 1), :], mat_tile.shape) for m in range(MATS)
    ]
    out = jnp.where(mat_tile == 1.0, v[1], v[0])
    out = jnp.where(mat_tile == 2.0, v[2], out)
    return jnp.where(mat_tile == 3.0, v[3], out)


def fill_plane(dst, index, k, own, x_low, x_high, y_low, y_high, fill):
    g, j = divmod(k, PER)
    dst[index, PAD : PAD + RHALO, 0:COLS] = y_low[k]
    dst[index, TOP : TOP + ROWS, 0:COLS] = own
    dst[index, TOP + ROWS : TOP + ROWS + RHALO, 0:COLS] = y_high[k]
    dst[index, PAD : PAD + RHALO, COLS:WIDE] = unpack_halo(
        y_low[PLANES + g], y_low[PLANES + GROUPS + g], j, fill
    )
    dst[index, TOP : TOP + ROWS, COLS:WIDE] = unpack_halo(x_low[g], x_high[g], j, fill)
    dst[index, TOP + ROWS : TOP + ROWS + RHALO, COLS:WIDE] = unpack_halo(
        y_high[PLANES + g], y_high[PLANES + GROUPS + g], j, fill
    )


def harmonic(a, b):
    return 2.0 * a * b / (a + b)


def first_kernel(
    diff, b, pot, cap, mat, x_low, x_high, y_low, y_high, got,
    second, cap_w, mat_w, gy, gx, gz, scale, z0_out, w0_out, u_out,
    b_w, w, za, zb, w0, scatter, near_hot, turned, values, acc,
):
    halves = (x_low, x_high, y_low, y_high)
    for k in range(FIELDS):
        fill_plane(b_w, k, k, b[k], *halves, 0.0)
    for l in range(LAYERS):
        fill_plane(za, l, FIELDS + l, pot[l], *halves, 0.0)
        fill_plane(cap_w, l, FIELDS + LAYERS + l, cap[l], *halves, 1.0)
        fill_plane(mat_w, l, FIELDS + 2 * LAYERS + l, mat[l].astype(F32), *halves, 0.0)

    for row in tile_rows(0, 7):
        for l in range(LAYERS):
            here = pl.ds(row, 8)
            m = mat_w[l, here, :]
            is1, is2, is3 = m == 1.0, m == 2.0, m == 3.0
            down = jnp.exp(-0.5 * za[l, here, :])
            up = jnp.exp(0.5 * za[l, here, :])
            drift = (down, up, down * down, up * up, down)
            for s in range(SPECIES):
                d = jnp.where(is1, diff[1, s], diff[0, s])
                d = jnp.where(is2, diff[2, s], d)
                d = jnp.where(is3, diff[3, s], d)
                w[s * LAYERS + l, here, :] = d * drift[s]

    me_x = lax.axis_index("grp")
    lane = lanes((8, WIDE))
    closed = ((lane == COLS - 1) & (me_x == N_GRP - 1)) | ((lane == WIDE - 1) & (me_x == 0))

    @pl.loop(0, SPECIES)
    def _(s):
        for row in tile_rows(0, 7):
            here, above = pl.ds(row, 8), pl.ds(row + 1, 8)
            for l in range(LAYERS):
                k = s * LAYERS + l
                c = w[k, here, :]
                gy[k, here, :] = harmonic(c, w[k, above, :])
                gx[k, here, :] = jnp.where(closed, 0.0, harmonic(c, pltpu.roll(c, WIDE - 1, 1)))
                if l + 1 < LAYERS:
                    gz[k, here, :] = 0.5 * harmonic(c, w[k + 1, here, :])
        for row in tile_rows(0, 7):
            here, below = pl.ds(row, 8), pl.ds(row - 1, 8)
            for l in range(LAYERS):
                k = s * LAYERS + l
                ex = gx[k, here, :]
                d = cap_w[l, here, :] + gy[k, here, :] + gy[k, below, :] + ex + pltpu.roll(ex, 1, 1)
                if l + 1 < LAYERS:
                    d = d + gz[k, here, :]
                if l > 0:
                    d = d + gz[k - 1, here, :]
                scale[k, here, :] = DAMPING / d

    ops = (cap_w, gy, gx, gz, scale)
    all_tiles, mid, own = tile_rows(0, 7), tile_rows(1, 6), tile_rows(2, 5)

    turned[...] = got[...].T
    build_scatter(got, scatter)
    build_near(got, near_hot)
    sol = coarse_solve(local_sums(turned, 0), turned, scatter)
    spread_values(exact_dot(sol, near_hot[...]), values)

    start_sweep(b_w, za, scale, all_tiles)
    sweep(za, b_w, zb, ops, all_tiles)
    sweep(zb, b_w, za, ops, all_tiles)

    cap_o, gy_o, gx_o, gz_o, scale_o = ops

    @pl.loop(0, SPECIES)
    def _(s):
        for row in mid:
            here = pl.ds(row, 8)
            us, outs = a_tile(za, cap_o, gy_o, gx_o, gz_o, s, row)
            for l in range(LAYERS):
                k = s * LAYERS + l
                smooth = us[l] + scale[k, here, :] * (b_w[k, here, :] - outs[l])
                zb[k, here, :] = smooth + coarse_at(values, mat_w[l, here, :], s, row)

    for k in range(FIELDS):
        z0_out[k] = zb[k, TOP : TOP + ROWS, 0:COLS]
    image(zb, w0, ops, mid)
    for k in range(FIELDS):
        w0_out[k] = w0[k, TOP : TOP + ROWS, 0:COLS]
    start_sweep(w0, za, scale, mid)
    sweep(za, w0, zb, ops, mid)
    sweep(zb, w0, za, ops, mid)
    sweep(za, w0, u_out, ops, mid)

    acc[...] = jnp.zeros(acc.shape, F32)
    own_lane = lanes((8, COLS))
    sub = subs((8, COLS))

    @pl.loop(0, SPECIES)
    def _(s):
        def keep(group, v):
            acc[pl.ds(group * SPECIES + s, 1), :] = fold(v)

        zero = jnp.zeros((8, COLS), F32)
        rw, rau, mom = [zero] * MATS, [zero] * MATS, [zero] * 4
        pairs, cy, cx = [zero] * 6, [zero] * 16, [zero] * 16
        codes = (3.0, 5.0, 9.0, 6.0, 10.0, 12.0)

        def power(m):
            p = jnp.where(m == 1.0, 2.0, 1.0)
            p = jnp.where(m == 2.0, 4.0, p)
            return jnp.where(m == 3.0, 8.0, p)

        for row in own:
            here = pl.ds(row, 8)
            above = pl.ds(row + 1, 8)
            us, outs = a_tile(u_out, cap_o, gy_o, gx_o, gz_o, s, row)
            side_g, side_c = zero, zero - 1.0
            for l in range(LAYERS):
                k = s * LAYERS + l
                m_wide = mat_w[l, here, :]
                m = m_wide[:, :COLS]
                u, au = us[l][:, :COLS], outs[l][:, :COLS]
                wv, zv, bv = w0_out[k, row - TOP : row - TOP + 8, :], z0_out[k, row - TOP : row - TOP + 8, :], b[k, row - TOP : row - TOP + 8, :]
                mom[0] = mom[0] + bv * zv
                mom[1] = mom[1] + zv * wv
                mom[2] = mom[2] + wv * u
                mom[3] = mom[3] + u * au
                for i in range(MATS):
                    is_i = m == float(i)
                    rw[i] = rw[i] + jnp.where(is_i, wv, 0.0)
                    rau[i] = rau[i] + jnp.where(is_i, au, 0.0)
                m_y = mat_w[l, above, 0:COLS]
                m_x = pltpu.roll(m_wide, WIDE - 1, 1)[:, :COLS]
                ey, ex = gy[k, here, 0:COLS], gx[k, here, 0:COLS]
                p = power(m)
                last = row == own[-1]
                code = p + power(m_y)
                if last:
                    code = jnp.where(sub == 7, 0.0, code)
                kinds = [(code, ey), (jnp.where(own_lane == COLS - 1, 0.0, p + power(m_x)), ex)]
                if l + 1 < LAYERS:
                    kinds.append((p + power(mat_w[l + 1, here, 0:COLS]), gz[k, here, 0:COLS]))
                for code, edge in kinds:
                    for i in range(6):
                        pairs[i] = pairs[i] + jnp.where(code == codes[i], edge, 0.0)
                if last:
                    code = jnp.where(sub == 7, m * 4.0 + m_y, -1.0)
                    for i in range(16):
                        cy[i] = cy[i] + jnp.where(code == float(i), ey, 0.0)
                at_end = own_lane == COLS - 1 - l
                side_g = jnp.where(at_end, turn(ex, -l), side_g)
                side_c = jnp.where(at_end, turn(m * 4.0 + m_x, -l), side_c)
            for i in range(16):
                cx[i] = cx[i] + jnp.where(side_c == float(i), side_g, 0.0)
        for i in range(MATS):
            keep(G_RW + i, rw[i])
            keep(G_RAU + i, rau[i])
            keep(G_MOM + i, mom[i])
        for i in range(6):
            keep(G_S + i, pairs[i])
        for i in range(16):
            keep(G_CY + i, cy[i])
            keep(G_CX + i, cx[i])

    for i in range(MATS):
        total = jnp.zeros((ROWS, COLS), F32)
        for l in range(LAYERS):
            total = total + jnp.where(mat[l] == i, cap[l], 0.0)
        acc[ROW_CAP + i : ROW_CAP + i + 1, :] = fold(total)
    even = lax.rem(subs((WIDE, COLS)), 2) == 0
    second[...] = jnp.where(even, place(acc[0:COLS, :]), place(acc[COLS:WIDE, :]))


def next_y(x):
    y = lax.rem(lanes(x.shape), N_GY)
    return jnp.where(y == N_GY - 1, turn(x, N_GY - 1), turn(x, -1))


def prev_y(x):
    y = lax.rem(lanes(x.shape), N_GY)
    return jnp.where(y == 0, turn(x, -(N_GY - 1)), turn(x, 1))


def total_of(x):
    return jnp.sum(jnp.sum(x, axis=0, keepdims=True), axis=1, keepdims=True)


def second_kernel(
    b, got, got2, cap, mat, gy, gx, gz, scale, z0, w0, u,
    out_x, out_r, out_z,
    v1, w1, za, zb, scatter, gather, near_hot, turned, turned2, values, values2,
):
    turned[...] = got[...].T
    turned2[0:COLS, :] = got2[pl.ds(0, TOTAL, stride=2), :].T
    turned2[COLS:WIDE, :] = got2[pl.ds(1, TOTAL, stride=2), :].T
    build_scatter(got, scatter)
    build_gather(turned, gather)
    build_near(got, near_hot)

    sums_w = local_sums(turned2, G_RW)
    sol = coarse_solve(sums_w, turned, scatter)
    spread_values(exact_dot(sol, near_hot[...]), values)
    c_all = exact_dot(sol, gather[...])
    c = [c_all[:, m * TOTAL : (m + 1) * TOTAL] for m in range(MATS)]

    def rows5(group):
        return turned2[group * SPECIES : group * SPECIES + 8, :]

    live = subs((8, TOTAL)) < SPECIES
    bc = [turned2[ROW_CAP + m : ROW_CAP + m + 1, :] * c[m] for m in range(MATS)]
    n = 0
    for i in range(MATS):
        for j in range(i + 1, MATS):
            f = rows5(G_S + n) * (c[i] - c[j])
            bc[i] = bc[i] + f
            bc[j] = bc[j] - f
            n += 1
    c_y = [next_y(v) for v in c]
    c_x = [turn(v, -N_GY) for v in c]
    back_y = [jnp.zeros((8, TOTAL), F32)] * MATS
    back_x = [jnp.zeros((8, TOTAL), F32)] * MATS
    for i in range(MATS):
        for j in range(MATS):
            f = rows5(G_CY + 4 * i + j) * (c[i] - c_y[j])
            bc[i] = bc[i] + f
            back_y[j] = back_y[j] + f
            f = rows5(G_CX + 4 * i + j) * (c[i] - c_x[j])
            bc[i] = bc[i] + f
            back_x[j] = back_x[j] + f
    for j in range(MATS):
        bc[j] = jnp.where(live, bc[j] - prev_y(back_y[j]) - turn(back_x[j], N_GY), 0.0)
    bc_all = jnp.concatenate(bc, axis=1)
    sums_au = local_sums(turned2, G_RAU)
    sol2 = coarse_solve(sums_au + bc_all, turned, scatter)
    spread_values(exact_dot(sol2, near_hot[...]), values2)

    def moment(i):
        return total_of(jnp.where(live, rows5(G_MOM + i), 0.0))

    m0, m1 = moment(0), moment(1)
    m2 = moment(2) + total_of(sums_w * c_all)
    m3 = moment(3) + total_of((2.0 * sums_au + bc_all) * c_all)
    a0 = m0 / m1
    rz1 = m0 - 2.0 * a0 * m1 + a0 * a0 * m2
    g = 1.0 + rz1 / m0
    a1 = rz1 / (g * g * m1 - 2.0 * a0 * g * m2 + a0 * a0 * m3)
    ca = jnp.broadcast_to(a0 + a1 * g, (8, COLS))
    cb = jnp.broadcast_to(a1 * a0, (8, COLS))

    ops = (cap, gy, gx, gz, scale)
    mid, own = tile_rows(1, 6), tile_rows(2, 5)

    @pl.loop(0, SPECIES)
    def _(s):
        for row in mid:
            here = pl.ds(row, 8)
            for l in range(LAYERS):
                k = s * LAYERS + l
                v1[k, here, :] = u[k, here, :] + coarse_at(values, mat[l, here, :], s, row)

    image(v1, w1, ops, mid)
    start_sweep(w1, za, scale, mid)
    sweep(za, w1, zb, ops, mid)
    sweep(zb, w1, za, ops, mid)

    @pl.loop(0, SPECIES)
    def _(s):
        for row in own:
            here = pl.ds(row, 8)
            us, outs = a_tile(za, cap, gy, gx, gz, s, row)
            for l in range(LAYERS):
                k = s * LAYERS + l
                w1v = w1[k, here, :]
                v2 = us[l] + scale[k, here, :] * (w1v - outs[l])
                v2 = (v2 + coarse_at(values2, mat[l, here, :], s, row))[:, :COLS]
                w1v = w1v[:, :COLS]
                v1v = v1[k, here, 0:COLS]
                rows = pl.ds(row - TOP, 8)
                z0v, w0v = z0[k, rows, :], w0[k, rows, :]
                out_x[k, rows, :] = ca * z0v - cb * v1v
                out_r[k, rows, :] = b[k, rows, :] - ca * w0v + cb * w1v
                out_z[k, rows, :] = z0v - ca * v1v + cb * v2


def shape(*dims):
    return jax.ShapeDtypeStruct(dims, F32)


VMEM = pl.BlockSpec(memory_space=pltpu.VMEM)
SMEM = pl.BlockSpec(memory_space=pltpu.SMEM)
PARAMS = pltpu.CompilerParams(vmem_limit_bytes=26 * 1024 * 1024)


def run(kernel, outs, scratch, in_specs, *args):
    return pl.pallas_call(
        kernel,
        out_shape=outs,
        in_specs=in_specs,
        out_specs=jax.tree.map(lambda _: VMEM, outs),
        scratch_shapes=scratch,
        compiler_params=PARAMS,
    )(*args)


def shifts(axis, count):
    forward = [(i, (i + 1) % count) for i in range(count)]
    backward = [(target, source) for source, target in forward]
    return (functools.partial(lax.ppermute, axis_name=axis, perm=p) for p in (forward, backward))


def to_all(rows):
    got = lax.all_to_all(rows.reshape(TOTAL, -1, COLS), BOTH, 0, 0, tiled=True)
    return got.reshape(rows.shape)


def body(right_side, potential, capacity, diffusivity, material, coarse_map, coarse_inverse):
    b = right_side.reshape(FIELDS, ROWS, COLS)
    own = (b, potential, capacity, material)
    right, left = shifts("grp", N_GRP)
    down, up = shifts("gy", N_GY)

    packed = shape(GROUPS, ROWS, COLS)
    to_low, to_high = run(pack_kernel, (packed, packed), [], [VMEM] * 4, *own)
    x_low, x_high = right(to_high), left(to_low)

    first = run(
        sums_kernel,
        shape(TOTAL, COLS),
        [pltpu.VMEM((24, COLS), F32), pltpu.VMEM((8, COLS), jnp.int32)],
        [VMEM] * 4,
        b, material, coarse_map, jnp.transpose(coarse_inverse, (1, 0, 2)),
    )

    strips = shape(PLANES + 2 * GROUPS, RHALO, COLS)
    to_low, to_high = run(rows_kernel, (strips, strips), [], [VMEM] * 6, *own, x_low, x_high)
    first, to_low, to_high = lax.optimization_barrier((first, to_low, to_high))
    y_low, y_high = down(to_high), up(to_low)
    got = to_all(first)

    wide = shape(FIELDS, TALL, WIDE)
    thin = shape(LAYERS, TALL, WIDE)
    field = shape(FIELDS, ROWS, COLS)
    big = pltpu.VMEM((FIELDS, TALL, WIDE), F32)
    hot = pltpu.VMEM((NC, MATS * TOTAL), jnp.bfloat16)
    near = pltpu.VMEM((NC, COLS), jnp.bfloat16)
    square = pltpu.VMEM((COLS + 8, COLS), F32)
    values = pltpu.VMEM((3 * MATS, 8, WIDE), F32)
    second, cap_w, mat_w, gy, gx, gz, scale, z0, w0, u = run(
        first_kernel,
        (shape(2 * TOTAL, COLS), thin, thin, wide, wide, wide, wide, field, field, wide),
        [big] * 5 + [hot, near, pltpu.VMEM((COLS, COLS), F32), values, pltpu.VMEM((WIDE, COLS), F32)],
        [SMEM] + [VMEM] * 9,
        diffusivity.T, *own, x_low, x_high, y_low, y_high, got,
    )
    got2 = to_all(second)
    out = run(
        second_kernel,
        (field, field, field),
        [big] * 4
        + [hot, hot, near, pltpu.VMEM((COLS, COLS), F32), pltpu.VMEM((WIDE, COLS), F32), values, values],
        [VMEM] * 12,
        b, got, got2, cap_w, mat_w, gy, gx, gz, scale, z0, w0, u,
    )
    return tuple(o.reshape(right_side.shape) for o in out)


def solution(mesh):
    placed = (
        P(None, None, "gy", "grp"),
        P(None, "gy", "grp"),
        P(None, "gy", "grp"),
        P(),
        P(None, "gy", "grp"),
        P("gy", "grp", None),
        P(("grp", "gy"), None, None),
    )
    return jax.shard_map(
        body,
        mesh=mesh,
        in_specs=placed,
        out_specs=(P(None, None, "gy", "grp"),) * 3,
        check_vma=False,
    )
```

```python
import functools

import jax
import jax.numpy as jnp
from jax import lax
from jax.experimental import pallas as pl
from jax.experimental.pallas import tpu as pltpu
from jax.sharding import PartitionSpec as P

SPECIES = 5
LAYERS = 4
MATS = 4
FIELDS = SPECIES * LAYERS
PLANES = FIELDS + 3 * LAYERS
POT0, CAP0, MAT0 = FIELDS, FIELDS + LAYERS, FIELDS + 2 * LAYERS
ROWS = 32
COLS = 128
N_GRP = 4
N_GY = 32
TOTAL = N_GRP * N_GY
NC = 512
DAMPING = 2.0 / 3.0
BOTH = ("grp", "gy")

HALO = 12
PER = 10
GROUPS = -(-PLANES // PER)
RHALO = 16
PAD = 8
WIDE = 2 * COLS
TALL = ROWS + 2 * RHALO + 2 * PAD
TOP = PAD + RHALO
F32 = jnp.float32

G_RW, G_RAU, G_S, G_CY, G_CX, G_MOM = 0, 4, 8, 14, 30, 46
ROW_CAP = 250
MAP_LANE = 20
INV_LANE = 24


def lanes(shape):
    return lax.broadcasted_iota(jnp.int32, shape, 1)


def subs(shape):
    return lax.broadcasted_iota(jnp.int32, shape, 0)


def pack_kernel(planes, to_low, to_high):
    lane = lanes((ROWS, COLS))
    for g in range(GROUPS):
        low = jnp.zeros((ROWS, COLS), F32)
        high = jnp.zeros((ROWS, COLS), F32)
        for j in range(min(PER, PLANES - g * PER)):
            v = planes[g * PER + j]
            inside = (lane >= HALO * j) & (lane < HALO * (j + 1))
            low = jnp.where(inside, turn(v, HALO * j), low)
            high = jnp.where(inside, turn(v, HALO * j + HALO), high)
        to_low[g] = low
        to_high[g] = high


def turn(v, shift):
    shift = shift % v.shape[1]
    return v if shift == 0 else pltpu.roll(v, shift, 1)


def place(rows):
    n = rows.shape[0]
    total = jnp.sum(rows, axis=1, keepdims=True)
    spread = jnp.where(lanes((n, COLS)) == subs((n, COLS)), total, 0.0)
    return jnp.sum(spread, axis=0, keepdims=True)


def fold(v):
    return jnp.sum(v, axis=0, keepdims=True)


def sums_kernel(planes, cmap, inverse, out, acc, ids):
    acc[...] = jnp.zeros(acc.shape, F32)
    row = jnp.zeros((1, COLS), F32)
    for s in range(SPECIES):
        acc[0:4, 0:SPECIES] = inverse[s]
        for k in range(4):
            row = row + turn(acc[k : k + 1, :], INV_LANE + (k * SPECIES + s) * SPECIES)
    acc[0:4, :] = jnp.zeros((4, COLS), F32)
    ids[...] = jnp.zeros(ids.shape, jnp.int32)
    ids[0:1, 0:MATS] = cmap[0]
    q = ids[0:1, :]
    row = row + turn(((q & 3) * TOTAL + (q >> 2)).astype(F32), MAP_LANE)
    for s in range(SPECIES):
        for m in range(MATS):
            total = jnp.zeros((ROWS, COLS), F32)
            for l in range(LAYERS):
                total = total + jnp.where(planes[MAT0 + l] == m, planes[s * LAYERS + l], 0.0)
            acc[m * SPECIES + s : m * SPECIES + s + 1, :] = fold(total)
    row = row + place(acc[...])
    out[...] = jnp.broadcast_to(row, (TOTAL, COLS))


def rows_kernel(planes, from_low, from_high, to_low, to_high):
    for k in range(PLANES):
        to_low[k] = planes[k, :RHALO]
        to_high[k] = planes[k, ROWS - RHALO :]
    for g in range(GROUPS):
        for i, part in enumerate((from_low, from_high)):
            k = PLANES + i * GROUPS + g
            to_low[k] = part[g, :RHALO]
            to_high[k] = part[g, ROWS - RHALO :]


def unpack_halo(low, high, j, fill):
    shape = low.shape
    lane = lanes(shape)
    right = turn(high, -HALO * j)
    left = turn(low, -HALO * (j + 1))
    return jnp.where(lane < HALO, right, jnp.where(lane >= COLS - HALO, left, fill))


def after(v, nxt, axis):
    first = lax.broadcasted_iota(jnp.int32, v.shape, axis) == 0
    return pltpu.roll(jnp.where(first, nxt, v), v.shape[axis] - 1, axis)


def before(v, prev, axis):
    last = lax.broadcasted_iota(jnp.int32, v.shape, axis) == v.shape[axis] - 1
    return pltpu.roll(jnp.where(last, prev, v), 1, axis)


def stencil(src, ops, s, tiles, exact, emit):
    cap, gy, gx, gz = ops[:4]
    base = s * LAYERS

    def load(ref, l, row):
        return ref[base + l, pl.ds(row, 8), :]

    now = [load(src, l, tiles[0]) for l in range(LAYERS)]
    flux = [None] * LAYERS
    if exact:
        for l in range(LAYERS):
            u = load(src, l, tiles[0] - 8)
            flux[l] = load(gy, l, tiles[0] - 8) * (u - after(u, now[l], 0))
    for row in tiles:
        outer = row == tiles[-1] and not exact
        nxt = now if outer else [load(src, l, row + 8) for l in range(LAYERS)]
        flux_z = None
        for l in range(LAYERS):
            u = now[l]
            flux_x = load(gx, l, row) * (u - pltpu.roll(u, WIDE - 1, 1))
            out = cap[l, pl.ds(row, 8), :] * u + (flux_x - pltpu.roll(flux_x, 1, 1))
            flux_y = load(gy, l, row) * (u - after(u, nxt[l], 0))
            out = out + (flux_y - before(flux_y, flux_y if flux[l] is None else flux[l], 0))
            flux[l] = flux_y
            if flux_z is not None:
                out = out - flux_z
            if l + 1 < LAYERS:
                flux_z = load(gz, l, row) * (u - now[l + 1])
                out = out + flux_z
            emit(row, l, u, out)
        now = nxt


def tile_rows(first, last):
    return [PAD + 8 * t for t in range(first, last + 1)]


def sweep(src, resid, dst, ops, tiles):
    scale = ops[4]

    @pl.loop(0, SPECIES)
    def _(s):
        def emit(row, l, u, out):
            k, here = s * LAYERS + l, pl.ds(row, 8)
            dst[k, here, :] = u + scale[k, here, :] * (resid[k, here, :] - out)

        stencil(src, ops, s, tiles, False, emit)


def image(src, dst, ops, tiles):
    @pl.loop(0, SPECIES)
    def _(s):
        def emit(row, l, u, out):
            dst[s * LAYERS + l, pl.ds(row, 8), :] = out

        stencil(src, ops, s, tiles, False, emit)


def start_sweep(resid, dst, scale, tiles):
    @pl.loop(0, SPECIES)
    def _(s):
        for row in tiles:
            for l in range(LAYERS):
                k = s * LAYERS + l
                here = pl.ds(row, 8)
                dst[k, here, :] = scale[k, here, :] * resid[k, here, :]


def split3(x):
    hi = x.astype(jnp.bfloat16)
    rest = x - hi.astype(F32)
    mid = rest.astype(jnp.bfloat16)
    lo = (rest - mid.astype(F32)).astype(jnp.bfloat16)
    return jnp.concatenate([hi, mid, lo], axis=0)


def exact_dot(x, onehot):
    n = x.shape[0]
    y = jnp.dot(
        jnp.concatenate([split3(x)], axis=0), onehot, preferred_element_type=F32
    )
    return y[:n] + y[n : 2 * n] + y[2 * n :]


def build_scatter(got, onehot):
    for m in range(MATS):
        col = jnp.broadcast_to(got[:, MAP_LANE + m : MAP_LANE + m + 1], (TOTAL, COLS))
        for k in range(4):
            target = (lanes((TOTAL, COLS)) + k * COLS).astype(F32)
            onehot[m * TOTAL : (m + 1) * TOTAL, k * COLS : (k + 1) * COLS] = jnp.where(
                col == target, 1.0, 0.0
            ).astype(jnp.bfloat16)


def build_gather(turned, onehot):
    for m in range(MATS):
        row = jnp.broadcast_to(turned[MAP_LANE + m : MAP_LANE + m + 1, :], (COLS, TOTAL))
        for k in range(4):
            target = (subs((COLS, TOTAL)) + k * COLS).astype(F32)
            onehot[k * COLS : (k + 1) * COLS, m * TOTAL : (m + 1) * TOTAL] = jnp.where(
                row == target, 1.0, 0.0
            ).astype(jnp.bfloat16)


def build_near(got, onehot):
    gx, gy = lax.axis_index("grp"), lax.axis_index("gy")
    lane = lanes((1, COLS))
    row = jnp.full((1, COLS), -1.0, F32)
    for iy in range(3):
        y = lax.rem(gy + (N_GY - 1 + iy), N_GY)
        for ix in range(3):
            x = jnp.clip(gx + (ix - 1), 0, N_GRP - 1)
            region = iy * 3 + ix
            here = got[pl.ds(x * N_GY + y, 1), :]
            inside = (lane >= region * MATS) & (lane < (region + 1) * MATS)
            row = jnp.where(inside, turn(here, region * MATS - MAP_LANE), row)
    for k in range(4):
        target = (subs((COLS, COLS)) + k * COLS).astype(F32)
        onehot[k * COLS : (k + 1) * COLS, :] = jnp.where(
            jnp.broadcast_to(row, (COLS, COLS)) == target, 1.0, 0.0
        ).astype(jnp.bfloat16)


def coarse_solve(sums, turned, scatter):
    res = exact_dot(sums, scatter[...])
    parts = []
    for k in range(4):
        total = None
        for t in range(SPECIES):
            start = INV_LANE + k * SPECIES * SPECIES + t * SPECIES
            term = turned[start : start + 8, :] * res[t : t + 1, k * COLS : (k + 1) * COLS]
            total = term if total is None else total + term
        parts.append(total)
    sol = jnp.concatenate(parts, axis=1)
    return jnp.where(subs(sol.shape) < SPECIES, sol, 0.0)


def local_sums(turned, group):
    x = jnp.concatenate(
        [turned[(group + m) * SPECIES : (group + m) * SPECIES + 8, :] for m in range(MATS)], axis=1
    )
    return jnp.where(subs(x.shape) < SPECIES, x, 0.0)


def spread_values(near, values):
    lane = lanes((8, COLS))
    for iy in range(3):
        for m in range(MATS):
            cols = [
                jnp.broadcast_to(
                    near[:, (iy * 3 + ix) * MATS + m : (iy * 3 + ix) * MATS + m + 1], (8, COLS)
                )
                for ix in range(3)
            ]
            values[iy * MATS + m, :, 0:COLS] = cols[1]
            values[iy * MATS + m, :, COLS:WIDE] = jnp.where(lane < COLS // 2, cols[2], cols[0])


def region_of(row):
    return 0 if row < TOP else (1 if row < TOP + ROWS else 2)


def coarse_at(values, mat_tile, s, row):
    iy = region_of(row)
    n = mat_tile.shape[1]
    v = [
        jnp.broadcast_to(values[iy * MATS + m, pl.ds(s, 1), :][:, :n], mat_tile.shape)
        for m in range(MATS)
    ]
    out = jnp.where(mat_tile == 1.0, v[1], v[0])
    out = jnp.where(mat_tile == 2.0, v[2], out)
    return jnp.where(mat_tile == 3.0, v[3], out)


def fill_plane(dst, index, k, own, x_low, x_high, y_low, y_high, fill):
    g, j = divmod(k, PER)
    dst[index, PAD : PAD + RHALO, 0:COLS] = y_low[k]
    dst[index, TOP : TOP + ROWS, 0:COLS] = own
    dst[index, TOP + ROWS : TOP + ROWS + RHALO, 0:COLS] = y_high[k]
    dst[index, PAD : PAD + RHALO, COLS:WIDE] = unpack_halo(
        y_low[PLANES + g], y_low[PLANES + GROUPS + g], j, fill
    )
    dst[index, TOP : TOP + ROWS, COLS:WIDE] = unpack_halo(x_low[g], x_high[g], j, fill)
    dst[index, TOP + ROWS : TOP + ROWS + RHALO, COLS:WIDE] = unpack_halo(
        y_high[PLANES + g], y_high[PLANES + GROUPS + g], j, fill
    )


def harmonic(a, b):
    return 2.0 * a * b / (a + b)


def table_kernel(
    diff, planes, x_low, x_high, y_low, y_high,
    cap_w, mat_w, gy, gx, gz, scale, y0, acc,
    b_w, w, za, code_y, code_x, code_z, code_cx,
):
    halves = (x_low, x_high, y_low, y_high)
    for k in range(FIELDS):
        fill_plane(b_w, k, k, planes[k], *halves, 0.0)
    for l in range(LAYERS):
        fill_plane(za, l, POT0 + l, planes[POT0 + l], *halves, 0.0)
        fill_plane(cap_w, l, CAP0 + l, planes[CAP0 + l], *halves, 1.0)
        fill_plane(mat_w, l, MAT0 + l, planes[MAT0 + l], *halves, 0.0)

    for row in tile_rows(0, 7):
        for l in range(LAYERS):
            here = pl.ds(row, 8)
            m = mat_w[l, here, :]
            is1, is2, is3 = m == 1.0, m == 2.0, m == 3.0
            down = jnp.exp(-0.5 * za[l, here, :])
            up = jnp.exp(0.5 * za[l, here, :])
            drift = (down, up, down * down, up * up, down)
            for s in range(SPECIES):
                d = jnp.where(is1, diff[1, s], diff[0, s])
                d = jnp.where(is2, diff[2, s], d)
                d = jnp.where(is3, diff[3, s], d)
                w[s * LAYERS + l, here, :] = d * drift[s]

    me_x = lax.axis_index("grp")
    lane = lanes((8, WIDE))
    closed = ((lane == COLS - 1) & (me_x == N_GRP - 1)) | ((lane == WIDE - 1) & (me_x == 0))
    all_tiles, mid, own = tile_rows(0, 7), tile_rows(1, 6), tile_rows(2, 5)

    @pl.loop(0, SPECIES)
    def _(s):
        def load(l, row):
            return w[s * LAYERS + l, pl.ds(row, 8), :]

        now = [load(l, all_tiles[0]) for l in range(LAYERS)]
        edge_y = [None] * LAYERS
        for row in all_tiles:
            here = pl.ds(row, 8)
            nxt = now if row == all_tiles[-1] else [load(l, row + 8) for l in range(LAYERS)]
            ez_below = None
            for l in range(LAYERS):
                k = s * LAYERS + l
                c = now[l]
                ey = harmonic(c, after(c, nxt[l], 0))
                ex = jnp.where(closed, 0.0, harmonic(c, pltpu.roll(c, WIDE - 1, 1)))
                gy[k, here, :] = ey
                gx[k, here, :] = ex
                d = cap_w[l, here, :] + ey + before(ey, ey if edge_y[l] is None else edge_y[l], 0)
                d = d + ex + pltpu.roll(ex, 1, 1)
                edge_y[l] = ey
                if ez_below is not None:
                    d = d + ez_below
                if l + 1 < LAYERS:
                    ez_below = 0.5 * harmonic(c, now[l + 1])
                    gz[k, here, :] = ez_below
                    d = d + ez_below
                scale[k, here, :] = DAMPING / d
            now = nxt

    ops = (cap_w, gy, gx, gz, scale)
    start_sweep(b_w, za, scale, all_tiles)
    sweep(za, b_w, y0, ops, all_tiles)
    sweep(y0, b_w, za, ops, all_tiles)
    sweep(za, b_w, y0, ops, mid)

    acc[...] = jnp.zeros(acc.shape, F32)
    own_lane = lanes((8, COLS))
    sub = subs((8, COLS))

    def power(m):
        p = jnp.where(m == 1.0, 2.0, 1.0)
        p = jnp.where(m == 2.0, 4.0, p)
        return jnp.where(m == 3.0, 8.0, p)

    for row in own:
        rows = pl.ds(row - TOP, 8)
        side = jnp.full((8, COLS), -1.0, F32)
        for l in range(LAYERS):
            m_wide = mat_w[l, pl.ds(row, 8), :]
            m = m_wide[:, :COLS]
            m_y = after(m, mat_w[l, pl.ds(row + 8, 8), 0:COLS], 0)
            m_x = pltpu.roll(m_wide, WIDE - 1, 1)[:, :COLS]
            p = power(m)
            code = p + power(m_y)
            if row == own[-1]:
                code = jnp.where(sub == 7, -1.0 - (m * 4.0 + m_y), code)
            code_y[l, rows, :] = code
            code_x[l, rows, :] = jnp.where(own_lane == COLS - 1, 0.0, p + power(m_x))
            if l + 1 < LAYERS:
                code_z[l, rows, :] = p + power(mat_w[l + 1, pl.ds(row, 8), 0:COLS])
            side = jnp.where(own_lane == COLS - 1 - l, turn(m * 4.0 + m_x, -l), side)
        code_cx[rows, :] = side

    @pl.loop(0, SPECIES)
    def _(s):
        zero = jnp.zeros((8, COLS), F32)
        pairs, cy, cx = [zero] * 6, [zero] * 16, [zero] * 16
        codes = (3.0, 5.0, 9.0, 6.0, 10.0, 12.0)
        for row in own:
            here, rows = pl.ds(row, 8), pl.ds(row - TOP, 8)
            side = zero
            for l in range(LAYERS):
                k = s * LAYERS + l
                ex = gx[k, here, 0:COLS]
                ey = gy[k, here, 0:COLS]
                kinds = [(code_y[l, rows, :], ey), (code_x[l, rows, :], ex)]
                if l + 1 < LAYERS:
                    kinds.append((code_z[l, rows, :], gz[k, here, 0:COLS]))
                for code, edge in kinds:
                    for i in range(6):
                        pairs[i] = pairs[i] + jnp.where(code == codes[i], edge, 0.0)
                if row == own[-1]:
                    for i in range(16):
                        cy[i] = cy[i] + jnp.where(kinds[0][0] == -1.0 - i, ey, 0.0)
                side = jnp.where(own_lane == COLS - 1 - l, turn(ex, -l), side)
            code = code_cx[rows, :]
            for i in range(16):
                cx[i] = cx[i] + jnp.where(code == float(i), side, 0.0)
        for group, sums in ((G_S, pairs), (G_CY, cy), (G_CX, cx)):
            for i, v in enumerate(sums):
                acc[pl.ds((group + i) * SPECIES + s, 1), :] = fold(v)

    for i in range(MATS):
        total = jnp.zeros((ROWS, COLS), F32)
        for l in range(LAYERS):
            total = total + jnp.where(planes[MAT0 + l] == i, planes[CAP0 + l], 0.0)
        acc[ROW_CAP + i : ROW_CAP + i + 1, :] = fold(total)


def first_kernel(
    planes, got, cap_w, mat_w, gy, gx, gz, scale, y0, acc_in,
    second, z0_out, w0_out, u_out,
    za, zb, w0, scatter, near_hot, turned, values, acc,
):
    ops = (cap_w, gy, gx, gz, scale)
    mid, own = tile_rows(1, 6), tile_rows(2, 5)

    turned[...] = got[...].T
    build_scatter(got, scatter)
    build_near(got, near_hot)
    sol = coarse_solve(local_sums(turned, 0), turned, scatter)
    spread_values(exact_dot(sol, near_hot[...]), values)

    @pl.loop(0, SPECIES)
    def _(s):
        for row in mid:
            here = pl.ds(row, 8)
            for l in range(LAYERS):
                k = s * LAYERS + l
                zb[k, here, :] = y0[k, here, :] + coarse_at(values, mat_w[l, here, :], s, row)

    for k in range(FIELDS):
        z0_out[k] = zb[k, TOP : TOP + ROWS, 0:COLS]
    image(zb, w0, ops, mid)
    for k in range(FIELDS):
        w0_out[k] = w0[k, TOP : TOP + ROWS, 0:COLS]
    start_sweep(w0, za, scale, mid)
    sweep(za, w0, zb, ops, mid)
    sweep(zb, w0, za, ops, mid)
    sweep(za, w0, u_out, ops, mid)

    acc[...] = acc_in[...]

    @pl.loop(0, SPECIES)
    def _(s):
        zero = jnp.zeros((8, COLS), F32)
        rw, rau, mom = [zero] * MATS, [zero] * MATS, [zero] * 4

        def emit(row, l, u, au):
            k, rows = s * LAYERS + l, pl.ds(row - TOP, 8)
            m = mat_w[l, pl.ds(row, 8), 0:COLS]
            u, au = u[:, :COLS], au[:, :COLS]
            wv, zv, bv = w0_out[k, rows, :], z0_out[k, rows, :], planes[k, rows, :]
            mom[0] = mom[0] + bv * zv
            mom[1] = mom[1] + zv * wv
            mom[2] = mom[2] + wv * u
            mom[3] = mom[3] + u * au
            for i in range(MATS):
                is_i = m == float(i)
                rw[i] = rw[i] + jnp.where(is_i, wv, 0.0)
                rau[i] = rau[i] + jnp.where(is_i, au, 0.0)

        stencil(u_out, ops, s, own, True, emit)
        for group, sums in ((G_RW, rw), (G_RAU, rau), (G_MOM, mom)):
            for i, v in enumerate(sums):
                acc[pl.ds((group + i) * SPECIES + s, 1), :] = fold(v)

    even = lax.rem(subs((WIDE, COLS)), 2) == 0
    second[...] = jnp.where(even, place(acc[0:COLS, :]), place(acc[COLS:WIDE, :]))


def next_y(x):
    y = lax.rem(lanes(x.shape), N_GY)
    return jnp.where(y == N_GY - 1, turn(x, N_GY - 1), turn(x, -1))


def prev_y(x):
    y = lax.rem(lanes(x.shape), N_GY)
    return jnp.where(y == 0, turn(x, -(N_GY - 1)), turn(x, 1))


def total_of(x):
    return jnp.sum(jnp.sum(x, axis=0, keepdims=True), axis=1, keepdims=True)


def second_kernel(
    planes, got, got2, cap, mat, gy, gx, gz, scale, z0, w0, u,
    out_x, out_r, out_z,
    v1, w1, za, zb, scatter, gather, near_hot, turned, turned2, values, values2,
):
    turned[...] = got[...].T
    turned2[0:COLS, :] = got2[pl.ds(0, TOTAL, stride=2), :].T
    turned2[COLS:WIDE, :] = got2[pl.ds(1, TOTAL, stride=2), :].T
    build_scatter(got, scatter)
    build_gather(turned, gather)
    build_near(got, near_hot)

    sums_w = local_sums(turned2, G_RW)
    sol = coarse_solve(sums_w, turned, scatter)
    spread_values(exact_dot(sol, near_hot[...]), values)
    c_all = exact_dot(sol, gather[...])
    c = [c_all[:, m * TOTAL : (m + 1) * TOTAL] for m in range(MATS)]

    def rows5(group):
        return turned2[group * SPECIES : group * SPECIES + 8, :]

    live = subs((8, TOTAL)) < SPECIES
    bc = [turned2[ROW_CAP + m : ROW_CAP + m + 1, :] * c[m] for m in range(MATS)]
    n = 0
    for i in range(MATS):
        for j in range(i + 1, MATS):
            f = rows5(G_S + n) * (c[i] - c[j])
            bc[i] = bc[i] + f
            bc[j] = bc[j] - f
            n += 1
    c_y = [next_y(v) for v in c]
    c_x = [turn(v, -N_GY) for v in c]
    back_y = [jnp.zeros((8, TOTAL), F32)] * MATS
    back_x = [jnp.zeros((8, TOTAL), F32)] * MATS
    for i in range(MATS):
        for j in range(MATS):
            f = rows5(G_CY + 4 * i + j) * (c[i] - c_y[j])
            bc[i] = bc[i] + f
            back_y[j] = back_y[j] + f
            f = rows5(G_CX + 4 * i + j) * (c[i] - c_x[j])
            bc[i] = bc[i] + f
            back_x[j] = back_x[j] + f
    for j in range(MATS):
        bc[j] = jnp.where(live, bc[j] - prev_y(back_y[j]) - turn(back_x[j], N_GY), 0.0)
    bc_all = jnp.concatenate(bc, axis=1)
    sums_au = local_sums(turned2, G_RAU)
    sol2 = coarse_solve(sums_au + bc_all, turned, scatter)
    spread_values(exact_dot(sol2, near_hot[...]), values2)

    def moment(i):
        return total_of(jnp.where(live, rows5(G_MOM + i), 0.0))

    m0, m1 = moment(0), moment(1)
    m2 = moment(2) + total_of(sums_w * c_all)
    m3 = moment(3) + total_of((2.0 * sums_au + bc_all) * c_all)
    a0 = m0 / m1
    rz1 = m0 - 2.0 * a0 * m1 + a0 * a0 * m2
    g = 1.0 + rz1 / m0
    a1 = rz1 / (g * g * m1 - 2.0 * a0 * g * m2 + a0 * a0 * m3)
    ca = jnp.broadcast_to(a0 + a1 * g, (8, COLS))
    cb = jnp.broadcast_to(a1 * a0, (8, COLS))

    ops = (cap, gy, gx, gz, scale)
    mid, own = tile_rows(1, 6), tile_rows(2, 5)

    @pl.loop(0, SPECIES)
    def _(s):
        for row in mid:
            here = pl.ds(row, 8)
            for l in range(LAYERS):
                k = s * LAYERS + l
                v1[k, here, :] = u[k, here, :] + coarse_at(values, mat[l, here, :], s, row)

    image(v1, w1, ops, mid)
    start_sweep(w1, za, scale, mid)
    sweep(za, w1, zb, ops, mid)
    sweep(zb, w1, za, ops, mid)

    @pl.loop(0, SPECIES)
    def _(s):
        def emit(row, l, u_, out):
            k, here, rows = s * LAYERS + l, pl.ds(row, 8), pl.ds(row - TOP, 8)
            w1v = w1[k, here, 0:COLS]
            v2 = u_[:, :COLS] + scale[k, here, 0:COLS] * (w1v - out[:, :COLS])
            v2 = v2 + coarse_at(values2, mat[l, here, 0:COLS], s, row)
            v1v = v1[k, here, 0:COLS]
            z0v, w0v = z0[k, rows, :], w0[k, rows, :]
            out_x[k, rows, :] = ca * z0v - cb * v1v
            out_r[k, rows, :] = planes[k, rows, :] - ca * w0v + cb * w1v
            out_z[k, rows, :] = z0v - ca * v1v + cb * v2

        stencil(za, ops, s, own, True, emit)


def shape(*dims):
    return jax.ShapeDtypeStruct(dims, F32)


VMEM = pl.BlockSpec(memory_space=pltpu.VMEM)
SMEM = pl.BlockSpec(memory_space=pltpu.SMEM)
PARAMS = pltpu.CompilerParams(vmem_limit_bytes=18 * 1024 * 1024)


def run(kernel, outs, scratch, in_specs, cost, *args):
    return pl.pallas_call(
        kernel,
        out_shape=outs,
        in_specs=in_specs,
        out_specs=jax.tree.map(lambda _: VMEM, outs),
        scratch_shapes=scratch,
        compiler_params=PARAMS,
        cost_estimate=pl.CostEstimate(flops=cost, bytes_accessed=1 << 20, transcendentals=0),
    )(*args)


def shifts(axis, count):
    forward = [(i, (i + 1) % count) for i in range(count)]
    backward = [(target, source) for source, target in forward]
    return (functools.partial(lax.ppermute, axis_name=axis, perm=p) for p in (forward, backward))


def to_all(rows):
    got = lax.all_to_all(rows.reshape(TOTAL, -1, COLS), BOTH, 0, 0, tiled=True)
    return got.reshape(rows.shape)


def body(right_side, potential, capacity, diffusivity, material, coarse_map, coarse_inverse):
    b = right_side.reshape(FIELDS, ROWS, COLS)
    right, left = shifts("grp", N_GRP)
    down, up = shifts("gy", N_GY)

    planes = jnp.concatenate([b, potential, capacity, material.astype(F32)])
    packed = shape(GROUPS, ROWS, COLS)
    to_low, to_high = run(pack_kernel, (packed, packed), [], [VMEM], 1 << 20, planes)
    x_low, x_high = right(to_high), left(to_low)
    first = run(
        sums_kernel,
        shape(TOTAL, COLS),
        [pltpu.VMEM((24, COLS), F32), pltpu.VMEM((8, COLS), jnp.int32)],
        [VMEM] * 3,
        1 << 20,
        planes, coarse_map, jnp.transpose(coarse_inverse, (1, 0, 2)),
    )

    strips = shape(PLANES + 2 * GROUPS, RHALO, COLS)
    to_low, to_high = run(
        rows_kernel, (strips, strips), [], [VMEM] * 3, 1 << 20, planes, x_low, x_high
    )
    first, to_low, to_high = lax.optimization_barrier((first, to_low, to_high))
    y_low, y_high = down(to_high), up(to_low)
    got, y_low, y_high = lax.optimization_barrier((to_all(first), y_low, y_high))

    wide = shape(FIELDS, TALL, WIDE)
    thin = shape(LAYERS, TALL, WIDE)
    field = shape(FIELDS, ROWS, COLS)
    big = pltpu.VMEM((FIELDS, TALL, WIDE), F32)
    hot = pltpu.VMEM((NC, MATS * TOTAL), jnp.bfloat16)
    near = pltpu.VMEM((NC, COLS), jnp.bfloat16)
    code = pltpu.VMEM((LAYERS, ROWS, COLS), F32)
    values = pltpu.VMEM((3 * MATS, 8, WIDE), F32)
    cap_w, mat_w, gy, gx, gz, scale, y0, acc = run(
        table_kernel,
        (thin, thin, wide, wide, wide, wide, wide, shape(WIDE, COLS)),
        [big] * 3 + [code] * 3 + [pltpu.VMEM((ROWS, COLS), F32)],
        [SMEM] + [VMEM] * 5,
        1 << 30,
        diffusivity.T, planes, x_low, x_high, y_low, y_high,
    )
    second, z0, w0, u = run(
        first_kernel,
        (shape(2 * TOTAL, COLS), field, field, wide),
        [big] * 3 + [hot, near, pltpu.VMEM((COLS, COLS), F32), values, pltpu.VMEM((WIDE, COLS), F32)],
        [VMEM] * 10,
        1 << 30,
        planes, got, cap_w, mat_w, gy, gx, gz, scale, y0, acc,
    )
    got2 = to_all(second)
    out = run(
        second_kernel,
        (field, field, field),
        [big] * 4
        + [hot, hot, near, pltpu.VMEM((COLS, COLS), F32), pltpu.VMEM((WIDE, COLS), F32), values, values],
        [VMEM] * 12,
        1 << 30,
        planes, got, got2, cap_w, mat_w, gy, gx, gz, scale, z0, w0, u,
    )
    return tuple(o.reshape(right_side.shape) for o in out)


def solution(mesh):
    placed = (
        P(None, None, "gy", "grp"),
        P(None, "gy", "grp"),
        P(None, "gy", "grp"),
        P(),
        P(None, "gy", "grp"),
        P("gy", "grp", None),
        P(("grp", "gy"), None, None),
    )
    return jax.shard_map(
        body,
        mesh=mesh,
        in_specs=placed,
        out_specs=(P(None, None, "gy", "grp"),) * 3,
        check_vma=False,
    )
```

```python
import functools

import jax
import jax.numpy as jnp
from jax import lax
from jax.experimental import pallas as pl
from jax.experimental.pallas import tpu as pltpu
from jax.sharding import PartitionSpec as P

SPECIES = 5
LAYERS = 4
MATS = 4
FIELDS = SPECIES * LAYERS
PLANES = FIELDS + 3 * LAYERS
POT0, CAP0, MAT0 = FIELDS, FIELDS + LAYERS, FIELDS + 2 * LAYERS
ROWS = 32
COLS = 128
N_GRP = 4
N_GY = 32
TOTAL = N_GRP * N_GY
NC = 512
DAMPING = 2.0 / 3.0
BOTH = ("grp", "gy")

HALO = 12
PER = 10
GROUPS = -(-PLANES // PER)
RHALO = 16
TALL = ROWS + 2 * RHALO
TOP = RHALO
HALF = COLS // 2
LATE = COLS + HALO - HALF
SEAM = 96
F32 = jnp.float32

G_RW, G_RAU, G_S, G_CY, G_CX, G_MOM = 0, 4, 8, 14, 30, 46
ROW_CAP = 250
MAP_LANE = 20
INV_LANE = 24


def lanes(shape):
    return lax.broadcasted_iota(jnp.int32, shape, 1)


def subs(shape):
    return lax.broadcasted_iota(jnp.int32, shape, 0)


def pack_kernel(planes, to_low, to_high):
    lane = lanes((ROWS, COLS))
    for g in range(GROUPS):
        low = jnp.zeros((ROWS, COLS), F32)
        high = jnp.zeros((ROWS, COLS), F32)
        for j in range(min(PER, PLANES - g * PER)):
            v = planes[g * PER + j]
            inside = (lane >= HALO * j) & (lane < HALO * (j + 1))
            low = jnp.where(inside, turn(v, HALO * j), low)
            high = jnp.where(inside, turn(v, HALO * j + HALO), high)
        to_low[g] = low
        to_high[g] = high


def turn(v, shift):
    shift = shift % v.shape[1]
    return v if shift == 0 else pltpu.roll(v, shift, 1)


def place(rows):
    n = rows.shape[0]
    total = jnp.sum(rows, axis=1, keepdims=True)
    spread = jnp.where(lanes((n, COLS)) == subs((n, COLS)), total, 0.0)
    return jnp.sum(spread, axis=0, keepdims=True)


def fold(v):
    return jnp.sum(v, axis=0, keepdims=True)


def harmonic(a, b):
    return 2.0 * a * b / (a + b)


def after(v, nxt, axis):
    first = lax.broadcasted_iota(jnp.int32, v.shape, axis) == 0
    return pltpu.roll(jnp.where(first, nxt, v), v.shape[axis] - 1, axis)


def power(m):
    p = jnp.where(m == 1.0, 2.0, 1.0)
    p = jnp.where(m == 2.0, 4.0, p)
    return jnp.where(m == 3.0, 8.0, p)


def own_kernel(diff, planes, cmap, inverse, out, acc, w, code_y, code_x, code_z, part, ids):
    part[...] = jnp.zeros(part.shape, F32)
    row = jnp.zeros((1, COLS), F32)
    for s in range(SPECIES):
        part[0:4, 0:SPECIES] = inverse[s]
        for k in range(4):
            row = row + turn(part[k : k + 1, :], INV_LANE + (k * SPECIES + s) * SPECIES)
    part[0:4, :] = jnp.zeros((4, COLS), F32)
    ids[...] = jnp.zeros(ids.shape, jnp.int32)
    ids[0:1, 0:MATS] = cmap[0]
    q = ids[0:1, :]
    row = row + turn(((q & 3) * TOTAL + (q >> 2)).astype(F32), MAP_LANE)
    for s in range(SPECIES):
        for m in range(MATS):
            total = jnp.zeros((ROWS, COLS), F32)
            for l in range(LAYERS):
                total = total + jnp.where(planes[MAT0 + l] == m, planes[s * LAYERS + l], 0.0)
            part[m * SPECIES + s : m * SPECIES + s + 1, :] = fold(total)
    out[...] = jnp.broadcast_to(row + place(part[...]), (TOTAL, COLS))

    acc[...] = jnp.zeros(acc.shape, F32)
    lane, sub = lanes((8, COLS)), subs((8, COLS))
    tiles = [8 * t for t in range(ROWS // 8)]
    for r in tiles:
        here = pl.ds(r, 8)
        for l in range(LAYERS):
            m = planes[MAT0 + l, here, :]
            is1, is2, is3 = m == 1.0, m == 2.0, m == 3.0
            down = jnp.exp(-0.5 * planes[POT0 + l, here, :])
            up = jnp.exp(0.5 * planes[POT0 + l, here, :])
            drift = (down, up, down * down, up * up, down)
            for s in range(SPECIES):
                d = jnp.where(is1, diff[1, s], diff[0, s])
                d = jnp.where(is2, diff[2, s], d)
                d = jnp.where(is3, diff[3, s], d)
                w[s * LAYERS + l, here, :] = d * drift[s]
            p = power(m)
            if r == tiles[-1]:
                code = jnp.where(sub == 7, 0.0, p + power(after(m, m, 0)))
            else:
                code = p + power(after(m, planes[MAT0 + l, pl.ds(r + 8, 8), :], 0))
            code_y[l, here, :] = code
            code_x[l, here, :] = jnp.where(lane == COLS - 1, 0.0, p + power(turn(m, -1)))
            if l + 1 < LAYERS:
                code_z[l, here, :] = p + power(planes[MAT0 + l + 1, here, :])

    @pl.loop(0, SPECIES)
    def _(s):
        pairs = [jnp.zeros((8, COLS), F32)] * 6
        codes = (3.0, 5.0, 9.0, 6.0, 10.0, 12.0)
        for r in tiles:
            here = pl.ds(r, 8)
            for l in range(LAYERS):
                k = s * LAYERS + l
                c = w[k, here, :]
                nxt = c if r == tiles[-1] else w[k, pl.ds(r + 8, 8), :]
                kinds = [
                    (code_y[l, here, :], harmonic(c, after(c, nxt, 0))),
                    (code_x[l, here, :], harmonic(c, turn(c, -1))),
                ]
                if l + 1 < LAYERS:
                    kinds.append((code_z[l, here, :], 0.5 * harmonic(c, w[k + 1, here, :])))
                for code, edge in kinds:
                    for i in range(6):
                        pairs[i] = pairs[i] + jnp.where(code == codes[i], edge, 0.0)
        for i in range(6):
            acc[pl.ds((G_S + i) * SPECIES + s, 1), :] = fold(pairs[i])

    for i in range(MATS):
        total = jnp.zeros((ROWS, COLS), F32)
        for l in range(LAYERS):
            total = total + jnp.where(planes[MAT0 + l] == i, planes[CAP0 + l], 0.0)
        acc[ROW_CAP + i : ROW_CAP + i + 1, :] = fold(total)


def rows_kernel(planes, from_low, from_high, to_low, to_high):
    for k in range(PLANES):
        to_low[k] = planes[k, :RHALO]
        to_high[k] = planes[k, ROWS - RHALO :]
    for g in range(GROUPS):
        for i, part in enumerate((from_low, from_high)):
            k = PLANES + i * GROUPS + g
            to_low[k] = part[g, :RHALO]
            to_high[k] = part[g, ROWS - RHALO :]


def at(l, y):
    return pl.ds(pl.multiple_of((y + l * TALL) * 8, 8), 8)


def each_row(first, count, step, carry=()):
    def block(i, carry):
        for r in range(4):
            carry = step(first + 4 * i + r, carry)
        return carry

    return lax.fori_loop(0, count // 4, block, carry)


def stencil(src, ops, wide, emit, carry=()):
    cap, gy, gx, gz = ops[:4]
    first = TOP - wide
    span = range(LAYERS)
    now = [src[at(l, first), :] for l in span]
    flux = [gy[at(l, first - 1), :] * (src[at(l, first - 1), :] - now[l]) for l in span]

    def step(y, carry):
        now, flux, carry = carry
        nxt, out_flux = [], []
        flux_z = None
        for l in span:
            here = at(l, y)
            u = now[l]
            above = src[at(l, y + 1), :]
            flux_x = gx[here, :] * (u - turn(u, -1))
            flux_y = gy[here, :] * (u - above)
            out = cap[here, :] * u + (flux_x - turn(flux_x, 1)) + (flux_y - flux[l])
            if flux_z is not None:
                out = out - flux_z
            if l + 1 < LAYERS:
                flux_z = gz[here, :] * (u - now[l + 1])
                out = out + flux_z
            nxt.append(above)
            out_flux.append(flux_y)
            carry = emit(l, y, u, out, carry)
        return nxt, out_flux, carry

    return each_row(first, ROWS + 2 * wide, step, (now, flux, carry))[2]


def sweep(src, resid, dst, ops, wide):
    scale = ops[4]

    def emit(l, y, u, out, carry):
        here = at(l, y)
        dst[here, :] = u + scale[here, :] * (resid[here, :] - out)
        return carry

    stencil(src, ops, wide, emit)


def image(src, dst, ops, wide):
    def emit(l, y, u, out, carry):
        dst[at(l, y), :] = out
        return carry

    stencil(src, ops, wide, emit)


def start_sweep(resid, dst, scale, wide):
    def step(y, carry):
        for l in range(LAYERS):
            here = at(l, y)
            dst[here, :] = scale[here, :] * resid[here, :]
        return carry

    each_row(TOP - wide, ROWS + 2 * wide, step)


def used(tile):
    lane, sub = lanes(tile.shape), subs(tile.shape)
    early = (sub < SPECIES) & (lane >= HALO) & (lane < HALO + SEAM)
    place_in = lane & (HALF - 1)
    late = (sub >= SPECIES) & (place_in >= SEAM - LATE) & (place_in < COLS - LATE)
    late = late & ((sub < 7) | (lane < HALF))
    return jnp.where(early | late, tile, 0.0)


def by_species(tile):
    lane, sub = lanes(tile.shape), subs(tile.shape)
    left = lane < HALF
    out = tile
    out = out + jnp.where((sub == 0) & left, pltpu.roll(tile, 3, 0), 0.0)
    pick = ((sub == 1) & ~left) | ((sub == 2) & left)
    out = out + jnp.where(pick, pltpu.roll(tile, 4, 0), 0.0)
    pick = ((sub == 3) & ~left) | ((sub == 4) & left)
    out = out + jnp.where(pick, pltpu.roll(tile, 5, 0), 0.0)
    return out[:SPECIES]


def keep(acc, group, tile):
    acc[group * SPECIES : (group + 1) * SPECIES, :] = by_species(tile)


def split3(x):
    hi = x.astype(jnp.bfloat16)
    rest = x - hi.astype(F32)
    mid = rest.astype(jnp.bfloat16)
    lo = (rest - mid.astype(F32)).astype(jnp.bfloat16)
    return jnp.concatenate([hi, mid, lo], axis=0)


def exact_dot(x, onehot):
    n = x.shape[0]
    y = jnp.dot(
        jnp.concatenate([split3(x)], axis=0), onehot, preferred_element_type=F32
    )
    return y[:n] + y[n : 2 * n] + y[2 * n :]


def build_scatter(got, onehot):
    for m in range(MATS):
        col = jnp.broadcast_to(got[:, MAP_LANE + m : MAP_LANE + m + 1], (TOTAL, COLS))
        for k in range(4):
            target = (lanes((TOTAL, COLS)) + k * COLS).astype(F32)
            onehot[m * TOTAL : (m + 1) * TOTAL, k * COLS : (k + 1) * COLS] = jnp.where(
                col == target, 1.0, 0.0
            ).astype(jnp.bfloat16)


def build_gather(turned, onehot):
    for m in range(MATS):
        row = jnp.broadcast_to(turned[MAP_LANE + m : MAP_LANE + m + 1, :], (COLS, TOTAL))
        for k in range(4):
            target = (subs((COLS, TOTAL)) + k * COLS).astype(F32)
            onehot[k * COLS : (k + 1) * COLS, m * TOTAL : (m + 1) * TOTAL] = jnp.where(
                row == target, 1.0, 0.0
            ).astype(jnp.bfloat16)


def build_near(got, onehot):
    gx, gy = lax.axis_index("grp"), lax.axis_index("gy")
    lane = lanes((1, COLS))
    row = jnp.full((1, COLS), -1.0, F32)
    for iy in range(3):
        y = lax.rem(gy + (N_GY - 1 + iy), N_GY)
        for ix in range(3):
            x = jnp.clip(gx + (ix - 1), 0, N_GRP - 1)
            region = iy * 3 + ix
            here = got[pl.ds(x * N_GY + y, 1), :]
            inside = (lane >= region * MATS) & (lane < (region + 1) * MATS)
            row = jnp.where(inside, turn(here, region * MATS - MAP_LANE), row)
    for k in range(4):
        target = (subs((COLS, COLS)) + k * COLS).astype(F32)
        onehot[k * COLS : (k + 1) * COLS, :] = jnp.where(
            jnp.broadcast_to(row, (COLS, COLS)) == target, 1.0, 0.0
        ).astype(jnp.bfloat16)


def coarse_solve(sums, turned, scatter):
    res = exact_dot(sums, scatter[...])
    parts = []
    for k in range(4):
        total = None
        for t in range(SPECIES):
            start = INV_LANE + k * SPECIES * SPECIES + t * SPECIES
            term = turned[start : start + 8, :] * res[t : t + 1, k * COLS : (k + 1) * COLS]
            total = term if total is None else total + term
        parts.append(total)
    sol = jnp.concatenate(parts, axis=1)
    return jnp.where(subs(sol.shape) < SPECIES, sol, 0.0)


def local_sums(turned, group):
    x = jnp.concatenate(
        [turned[(group + m) * SPECIES : (group + m) * SPECIES + 8, :] for m in range(MATS)], axis=1
    )
    return jnp.where(subs(x.shape) < SPECIES, x, 0.0)


def spread_values(near, values):
    lane, sub = lanes((8, COLS)), subs((8, COLS))

    def arrange(a, b, c):
        row = lambda s: jnp.broadcast_to(near[s : s + 1, :], (8, COLS))
        out = jnp.where(sub == 5, row(a), near)
        return jnp.where(sub == 7, row(c), jnp.where(sub == 6, row(b), out))

    left, right = arrange(0, 2, 4), arrange(1, 3, 4)
    early = sub < SPECIES
    for iy in range(3):
        for m in range(MATS):
            column = lambda v, ix: jnp.broadcast_to(
                v[:, (iy * 3 + ix) * MATS + m : (iy * 3 + ix) * MATS + m + 1], (8, COLS)
            )
            first = jnp.where(early & (lane < HALO), column(left, 0), column(left, 1))
            first = jnp.where(~early & (lane >= COLS - LATE), column(left, 2), first)
            second = jnp.where(lane >= HALF + COLS - LATE, column(right, 2), column(right, 1))
            values[(iy * MATS + m) * 8 : (iy * MATS + m + 1) * 8, :] = jnp.where(
                early | (lane < HALF), first, second
            )


def coarse_rows(values, mat, wide, emit):
    for iy, first, count in ((0, TOP - wide, wide), (1, TOP, ROWS), (2, TOP + ROWS, wide)):
        if count == 0:
            continue
        v = [values[(iy * MATS + m) * 8 : (iy * MATS + m + 1) * 8, :] for m in range(MATS)]

        def step(y, carry):
            for l in range(LAYERS):
                emit(l, y, coarse_pick(v, mat[at(l, y), :]))
            return carry

        each_row(first, count, step)


def coarse_pick(v, m):
    out = jnp.where(m == 1.0, v[1], v[0])
    out = jnp.where(m == 2.0, v[2], out)
    return jnp.where(m == 3.0, v[3], out)


def table_kernel(
    diff, planes, x_low, x_high, y_low, y_high, acc_in,
    cap_w, mat_w, gy, gx, gz, scale, y0, acc, b_w,
    w, za,
):
    lane, sub = lanes((8, COLS)), subs((8, COLS))
    left = lane < HALF

    def pick(strip, own, k, t):
        if t < 2:
            return y_low[strip, 8 * t : 8 * t + 8, :]
        if t < 6:
            return own[k, 8 * (t - 2) : 8 * (t - 2) + 8, :]
        return y_high[strip, 8 * (t - 6) : 8 * (t - 6) + 8, :]

    def both(k, t):
        g, j = divmod(k, PER)
        v = pick(k, planes, k, t)
        low = pick(PLANES + g, x_low, g, t)
        high = pick(PLANES + GROUPS + g, x_high, g, t)
        early = jnp.where(lane < HALO, turn(low, -HALO * j), turn(v, HALO))
        late = jnp.where(lane < COLS - LATE, turn(v, -LATE), turn(high, COLS - LATE - HALO * j))
        return early, late

    def put(dst, l, t, s, v):
        dst[pl.ds((l * TALL + 8 * t) * 8 + s, 8, stride=8), :] = v

    pairs = ((0, 1), (2, 3), (4, 4))
    d_late = [
        [jnp.where(left, diff[m, a], diff[m, b]) for m in range(MATS)] for a, b in pairs
    ]

    def choose(v, is1, is2, is3):
        return jnp.where(is3, v[3], jnp.where(is2, v[2], jnp.where(is1, v[1], v[0])))

    for l in range(LAYERS):
        for t in range(TALL // 8):
            late_b = []
            for s in range(SPECIES):
                early, late = both(s * LAYERS + l, t)
                put(b_w, l, t, s, early)
                late_b.append(late)
            for i, (a, b) in enumerate(pairs):
                put(b_w, l, t, SPECIES + i, jnp.where(left, late_b[a], turn(late_b[b], HALF)))
            for dst, base in ((cap_w, CAP0), (mat_w, MAT0)):
                early, late = both(base + l, t)
                late = jnp.where(left, late, turn(late, HALF))
                for s in range(8):
                    put(dst, l, t, s, early if s < SPECIES else late)
            m_early, m_late = early, late
            early, late = both(POT0 + l, t)
            late = jnp.where(left, late, turn(late, HALF))
            is_m = [m_early == float(m) for m in (1, 2, 3)]
            down, up = jnp.exp(-0.5 * early), jnp.exp(0.5 * early)
            drift = (down, up, down * down, up * up, down)
            for s in range(SPECIES):
                put(w, l, t, s, choose([diff[m, s] for m in range(MATS)], *is_m) * drift[s])
            is_m = [m_late == float(m) for m in (1, 2, 3)]
            down, up = jnp.exp(-0.5 * late), jnp.exp(0.5 * late)
            mixed = jnp.where(left, down, up)
            drift = (mixed, mixed * mixed, down)
            for i in range(3):
                put(w, l, t, SPECIES + i, choose(d_late[i], *is_m) * drift[i])

    me_x = lax.axis_index("grp")
    closed = ((sub >= SPECIES) & ((lane & (HALF - 1)) == COLS - 1 - LATE) & (me_x == N_GRP - 1)) | (
        (sub < SPECIES) & (lane == HALO - 1) & (me_x == 0)
    )
    span = range(LAYERS)
    first = TOP - 12

    def edge_step(y, carry):
        now, edge_y = carry
        nxt, out_y = [], []
        ez_below = None
        for l in span:
            here = at(l, y)
            c = now[l]
            above = w[at(l, y + 1), :]
            ey = harmonic(c, above)
            ex = jnp.where(closed, 0.0, harmonic(c, turn(c, -1)))
            gy[here, :] = ey
            gx[here, :] = ex
            d = cap_w[here, :] + ey + edge_y[l] + ex + turn(ex, 1)
            if ez_below is not None:
                d = d + ez_below
            if l + 1 < LAYERS:
                ez_below = 0.5 * harmonic(c, now[l + 1])
                gz[here, :] = ez_below
                d = d + ez_below
            scale[here, :] = DAMPING / d
            nxt.append(above)
            out_y.append(ey)
        return nxt, out_y

    now = [w[at(l, first), :] for l in span]
    edge_y = [harmonic(w[at(l, first - 1), :], now[l]) for l in span]
    each_row(first, ROWS + 24, edge_step, (now, edge_y))

    ops = (cap_w, gy, gx, gz, scale)
    start_sweep(b_w, za, scale, 12)
    sweep(za, b_w, y0, ops, 10)
    sweep(y0, b_w, za, ops, 10)
    sweep(za, b_w, y0, ops, 8)

    acc[...] = acc_in[...]
    zero = jnp.zeros((8, COLS), F32)
    last = TOP + ROWS - 1
    cy = [zero] * 16
    for l in span:
        code = mat_w[at(l, last), :] * 4.0 + mat_w[at(l, last + 1), :]
        edge = gy[at(l, last), :]
        for i in range(16):
            cy[i] = cy[i] + jnp.where(code == float(i), edge, 0.0)
    for i in range(16):
        keep(acc, G_CY + i, used(cy[i]))

    place_in = lane & (HALF - 1)

    def cross_step(y8, cx):
        side, side_code = zero, zero - 1.0
        for r in range(8):
            for l in span:
                here = at(l, TOP + 8 * y8 + r)
                p = r * LAYERS + l
                m = mat_w[here, :]
                code = m * 4.0 + turn(m, -1)
                target = place_in == COLS - 1 - LATE - p
                side = jnp.where(target, turn(gx[here, :], -p), side)
                side_code = jnp.where(target, turn(code, -p), side_code)
        return [cx[i] + jnp.where(side_code == float(i), side, 0.0) for i in range(16)]

    cx = lax.fori_loop(0, ROWS // 8, cross_step, [zero] * 16)
    valid = (sub >= SPECIES) & ((sub < 7) | left)
    for i in range(16):
        keep(acc, G_CX + i, jnp.where(valid, cx[i], 0.0))


def first_kernel(
    planes, got, cap_w, mat_w, gy, gx, gz, scale, y0, acc_in, b_w,
    second, z0, w0, u_out,
    za, zb, scatter, near_hot, turned, values, acc,
):
    ops = (cap_w, gy, gx, gz, scale)

    turned[...] = got[...].T
    build_scatter(got, scatter)
    build_near(got, near_hot)
    sol = coarse_solve(local_sums(turned, 0), turned, scatter)
    spread_values(exact_dot(sol, near_hot[...]), values)

    def add_coarse(l, y, c):
        z0[at(l, y), :] = y0[at(l, y), :] + c

    coarse_rows(values, mat_w, 8, add_coarse)
    image(z0, w0, ops, 8)
    start_sweep(w0, za, scale, 8)
    sweep(za, w0, zb, ops, 6)
    sweep(zb, w0, za, ops, 6)
    sweep(za, w0, u_out, ops, 4)

    acc[...] = acc_in[...]

    def emit(l, y, u, au, carry):
        rw, rau, mom = carry
        here = at(l, y)
        m = mat_w[here, :]
        wv, zv, bv = w0[here, :], z0[here, :], b_w[here, :]
        is_m = [m == float(i) for i in range(MATS)]
        rw = [rw[i] + jnp.where(is_m[i], wv, 0.0) for i in range(MATS)]
        rau = [rau[i] + jnp.where(is_m[i], au, 0.0) for i in range(MATS)]
        mom = [mom[0] + bv * zv, mom[1] + zv * wv, mom[2] + wv * u, mom[3] + u * au]
        return rw, rau, mom

    zero = jnp.zeros((8, COLS), F32)
    sums = stencil(u_out, ops, 0, emit, ([zero] * 4, [zero] * 4, [zero] * 4))
    for group, tiles in zip((G_RW, G_RAU, G_MOM), sums):
        for i, v in enumerate(tiles):
            keep(acc, group + i, used(v))

    even = lax.rem(subs((2 * TOTAL, COLS)), 2) == 0
    second[...] = jnp.where(even, place(acc[0:COLS, :]), place(acc[COLS : 2 * COLS, :]))


def next_y(x):
    y = lax.rem(lanes(x.shape), N_GY)
    return jnp.where(y == N_GY - 1, turn(x, N_GY - 1), turn(x, -1))


def prev_y(x):
    y = lax.rem(lanes(x.shape), N_GY)
    return jnp.where(y == 0, turn(x, -(N_GY - 1)), turn(x, 1))


def total_of(x):
    return jnp.sum(jnp.sum(x, axis=0, keepdims=True), axis=1, keepdims=True)


def second_kernel(
    planes, got, got2, cap, mat, gy, gx, gz, scale, z0, w0, u,
    out_x, out_r, out_z,
    v1, w1, za, zb, px, pr, pz, scatter, gather, near_hot, turned, turned2, values, values2,
):
    turned[...] = got[...].T
    turned2[0:COLS, :] = got2[pl.ds(0, TOTAL, stride=2), :].T
    turned2[COLS : 2 * COLS, :] = got2[pl.ds(1, TOTAL, stride=2), :].T
    build_scatter(got, scatter)
    build_gather(turned, gather)
    build_near(got, near_hot)

    sums_w = local_sums(turned2, G_RW)
    sol = coarse_solve(sums_w, turned, scatter)
    spread_values(exact_dot(sol, near_hot[...]), values)
    c_all = exact_dot(sol, gather[...])
    c = [c_all[:, m * TOTAL : (m + 1) * TOTAL] for m in range(MATS)]

    def rows5(group):
        return turned2[group * SPECIES : group * SPECIES + 8, :]

    live = subs((8, TOTAL)) < SPECIES
    bc = [turned2[ROW_CAP + m : ROW_CAP + m + 1, :] * c[m] for m in range(MATS)]
    n = 0
    for i in range(MATS):
        for j in range(i + 1, MATS):
            f = rows5(G_S + n) * (c[i] - c[j])
            bc[i] = bc[i] + f
            bc[j] = bc[j] - f
            n += 1
    c_y = [next_y(v) for v in c]
    c_x = [turn(v, -N_GY) for v in c]
    back_y = [jnp.zeros((8, TOTAL), F32)] * MATS
    back_x = [jnp.zeros((8, TOTAL), F32)] * MATS
    for i in range(MATS):
        for j in range(MATS):
            f = rows5(G_CY + 4 * i + j) * (c[i] - c_y[j])
            bc[i] = bc[i] + f
            back_y[j] = back_y[j] + f
            f = rows5(G_CX + 4 * i + j) * (c[i] - c_x[j])
            bc[i] = bc[i] + f
            back_x[j] = back_x[j] + f
    for j in range(MATS):
        bc[j] = jnp.where(live, bc[j] - prev_y(back_y[j]) - turn(back_x[j], N_GY), 0.0)
    bc_all = jnp.concatenate(bc, axis=1)
    sums_au = local_sums(turned2, G_RAU)
    sol2 = coarse_solve(sums_au + bc_all, turned, scatter)
    spread_values(exact_dot(sol2, near_hot[...]), values2)

    def moment(i):
        return total_of(jnp.where(live, rows5(G_MOM + i), 0.0))

    m0, m1 = moment(0), moment(1)
    m2 = moment(2) + total_of(sums_w * c_all)
    m3 = moment(3) + total_of((2.0 * sums_au + bc_all) * c_all)
    a0 = m0 / m1
    rz1 = m0 - 2.0 * a0 * m1 + a0 * a0 * m2
    g = 1.0 + rz1 / m0
    a1 = rz1 / (g * g * m1 - 2.0 * a0 * g * m2 + a0 * a0 * m3)
    ca = jnp.broadcast_to(a0 + a1 * g, (8, COLS))
    cb = jnp.broadcast_to(a1 * a0, (8, COLS))

    ops = (cap, gy, gx, gz, scale)

    def add_coarse(l, y, c):
        v1[at(l, y), :] = u[at(l, y), :] + c

    coarse_rows(values, mat, 4, add_coarse)
    image(v1, w1, ops, 4)
    start_sweep(w1, za, scale, 4)
    sweep(za, w1, zb, ops, 2)
    sweep(zb, w1, za, ops, 2)
    own_values = [values2[(MATS + m) * 8 : (MATS + m + 1) * 8, :] for m in range(MATS)]

    def emit(l, y, z, out, carry):
        here = at(l, y)
        w1v, v1v = w1[here, :], v1[here, :]
        z0v, w0v = z0[here, :], w0[here, :]
        v2 = z + scale[here, :] * (w1v - out) + coarse_pick(own_values, mat[here, :])
        px[here, :] = ca * z0v - cb * v1v
        pr[here, :] = ca * w0v - cb * w1v
        pz[here, :] = z0v - ca * v1v + cb * v2
        return carry

    stencil(za, ops, 0, emit)

    lane = lanes((8, COLS))

    def unpacked(src, l, row, s):
        start = (l * TALL + TOP + row) * 8
        early = src[pl.ds(start + s, 8, stride=8), :]
        late = src[pl.ds(start + SPECIES + s // 2, 8, stride=8), :]
        return jnp.where(
            lane < SEAM, turn(early, -HALO), turn(late, LATE - (s % 2) * HALF)
        )

    for s in range(SPECIES):
        for l in range(LAYERS):
            for row in range(0, ROWS, 8):
                k, rows = s * LAYERS + l, slice(row, row + 8)
                out_x[k, rows, :] = unpacked(px, l, row, s)
                out_r[k, rows, :] = planes[k, rows, :] - unpacked(pr, l, row, s)
                out_z[k, rows, :] = unpacked(pz, l, row, s)


def shape(*dims):
    return jax.ShapeDtypeStruct(dims, F32)


VMEM = pl.BlockSpec(memory_space=pltpu.VMEM)
SMEM = pl.BlockSpec(memory_space=pltpu.SMEM)
PARAMS = pltpu.CompilerParams(vmem_limit_bytes=20 * 1024 * 1024)


def run(kernel, outs, scratch, in_specs, cost, *args):
    return pl.pallas_call(
        kernel,
        out_shape=outs,
        in_specs=in_specs,
        out_specs=jax.tree.map(lambda _: VMEM, outs),
        scratch_shapes=scratch,
        compiler_params=PARAMS,
        cost_estimate=pl.CostEstimate(flops=cost, bytes_accessed=1 << 20, transcendentals=0),
    )(*args)


def shifts(axis, count):
    forward = [(i, (i + 1) % count) for i in range(count)]
    backward = [(target, source) for source, target in forward]
    return (functools.partial(lax.ppermute, axis_name=axis, perm=p) for p in (forward, backward))


def to_all(rows):
    got = lax.all_to_all(rows.reshape(TOTAL, -1, COLS), BOTH, 0, 0, tiled=True)
    return got.reshape(rows.shape)


def body(right_side, potential, capacity, diffusivity, material, coarse_map, coarse_inverse):
    b = right_side.reshape(FIELDS, ROWS, COLS)
    right, left = shifts("grp", N_GRP)
    down, up = shifts("gy", N_GY)

    planes = jnp.concatenate([b, potential, capacity, material.astype(F32)])
    packed = shape(GROUPS, ROWS, COLS)
    to_low, to_high = run(pack_kernel, (packed, packed), [], [VMEM], 1 << 20, planes)
    x_low, x_high = right(to_high), left(to_low)
    code = pltpu.VMEM((LAYERS, ROWS, COLS), F32)
    first, acc = run(
        own_kernel,
        (shape(TOTAL, COLS), shape(2 * COLS, COLS)),
        [pltpu.VMEM((FIELDS, ROWS, COLS), F32), code, code, code]
        + [pltpu.VMEM((24, COLS), F32), pltpu.VMEM((8, COLS), jnp.int32)],
        [SMEM] + [VMEM] * 3,
        1 << 20,
        diffusivity.T, planes, coarse_map, jnp.transpose(coarse_inverse, (1, 0, 2)),
    )

    strips = shape(PLANES + 2 * GROUPS, RHALO, COLS)
    to_low, to_high = run(
        rows_kernel, (strips, strips), [], [VMEM] * 3, 1 << 20, planes, x_low, x_high
    )
    first, to_low, to_high = lax.optimization_barrier((first, to_low, to_high))
    y_low, y_high = down(to_high), up(to_low)
    got, y_low, y_high = lax.optimization_barrier((to_all(first), y_low, y_high))

    packed = shape(LAYERS * TALL * 8, COLS)
    field = shape(FIELDS, ROWS, COLS)
    big = pltpu.VMEM(packed.shape, F32)
    hot = pltpu.VMEM((NC, MATS * TOTAL), jnp.bfloat16)
    near = pltpu.VMEM((NC, COLS), jnp.bfloat16)
    square = pltpu.VMEM((COLS, COLS), F32)
    double = pltpu.VMEM((2 * COLS, COLS), F32)
    values = pltpu.VMEM((3 * MATS * 8, COLS), F32)
    cap_w, mat_w, gy, gx, gz, scale, y0, acc, b_w = run(
        table_kernel,
        (packed,) * 7 + (shape(2 * COLS, COLS), packed),
        [big] * 2,
        [SMEM] + [VMEM] * 6,
        1 << 30,
        diffusivity.T, planes, x_low, x_high, y_low, y_high, acc,
    )
    second, z0, w0, u = run(
        first_kernel,
        (shape(2 * TOTAL, COLS), packed, packed, packed),
        [big] * 2 + [hot, near, square, values, double],
        [VMEM] * 11,
        1 << 30,
        planes, got, cap_w, mat_w, gy, gx, gz, scale, y0, acc, b_w,
    )
    got2 = to_all(second)
    out = run(
        second_kernel,
        (field, field, field),
        [big] * 7 + [hot, hot, near, square, double, values, values],
        [VMEM] * 12,
        1 << 30,
        planes, got, got2, cap_w, mat_w, gy, gx, gz, scale, z0, w0, u,
    )
    return tuple(o.reshape(right_side.shape) for o in out)


def solution(mesh):
    placed = (
        P(None, None, "gy", "grp"),
        P(None, "gy", "grp"),
        P(None, "gy", "grp"),
        P(),
        P(None, "gy", "grp"),
        P("gy", "grp", None),
        P(("grp", "gy"), None, None),
    )
    return jax.shard_map(
        body,
        mesh=mesh,
        in_specs=placed,
        out_specs=(P(None, None, "gy", "grp"),) * 3,
        check_vma=False,
    )
```

```python
import functools

import jax
import jax.numpy as jnp
from jax import lax
from jax.experimental import pallas as pl
from jax.experimental.pallas import tpu as pltpu
from jax.sharding import PartitionSpec as P

SPECIES = 5
LAYERS = 4
MATS = 4
FIELDS = SPECIES * LAYERS
PLANES = FIELDS + 3 * LAYERS
POT0, CAP0, MAT0 = FIELDS, FIELDS + LAYERS, FIELDS + 2 * LAYERS
ROWS = 32
COLS = 128
N_GRP = 4
N_GY = 32
TOTAL = N_GRP * N_GY
NC = 512
DAMPING = 2.0 / 3.0
BOTH = ("grp", "gy")

HALO = 12
GROUPS = LAYERS
RHALO = 16
TALL = ROWS + 2 * RHALO
TOP = RHALO
HALF = COLS // 2
LATE = COLS + HALO - HALF
SEAM = 96
F32 = jnp.float32

G_RW, G_RAU, G_S, G_CY, G_CX, G_MOM = 0, 4, 8, 14, 30, 46
ROW_CAP = 250
MAP_LANE = 20
INV_LANE = 24


def lanes(shape):
    return lax.broadcasted_iota(jnp.int32, shape, 1)


def subs(shape):
    return lax.broadcasted_iota(jnp.int32, shape, 0)


def pack_kernel(planes, to_low, to_high):
    lane = lanes((ROWS, COLS))
    for g in range(GROUPS):
        low = jnp.zeros((ROWS, COLS), F32)
        high = jnp.zeros((ROWS, COLS), F32)
        for j in range(PLANES // LAYERS):
            v = planes[j * LAYERS + g]
            inside = (lane >= HALO * j) & (lane < HALO * (j + 1))
            low = jnp.where(inside, turn(v, HALO * j), low)
            high = jnp.where(inside, turn(v, HALO * j + HALO), high)
        to_low[g] = low
        to_high[g] = high


def turn(v, shift):
    shift = shift % v.shape[1]
    return v if shift == 0 else pltpu.roll(v, shift, 1)


def place(rows):
    n = rows.shape[0]
    total = jnp.sum(rows, axis=1, keepdims=True)
    spread = jnp.where(lanes((n, COLS)) == subs((n, COLS)), total, 0.0)
    return jnp.sum(spread, axis=0, keepdims=True)


def fold(v):
    return jnp.sum(v, axis=0, keepdims=True)


def harmonic(a, b):
    return 2.0 * a * b / (a + b)


def after(v, nxt, axis):
    first = lax.broadcasted_iota(jnp.int32, v.shape, axis) == 0
    return pltpu.roll(jnp.where(first, nxt, v), v.shape[axis] - 1, axis)


def power(m):
    p = jnp.where(m == 1.0, 2.0, 1.0)
    p = jnp.where(m == 2.0, 4.0, p)
    return jnp.where(m == 3.0, 8.0, p)


def own_kernel(diff, planes, cmap, inverse, out, acc, w, code_y, code_x, code_z, part, ids):
    part[...] = jnp.zeros(part.shape, F32)
    row = jnp.zeros((1, COLS), F32)
    for s in range(SPECIES):
        part[0:4, 0:SPECIES] = inverse[s]
        for k in range(4):
            row = row + turn(part[k : k + 1, :], INV_LANE + (k * SPECIES + s) * SPECIES)
    part[0:4, :] = jnp.zeros((4, COLS), F32)
    ids[...] = jnp.zeros(ids.shape, jnp.int32)
    ids[0:1, 0:MATS] = cmap[0]
    q = ids[0:1, :]
    row = row + turn(((q & 3) * TOTAL + (q >> 2)).astype(F32), MAP_LANE)
    for s in range(SPECIES):
        for m in range(MATS):
            total = jnp.zeros((ROWS, COLS), F32)
            for l in range(LAYERS):
                total = total + jnp.where(planes[MAT0 + l] == m, planes[s * LAYERS + l], 0.0)
            part[m * SPECIES + s : m * SPECIES + s + 1, :] = fold(total)
    out[...] = jnp.broadcast_to(row + place(part[...]), (TOTAL, COLS))

    acc[...] = jnp.zeros(acc.shape, F32)
    lane, sub = lanes((8, COLS)), subs((8, COLS))
    tiles = [8 * t for t in range(ROWS // 8)]
    for r in tiles:
        here = pl.ds(r, 8)
        for l in range(LAYERS):
            m = planes[MAT0 + l, here, :]
            is1, is2, is3 = m == 1.0, m == 2.0, m == 3.0
            down = jnp.exp(-0.5 * planes[POT0 + l, here, :])
            up = jnp.exp(0.5 * planes[POT0 + l, here, :])
            drift = (down, up, down * down, up * up, down)
            for s in range(SPECIES):
                d = jnp.where(is1, diff[1, s], diff[0, s])
                d = jnp.where(is2, diff[2, s], d)
                d = jnp.where(is3, diff[3, s], d)
                w[s * LAYERS + l, here, :] = d * drift[s]
            p = power(m)
            if r == tiles[-1]:
                code = jnp.where(sub == 7, 0.0, p + power(after(m, m, 0)))
            else:
                code = p + power(after(m, planes[MAT0 + l, pl.ds(r + 8, 8), :], 0))
            code_y[l, here, :] = code
            code_x[l, here, :] = jnp.where(lane == COLS - 1, 0.0, p + power(turn(m, -1)))
            if l + 1 < LAYERS:
                code_z[l, here, :] = p + power(planes[MAT0 + l + 1, here, :])

    @pl.loop(0, SPECIES)
    def _(s):
        pairs = [jnp.zeros((8, COLS), F32)] * 6
        codes = (3.0, 5.0, 9.0, 6.0, 10.0, 12.0)
        for r in tiles:
            here = pl.ds(r, 8)
            for l in range(LAYERS):
                k = s * LAYERS + l
                c = w[k, here, :]
                nxt = c if r == tiles[-1] else w[k, pl.ds(r + 8, 8), :]
                kinds = [
                    (code_y[l, here, :], harmonic(c, after(c, nxt, 0))),
                    (code_x[l, here, :], harmonic(c, turn(c, -1))),
                ]
                if l + 1 < LAYERS:
                    kinds.append((code_z[l, here, :], 0.5 * harmonic(c, w[k + 1, here, :])))
                for code, edge in kinds:
                    for i in range(6):
                        pairs[i] = pairs[i] + jnp.where(code == codes[i], edge, 0.0)
        for i in range(6):
            acc[pl.ds((G_S + i) * SPECIES + s, 1), :] = fold(pairs[i])

    for i in range(MATS):
        total = jnp.zeros((ROWS, COLS), F32)
        for l in range(LAYERS):
            total = total + jnp.where(planes[MAT0 + l] == i, planes[CAP0 + l], 0.0)
        acc[ROW_CAP + i : ROW_CAP + i + 1, :] = fold(total)


def rows_kernel(planes, from_low, from_high, to_low, to_high):
    for k in range(PLANES):
        to_low[k] = planes[k, :RHALO]
        to_high[k] = planes[k, ROWS - RHALO :]
    for g in range(GROUPS):
        for i, part in enumerate((from_low, from_high)):
            k = PLANES + i * GROUPS + g
            to_low[k] = part[g, :RHALO]
            to_high[k] = part[g, ROWS - RHALO :]


def at(l, y):
    if isinstance(y, int):
        return pl.ds((y + l * TALL) * 8, 8)
    return pl.ds(pl.multiple_of((y + l * TALL) * 8, 8), 8)


class Later:
    def __init__(self):
        self.held = []

    def put(self, ref, where, value):
        self.held.append((ref, where, value))

    def flush(self):
        for ref, where, value in self.held:
            ref[where, :] = value
        self.held = []


LATER = Later()
BLOCK = 0


def each_row(first, count, step, carry=()):
    size = BLOCK if BLOCK and count % BLOCK == 0 else 4
    if BLOCK == 0:
        for r in range(count):
            carry = step(first + r, carry)
            LATER.flush()
        return carry

    def block(i, carry):
        for r in range(size):
            carry = step(first + size * i + r, carry)
        LATER.flush()
        return carry

    return lax.fori_loop(0, count // size, block, carry)


def stencil(src, ops, wide, emit, carry=()):
    cap, gy, gx, gz = ops[:4]
    first = TOP - wide
    span = range(LAYERS)
    now = [src[at(l, first), :] for l in span]
    flux = [gy[at(l, first - 1), :] * (src[at(l, first - 1), :] - now[l]) for l in span]

    def step(y, carry):
        now, flux, carry = carry
        nxt, out_flux = [], []
        flux_z = None
        for l in span:
            here = at(l, y)
            u = now[l]
            above = src[at(l, y + 1), :]
            flux_x = gx[here, :] * (u - turn(u, -1))
            flux_y = gy[here, :] * (u - above)
            out = cap[here, :] * u + (flux_x - turn(flux_x, 1)) + (flux_y - flux[l])
            if flux_z is not None:
                out = out - flux_z
            if l + 1 < LAYERS:
                flux_z = gz[here, :] * (u - now[l + 1])
                out = out + flux_z
            nxt.append(above)
            out_flux.append(flux_y)
            carry = emit(l, y, u, out, carry)
        return nxt, out_flux, carry

    return each_row(first, ROWS + 2 * wide, step, (now, flux, carry))[2]


def sweep(src, resid, dst, ops, wide):
    scale = ops[4]

    def emit(l, y, u, out, carry):
        here = at(l, y)
        LATER.put(dst, here, u + scale[here, :] * (resid[here, :] - out))
        return carry

    stencil(src, ops, wide, emit)


def image(src, dst, ops, wide):
    def emit(l, y, u, out, carry):
        LATER.put(dst, at(l, y), out)
        return carry

    stencil(src, ops, wide, emit)


def start_sweep(resid, dst, scale, wide):
    def step(y, carry):
        for l in range(LAYERS):
            here = at(l, y)
            LATER.put(dst, here, scale[here, :] * resid[here, :])
        return carry

    each_row(TOP - wide, ROWS + 2 * wide, step)


def used(tile):
    lane, sub = lanes(tile.shape), subs(tile.shape)
    early = (sub < SPECIES) & (lane >= HALO) & (lane < HALO + SEAM)
    place_in = lane & (HALF - 1)
    late = (sub >= SPECIES) & (place_in >= SEAM - LATE) & (place_in < COLS - LATE)
    late = late & ((sub < 7) | (lane < HALF))
    return jnp.where(early | late, tile, 0.0)


def by_species(tile):
    lane, sub = lanes(tile.shape), subs(tile.shape)
    left = lane < HALF
    out = tile
    out = out + jnp.where((sub == 0) & left, pltpu.roll(tile, 3, 0), 0.0)
    pick = ((sub == 1) & ~left) | ((sub == 2) & left)
    out = out + jnp.where(pick, pltpu.roll(tile, 4, 0), 0.0)
    pick = ((sub == 3) & ~left) | ((sub == 4) & left)
    out = out + jnp.where(pick, pltpu.roll(tile, 5, 0), 0.0)
    return out[:SPECIES]


def keep(acc, group, tile):
    acc[group * SPECIES : (group + 1) * SPECIES, :] = by_species(tile)


def split3(x):
    hi = x.astype(jnp.bfloat16)
    rest = x - hi.astype(F32)
    mid = rest.astype(jnp.bfloat16)
    lo = (rest - mid.astype(F32)).astype(jnp.bfloat16)
    return jnp.concatenate([hi, mid, lo], axis=0)


def exact_dot(x, onehot):
    n = x.shape[0]
    y = jnp.dot(
        jnp.concatenate([split3(x)], axis=0), onehot, preferred_element_type=F32
    )
    return y[:n] + y[n : 2 * n] + y[2 * n :]


def build_scatter(got, onehot):
    for m in range(MATS):
        col = jnp.broadcast_to(got[:, MAP_LANE + m : MAP_LANE + m + 1], (TOTAL, COLS))
        for k in range(4):
            target = (lanes((TOTAL, COLS)) + k * COLS).astype(F32)
            onehot[m * TOTAL : (m + 1) * TOTAL, k * COLS : (k + 1) * COLS] = jnp.where(
                col == target, 1.0, 0.0
            ).astype(jnp.bfloat16)


def build_gather(turned, onehot):
    for m in range(MATS):
        row = jnp.broadcast_to(turned[MAP_LANE + m : MAP_LANE + m + 1, :], (COLS, TOTAL))
        for k in range(4):
            target = (subs((COLS, TOTAL)) + k * COLS).astype(F32)
            onehot[k * COLS : (k + 1) * COLS, m * TOTAL : (m + 1) * TOTAL] = jnp.where(
                row == target, 1.0, 0.0
            ).astype(jnp.bfloat16)


def build_near(got, onehot):
    gx, gy = lax.axis_index("grp"), lax.axis_index("gy")
    lane = lanes((1, COLS))
    row = jnp.full((1, COLS), -1.0, F32)
    for iy in range(3):
        y = lax.rem(gy + (N_GY - 1 + iy), N_GY)
        for ix in range(3):
            x = jnp.clip(gx + (ix - 1), 0, N_GRP - 1)
            region = iy * 3 + ix
            here = got[pl.ds(x * N_GY + y, 1), :]
            inside = (lane >= region * MATS) & (lane < (region + 1) * MATS)
            row = jnp.where(inside, turn(here, region * MATS - MAP_LANE), row)
    for k in range(4):
        target = (subs((COLS, COLS)) + k * COLS).astype(F32)
        onehot[k * COLS : (k + 1) * COLS, :] = jnp.where(
            jnp.broadcast_to(row, (COLS, COLS)) == target, 1.0, 0.0
        ).astype(jnp.bfloat16)


def coarse_solve(sums, turned, scatter):
    res = exact_dot(sums, scatter[...])
    parts = []
    for k in range(4):
        total = None
        for t in range(SPECIES):
            start = INV_LANE + k * SPECIES * SPECIES + t * SPECIES
            term = turned[start : start + 8, :] * res[t : t + 1, k * COLS : (k + 1) * COLS]
            total = term if total is None else total + term
        parts.append(total)
    sol = jnp.concatenate(parts, axis=1)
    return jnp.where(subs(sol.shape) < SPECIES, sol, 0.0)


def local_sums(turned, group):
    x = jnp.concatenate(
        [turned[(group + m) * SPECIES : (group + m) * SPECIES + 8, :] for m in range(MATS)], axis=1
    )
    return jnp.where(subs(x.shape) < SPECIES, x, 0.0)


def spread_values(near, values):
    lane, sub = lanes((8, COLS)), subs((8, COLS))

    def arrange(a, b, c):
        row = lambda s: jnp.broadcast_to(near[s : s + 1, :], (8, COLS))
        out = jnp.where(sub == 5, row(a), near)
        return jnp.where(sub == 7, row(c), jnp.where(sub == 6, row(b), out))

    left, right = arrange(0, 2, 4), arrange(1, 3, 4)
    early = sub < SPECIES
    for iy in range(3):
        for m in range(MATS):
            column = lambda v, ix: jnp.broadcast_to(
                v[:, (iy * 3 + ix) * MATS + m : (iy * 3 + ix) * MATS + m + 1], (8, COLS)
            )
            first = jnp.where(early & (lane < HALO), column(left, 0), column(left, 1))
            first = jnp.where(~early & (lane >= COLS - LATE), column(left, 2), first)
            second = jnp.where(lane >= HALF + COLS - LATE, column(right, 2), column(right, 1))
            values[(iy * MATS + m) * 8 : (iy * MATS + m + 1) * 8, :] = jnp.where(
                early | (lane < HALF), first, second
            )


def coarse_rows(values, mat, wide, emit):
    for iy, first, count in ((0, TOP - wide, wide), (1, TOP, ROWS), (2, TOP + ROWS, wide)):
        if count == 0:
            continue
        v = [values[(iy * MATS + m) * 8 : (iy * MATS + m + 1) * 8, :] for m in range(MATS)]

        def step(y, carry):
            for l in range(LAYERS):
                emit(l, y, coarse_pick(v, mat[at(l, y), :]))
            return carry

        each_row(first, count, step)


def coarse_pick(v, m):
    out = jnp.where(m == 1.0, v[1], v[0])
    out = jnp.where(m == 2.0, v[2], out)
    return jnp.where(m == 3.0, v[3], out)


def table_kernel(
    diff, planes, x_low, x_high, y_low, y_high, acc_in,
    cap_w, mat_w, gy, gx, gz, scale, y0, acc, b_w,
    w, za,
):
    lane, sub = lanes((8, COLS)), subs((8, COLS))
    left = lane < HALF

    pairs = ((0, 1), (2, 3), (4, 4))
    d_late = [
        [jnp.where(left, diff[m, a], diff[m, b]) for m in range(MATS)] for a, b in pairs
    ]

    def choose(v, is1, is2, is3):
        return jnp.where(is3, v[3], jnp.where(is2, v[2], jnp.where(is1, v[1], v[0])))

    def fill(own, low, high, l, row, y):
        rows = pl.ds(row, 8)

        def both(kind):
            v = own[kind * LAYERS + l, rows, :]
            early = jnp.where(lane < HALO, turn(low[l, rows, :], -HALO * kind), turn(v, HALO))
            beyond = turn(high[l, rows, :], COLS - LATE - HALO * kind)
            return early, jnp.where(lane < COLS - LATE, turn(v, -LATE), beyond)

        def put(dst, s, v):
            dst[pl.ds((y + l * TALL) * 8 + s, 8, stride=8), :] = v

        late_b = []
        for s in range(SPECIES):
            early, late = both(s)
            put(b_w, s, early)
            late_b.append(late)
        for i, (a, b) in enumerate(pairs):
            put(b_w, SPECIES + i, jnp.where(left, late_b[a], turn(late_b[b], HALF)))
        for dst, kind in ((cap_w, SPECIES + 1), (mat_w, SPECIES + 2)):
            early, late = both(kind)
            late = jnp.where(left, late, turn(late, HALF))
            for s in range(8):
                put(dst, s, early if s < SPECIES else late)
        m_early, m_late = early, late
        early, late = both(SPECIES)
        late = jnp.where(left, late, turn(late, HALF))
        is_m = [m_early == float(m) for m in (1, 2, 3)]
        down, up = jnp.exp(-0.5 * early), jnp.exp(0.5 * early)
        drift = (down, up, down * down, up * up, down)
        for s in range(SPECIES):
            put(w, s, choose([diff[m, s] for m in range(MATS)], *is_m) * drift[s])
        is_m = [m_late == float(m) for m in (1, 2, 3)]
        down, up = jnp.exp(-0.5 * late), jnp.exp(0.5 * late)
        mixed = jnp.where(left, down, up)
        drift = (mixed, mixed * mixed, down)
        for i in range(3):
            put(w, SPECIES + i, choose(d_late[i], *is_m) * drift[i])

    edge_low = (y_low.at[PLANES : PLANES + GROUPS], y_low.at[PLANES + GROUPS : PLANES + 2 * GROUPS])
    edge_high = (y_high.at[PLANES : PLANES + GROUPS], y_high.at[PLANES + GROUPS : PLANES + 2 * GROUPS])

    @pl.loop(0, LAYERS)
    def _(l):
        for row in range(0, RHALO, 8):
            fill(y_low, *edge_low, l, row, row)

    @pl.loop(0, LAYERS)
    def _(l):
        for row in range(0, ROWS, 8):
            fill(planes, x_low, x_high, l, row, TOP + row)

    @pl.loop(0, LAYERS)
    def _(l):
        for row in range(0, RHALO, 8):
            fill(y_high, *edge_high, l, row, TOP + ROWS + row)

    me_x = lax.axis_index("grp")
    closed = ((sub >= SPECIES) & ((lane & (HALF - 1)) == COLS - 1 - LATE) & (me_x == N_GRP - 1)) | (
        (sub < SPECIES) & (lane == HALO - 1) & (me_x == 0)
    )
    span = range(LAYERS)
    first = TOP - 12

    def edge_step(y, carry):
        now, edge_y = carry
        nxt, out_y = [], []
        ez_below = None
        for l in span:
            here = at(l, y)
            c = now[l]
            above = w[at(l, y + 1), :]
            ey = harmonic(c, above)
            ex = jnp.where(closed, 0.0, harmonic(c, turn(c, -1)))
            LATER.put(gy, here, ey)
            LATER.put(gx, here, ex)
            d = cap_w[here, :] + ey + edge_y[l] + ex + turn(ex, 1)
            if ez_below is not None:
                d = d + ez_below
            if l + 1 < LAYERS:
                ez_below = 0.5 * harmonic(c, now[l + 1])
                LATER.put(gz, here, ez_below)
                d = d + ez_below
            LATER.put(scale, here, DAMPING / d)
            nxt.append(above)
            out_y.append(ey)
        return nxt, out_y

    now = [w[at(l, first), :] for l in span]
    edge_y = [harmonic(w[at(l, first - 1), :], now[l]) for l in span]
    each_row(first, ROWS + 24, edge_step, (now, edge_y))

    ops = (cap_w, gy, gx, gz, scale)
    start_sweep(b_w, za, scale, 12)
    sweep(za, b_w, y0, ops, 10)
    sweep(y0, b_w, za, ops, 10)
    sweep(za, b_w, y0, ops, 8)

    acc[...] = acc_in[...]
    zero = jnp.zeros((8, COLS), F32)
    last = TOP + ROWS - 1
    cy = [zero] * 16
    for l in span:
        code = mat_w[at(l, last), :] * 4.0 + mat_w[at(l, last + 1), :]
        edge = gy[at(l, last), :]
        for i in range(16):
            cy[i] = cy[i] + jnp.where(code == float(i), edge, 0.0)
    for i in range(16):
        keep(acc, G_CY + i, used(cy[i]))

    place_in = lane & (HALF - 1)

    def cross_step(y8, cx):
        side, side_code = zero, zero - 1.0
        for r in range(8):
            for l in span:
                here = at(l, TOP + 8 * y8 + r)
                p = r * LAYERS + l
                m = mat_w[here, :]
                code = m * 4.0 + turn(m, -1)
                target = place_in == COLS - 1 - LATE - p
                side = jnp.where(target, turn(gx[here, :], -p), side)
                side_code = jnp.where(target, turn(code, -p), side_code)
        return [cx[i] + jnp.where(side_code == float(i), side, 0.0) for i in range(16)]

    cx = lax.fori_loop(0, ROWS // 8, cross_step, [zero] * 16)
    valid = (sub >= SPECIES) & ((sub < 7) | left)
    for i in range(16):
        keep(acc, G_CX + i, jnp.where(valid, cx[i], 0.0))


def first_kernel(
    planes, got, cap_w, mat_w, gy, gx, gz, scale, y0, acc_in, b_w,
    second, z0, w0, u_out,
    za, zb, scatter, near_hot, turned, values, acc,
):
    ops = (cap_w, gy, gx, gz, scale)

    turned[...] = got[...].T
    build_scatter(got, scatter)
    build_near(got, near_hot)
    sol = coarse_solve(local_sums(turned, 0), turned, scatter)
    spread_values(exact_dot(sol, near_hot[...]), values)

    def add_coarse(l, y, c):
        LATER.put(z0, at(l, y), y0[at(l, y), :] + c)

    coarse_rows(values, mat_w, 8, add_coarse)
    image(z0, w0, ops, 8)
    start_sweep(w0, za, scale, 8)
    sweep(za, w0, zb, ops, 6)
    sweep(zb, w0, za, ops, 6)
    sweep(za, w0, u_out, ops, 4)

    acc[...] = acc_in[...]

    def emit(l, y, u, au, carry):
        rw, rau, mom = carry
        here = at(l, y)
        m = mat_w[here, :]
        wv, zv, bv = w0[here, :], z0[here, :], b_w[here, :]
        is_m = [m == float(i) for i in range(MATS)]
        rw = [rw[i] + jnp.where(is_m[i], wv, 0.0) for i in range(MATS)]
        rau = [rau[i] + jnp.where(is_m[i], au, 0.0) for i in range(MATS)]
        mom = [mom[0] + bv * zv, mom[1] + zv * wv, mom[2] + wv * u, mom[3] + u * au]
        return rw, rau, mom

    zero = jnp.zeros((8, COLS), F32)
    sums = stencil(u_out, ops, 0, emit, ([zero] * 4, [zero] * 4, [zero] * 4))
    for group, tiles in zip((G_RW, G_RAU, G_MOM), sums):
        for i, v in enumerate(tiles):
            keep(acc, group + i, used(v))

    even = lax.rem(subs((2 * TOTAL, COLS)), 2) == 0
    second[...] = jnp.where(even, place(acc[0:COLS, :]), place(acc[COLS : 2 * COLS, :]))


def next_y(x):
    y = lax.rem(lanes(x.shape), N_GY)
    return jnp.where(y == N_GY - 1, turn(x, N_GY - 1), turn(x, -1))


def prev_y(x):
    y = lax.rem(lanes(x.shape), N_GY)
    return jnp.where(y == 0, turn(x, -(N_GY - 1)), turn(x, 1))


def total_of(x):
    return jnp.sum(jnp.sum(x, axis=0, keepdims=True), axis=1, keepdims=True)


def second_kernel(
    planes, got, got2, cap, mat, gy, gx, gz, scale, z0, w0, u,
    out_x, out_r, out_z,
    v1, w1, za, zb, px, pr, pz, scatter, gather, near_hot, turned, turned2, values, values2,
):
    turned[...] = got[...].T
    turned2[0:COLS, :] = got2[pl.ds(0, TOTAL, stride=2), :].T
    turned2[COLS : 2 * COLS, :] = got2[pl.ds(1, TOTAL, stride=2), :].T
    build_scatter(got, scatter)
    build_gather(turned, gather)
    build_near(got, near_hot)

    sums_w = local_sums(turned2, G_RW)
    sol = coarse_solve(sums_w, turned, scatter)
    spread_values(exact_dot(sol, near_hot[...]), values)
    c_all = exact_dot(sol, gather[...])
    c = [c_all[:, m * TOTAL : (m + 1) * TOTAL] for m in range(MATS)]

    def rows5(group):
        return turned2[group * SPECIES : group * SPECIES + 8, :]

    live = subs((8, TOTAL)) < SPECIES
    bc = [turned2[ROW_CAP + m : ROW_CAP + m + 1, :] * c[m] for m in range(MATS)]
    n = 0
    for i in range(MATS):
        for j in range(i + 1, MATS):
            f = rows5(G_S + n) * (c[i] - c[j])
            bc[i] = bc[i] + f
            bc[j] = bc[j] - f
            n += 1
    c_y = [next_y(v) for v in c]
    c_x = [turn(v, -N_GY) for v in c]
    back_y = [jnp.zeros((8, TOTAL), F32)] * MATS
    back_x = [jnp.zeros((8, TOTAL), F32)] * MATS
    for i in range(MATS):
        for j in range(MATS):
            f = rows5(G_CY + 4 * i + j) * (c[i] - c_y[j])
            bc[i] = bc[i] + f
            back_y[j] = back_y[j] + f
            f = rows5(G_CX + 4 * i + j) * (c[i] - c_x[j])
            bc[i] = bc[i] + f
            back_x[j] = back_x[j] + f
    for j in range(MATS):
        bc[j] = jnp.where(live, bc[j] - prev_y(back_y[j]) - turn(back_x[j], N_GY), 0.0)
    bc_all = jnp.concatenate(bc, axis=1)
    sums_au = local_sums(turned2, G_RAU)
    sol2 = coarse_solve(sums_au + bc_all, turned, scatter)
    spread_values(exact_dot(sol2, near_hot[...]), values2)

    def moment(i):
        return total_of(jnp.where(live, rows5(G_MOM + i), 0.0))

    m0, m1 = moment(0), moment(1)
    m2 = moment(2) + total_of(sums_w * c_all)
    m3 = moment(3) + total_of((2.0 * sums_au + bc_all) * c_all)
    a0 = m0 / m1
    rz1 = m0 - 2.0 * a0 * m1 + a0 * a0 * m2
    g = 1.0 + rz1 / m0
    a1 = rz1 / (g * g * m1 - 2.0 * a0 * g * m2 + a0 * a0 * m3)
    ca = jnp.broadcast_to(a0 + a1 * g, (8, COLS))
    cb = jnp.broadcast_to(a1 * a0, (8, COLS))

    ops = (cap, gy, gx, gz, scale)

    def add_coarse(l, y, c):
        LATER.put(v1, at(l, y), u[at(l, y), :] + c)

    coarse_rows(values, mat, 4, add_coarse)
    image(v1, w1, ops, 4)
    start_sweep(w1, za, scale, 4)
    sweep(za, w1, zb, ops, 2)
    sweep(zb, w1, za, ops, 2)
    own_values = [values2[(MATS + m) * 8 : (MATS + m + 1) * 8, :] for m in range(MATS)]

    def emit(l, y, z, out, carry):
        here = at(l, y)
        w1v, v1v = w1[here, :], v1[here, :]
        z0v, w0v = z0[here, :], w0[here, :]
        v2 = z + scale[here, :] * (w1v - out) + coarse_pick(own_values, mat[here, :])
        LATER.put(px, here, ca * z0v - cb * v1v)
        LATER.put(pr, here, ca * w0v - cb * w1v)
        LATER.put(pz, here, z0v - ca * v1v + cb * v2)
        return carry

    stencil(za, ops, 0, emit)

    lane = lanes((8, COLS))

    def unpacked(src, l, row, s):
        start = (l * TALL + TOP + row) * 8
        early = src[pl.ds(start + s, 8, stride=8), :]
        late = src[pl.ds(start + SPECIES + s // 2, 8, stride=8), :]
        return jnp.where(
            lane < SEAM, turn(early, -HALO), turn(late, LATE - (s % 2) * HALF)
        )

    for s in range(SPECIES):
        for l in range(LAYERS):
            for row in range(0, ROWS, 8):
                k, rows = s * LAYERS + l, slice(row, row + 8)
                out_x[k, rows, :] = unpacked(px, l, row, s)
                out_r[k, rows, :] = planes[k, rows, :] - unpacked(pr, l, row, s)
                out_z[k, rows, :] = unpacked(pz, l, row, s)


def shape(*dims):
    return jax.ShapeDtypeStruct(dims, F32)


VMEM = pl.BlockSpec(memory_space=pltpu.VMEM)
SMEM = pl.BlockSpec(memory_space=pltpu.SMEM)
PARAMS = pltpu.CompilerParams(vmem_limit_bytes=20 * 1024 * 1024)


def run(kernel, outs, scratch, in_specs, cost, *args):
    return pl.pallas_call(
        kernel,
        out_shape=outs,
        in_specs=in_specs,
        out_specs=jax.tree.map(lambda _: VMEM, outs),
        scratch_shapes=scratch,
        compiler_params=PARAMS,
        cost_estimate=pl.CostEstimate(flops=cost, bytes_accessed=1 << 20, transcendentals=0),
    )(*args)


def shifts(axis, count):
    forward = [(i, (i + 1) % count) for i in range(count)]
    backward = [(target, source) for source, target in forward]
    return (functools.partial(lax.ppermute, axis_name=axis, perm=p) for p in (forward, backward))


def to_all(rows):
    got = lax.all_to_all(rows.reshape(TOTAL, -1, COLS), BOTH, 0, 0, tiled=True)
    return got.reshape(rows.shape)


def body(right_side, potential, capacity, diffusivity, material, coarse_map, coarse_inverse):
    b = right_side.reshape(FIELDS, ROWS, COLS)
    right, left = shifts("grp", N_GRP)
    down, up = shifts("gy", N_GY)

    planes = jnp.concatenate([b, potential, capacity, material.astype(F32)])
    packed = shape(GROUPS, ROWS, COLS)
    to_low, to_high = run(pack_kernel, (packed, packed), [], [VMEM], 1 << 20, planes)
    x_low, x_high = right(to_high), left(to_low)
    code = pltpu.VMEM((LAYERS, ROWS, COLS), F32)
    first, acc = run(
        own_kernel,
        (shape(TOTAL, COLS), shape(2 * COLS, COLS)),
        [pltpu.VMEM((FIELDS, ROWS, COLS), F32), code, code, code]
        + [pltpu.VMEM((24, COLS), F32), pltpu.VMEM((8, COLS), jnp.int32)],
        [SMEM] + [VMEM] * 3,
        1 << 20,
        diffusivity.T, planes, coarse_map, jnp.transpose(coarse_inverse, (1, 0, 2)),
    )

    strips = shape(PLANES + 2 * GROUPS, RHALO, COLS)
    to_low, to_high = run(
        rows_kernel, (strips, strips), [], [VMEM] * 3, 1 << 20, planes, x_low, x_high
    )
    first, to_low, to_high = lax.optimization_barrier((first, to_low, to_high))
    y_low, y_high = down(to_high), up(to_low)
    got, y_low, y_high = lax.optimization_barrier((to_all(first), y_low, y_high))

    packed = shape(LAYERS * TALL * 8, COLS)
    field = shape(FIELDS, ROWS, COLS)
    big = pltpu.VMEM(packed.shape, F32)
    hot = pltpu.VMEM((NC, MATS * TOTAL), jnp.bfloat16)
    near = pltpu.VMEM((NC, COLS), jnp.bfloat16)
    square = pltpu.VMEM((COLS, COLS), F32)
    double = pltpu.VMEM((2 * COLS, COLS), F32)
    values = pltpu.VMEM((3 * MATS * 8, COLS), F32)
    cap_w, mat_w, gy, gx, gz, scale, y0, acc, b_w = run(
        table_kernel,
        (packed,) * 7 + (shape(2 * COLS, COLS), packed),
        [big] * 2,
        [SMEM] + [VMEM] * 6,
        1 << 30,
        diffusivity.T, planes, x_low, x_high, y_low, y_high, acc,
    )
    second, z0, w0, u = run(
        first_kernel,
        (shape(2 * TOTAL, COLS), packed, packed, packed),
        [big] * 2 + [hot, near, square, values, double],
        [VMEM] * 11,
        1 << 30,
        planes, got, cap_w, mat_w, gy, gx, gz, scale, y0, acc, b_w,
    )
    got2 = to_all(second)
    out = run(
        second_kernel,
        (field, field, field),
        [big] * 7 + [hot, hot, near, square, double, values, values],
        [VMEM] * 12,
        1 << 30,
        planes, got, got2, cap_w, mat_w, gy, gx, gz, scale, z0, w0, u,
    )
    return tuple(o.reshape(right_side.shape) for o in out)


def solution(mesh):
    placed = (
        P(None, None, "gy", "grp"),
        P(None, "gy", "grp"),
        P(None, "gy", "grp"),
        P(),
        P(None, "gy", "grp"),
        P("gy", "grp", None),
        P(("grp", "gy"), None, None),
    )
    return jax.shard_map(
        body,
        mesh=mesh,
        in_specs=placed,
        out_specs=(P(None, None, "gy", "grp"),) * 3,
        check_vma=False,
    )
```

```python
import functools

import jax
import jax.numpy as jnp
from jax import lax
from jax.experimental import pallas as pl
from jax.experimental.pallas import tpu as pltpu
from jax.sharding import PartitionSpec as P

SPECIES = 5
LAYERS = 4
MATS = 4
FIELDS = SPECIES * LAYERS
PLANES = FIELDS + 3 * LAYERS
POT0, CAP0, MAT0 = FIELDS, FIELDS + LAYERS, FIELDS + 2 * LAYERS
ROWS = 32
COLS = 128
N_GRP = 4
N_GY = 32
TOTAL = N_GRP * N_GY
NC = 512
DAMPING = 2.0 / 3.0
BOTH = ("grp", "gy")

HALO = 12
GROUPS = LAYERS
RHALO = 16
TALL = ROWS + 2 * RHALO
TOP = RHALO
HALF = COLS // 2
LATE = COLS + HALO - HALF
SEAM = 96
F32 = jnp.float32

G_RW, G_RAU, G_S, G_CY, G_CX, G_MOM = 0, 4, 8, 14, 30, 46
ROW_CAP = 250
MAP_LANE = 20
INV_LANE = 24


def lanes(shape):
    return lax.broadcasted_iota(jnp.int32, shape, 1)


def subs(shape):
    return lax.broadcasted_iota(jnp.int32, shape, 0)


def pack_kernel(fields, mat, planes, to_low, to_high):
    planes[0:MAT0] = fields[...]
    planes[MAT0:PLANES] = mat[...].astype(F32)
    lane = lanes((ROWS, COLS))
    for g in range(GROUPS):
        low = jnp.zeros((ROWS, COLS), F32)
        high = jnp.zeros((ROWS, COLS), F32)
        for j in range(PLANES // LAYERS):
            v = planes[j * LAYERS + g]
            inside = (lane >= HALO * j) & (lane < HALO * (j + 1))
            low = jnp.where(inside, turn(v, HALO * j), low)
            high = jnp.where(inside, turn(v, HALO * j + HALO), high)
        to_low[g] = low
        to_high[g] = high


def turn(v, shift):
    shift = shift % v.shape[1]
    return v if shift == 0 else pltpu.roll(v, shift, 1)


def place(rows):
    n = rows.shape[0]
    total = jnp.sum(rows, axis=1, keepdims=True)
    spread = jnp.where(lanes((n, COLS)) == subs((n, COLS)), total, 0.0)
    return jnp.sum(spread, axis=0, keepdims=True)


def fold(v):
    return jnp.sum(v, axis=0, keepdims=True)


def harmonic(a, b):
    return 2.0 * a * b / (a + b)


def after(v, nxt, axis):
    first = lax.broadcasted_iota(jnp.int32, v.shape, axis) == 0
    return pltpu.roll(jnp.where(first, nxt, v), v.shape[axis] - 1, axis)


def power(m):
    p = jnp.where(m == 1.0, 2.0, 1.0)
    p = jnp.where(m == 2.0, 4.0, p)
    return jnp.where(m == 3.0, 8.0, p)


def own_kernel(diff, planes, cmap, inverse, out, acc, w, code_y, code_x, code_z, part, ids):
    part[...] = jnp.zeros(part.shape, F32)
    row = jnp.zeros((1, COLS), F32)
    for s in range(SPECIES):
        part[0:4, 0:SPECIES] = inverse[s]
        for k in range(4):
            row = row + turn(part[k : k + 1, :], INV_LANE + (k * SPECIES + s) * SPECIES)
    part[0:4, :] = jnp.zeros((4, COLS), F32)
    ids[...] = jnp.zeros(ids.shape, jnp.int32)
    ids[0:1, 0:MATS] = cmap[0]
    q = ids[0:1, :]
    row = row + turn(((q & 3) * TOTAL + (q >> 2)).astype(F32), MAP_LANE)
    for s in range(SPECIES):
        for m in range(MATS):
            total = jnp.zeros((ROWS, COLS), F32)
            for l in range(LAYERS):
                total = total + jnp.where(planes[MAT0 + l] == m, planes[s * LAYERS + l], 0.0)
            part[m * SPECIES + s : m * SPECIES + s + 1, :] = fold(total)
    out[...] = jnp.broadcast_to(row + place(part[...]), (TOTAL, COLS))

    acc[...] = jnp.zeros(acc.shape, F32)
    lane, sub = lanes((8, COLS)), subs((8, COLS))
    tiles = [8 * t for t in range(ROWS // 8)]
    for r in tiles:
        here = pl.ds(r, 8)
        for l in range(LAYERS):
            m = planes[MAT0 + l, here, :]
            is1, is2, is3 = m == 1.0, m == 2.0, m == 3.0
            down = jnp.exp(-0.5 * planes[POT0 + l, here, :])
            up = jnp.exp(0.5 * planes[POT0 + l, here, :])
            drift = (down, up, down * down, up * up, down)
            for s in range(SPECIES):
                d = jnp.where(is1, diff[1, s], diff[0, s])
                d = jnp.where(is2, diff[2, s], d)
                d = jnp.where(is3, diff[3, s], d)
                w[s * LAYERS + l, here, :] = d * drift[s]
            p = power(m)
            if r == tiles[-1]:
                code = jnp.where(sub == 7, 0.0, p + power(after(m, m, 0)))
            else:
                code = p + power(after(m, planes[MAT0 + l, pl.ds(r + 8, 8), :], 0))
            code_y[l, here, :] = code
            code_x[l, here, :] = jnp.where(lane == COLS - 1, 0.0, p + power(turn(m, -1)))
            if l + 1 < LAYERS:
                code_z[l, here, :] = p + power(planes[MAT0 + l + 1, here, :])

    @pl.loop(0, SPECIES)
    def _(s):
        pairs = [jnp.zeros((8, COLS), F32)] * 6
        codes = (3.0, 5.0, 9.0, 6.0, 10.0, 12.0)
        for r in tiles:
            here = pl.ds(r, 8)
            for l in range(LAYERS):
                k = s * LAYERS + l
                c = w[k, here, :]
                nxt = c if r == tiles[-1] else w[k, pl.ds(r + 8, 8), :]
                kinds = [
                    (code_y[l, here, :], harmonic(c, after(c, nxt, 0))),
                    (code_x[l, here, :], harmonic(c, turn(c, -1))),
                ]
                if l + 1 < LAYERS:
                    kinds.append((code_z[l, here, :], 0.5 * harmonic(c, w[k + 1, here, :])))
                for code, edge in kinds:
                    for i in range(6):
                        pairs[i] = pairs[i] + jnp.where(code == codes[i], edge, 0.0)
        for i in range(6):
            acc[pl.ds((G_S + i) * SPECIES + s, 1), :] = fold(pairs[i])

    for i in range(MATS):
        total = jnp.zeros((ROWS, COLS), F32)
        for l in range(LAYERS):
            total = total + jnp.where(planes[MAT0 + l] == i, planes[CAP0 + l], 0.0)
        acc[ROW_CAP + i : ROW_CAP + i + 1, :] = fold(total)


def rows_kernel(planes, from_low, from_high, to_low, to_high):
    for k in range(PLANES):
        to_low[k] = planes[k, :RHALO]
        to_high[k] = planes[k, ROWS - RHALO :]
    for g in range(GROUPS):
        for i, part in enumerate((from_low, from_high)):
            k = PLANES + i * GROUPS + g
            to_low[k] = part[g, :RHALO]
            to_high[k] = part[g, ROWS - RHALO :]


def at(l, y):
    if isinstance(y, int):
        return pl.ds((y + l * TALL) * 8, 8)
    return pl.ds(pl.multiple_of((y + l * TALL) * 8, 8), 8)


class Later:
    def __init__(self):
        self.held = []

    def put(self, ref, where, value):
        self.held.append((ref, where, value))

    def flush(self):
        for ref, where, value in self.held:
            ref[where, :] = value
        self.held = []


LATER = Later()
BLOCK = 0


def each_row(first, count, step, carry=()):
    size = BLOCK if BLOCK and count % BLOCK == 0 else 4
    if BLOCK == 0:
        for r in range(count):
            carry = step(first + r, carry)
            LATER.flush()
        return carry

    def block(i, carry):
        for r in range(size):
            carry = step(first + size * i + r, carry)
        LATER.flush()
        return carry

    return lax.fori_loop(0, count // size, block, carry)


def stencil(src, ops, wide, emit, carry=()):
    cap, gy, gx, gz = ops[:4]
    first = TOP - wide
    span = range(LAYERS)
    now = [src[at(l, first), :] for l in span]
    flux = [gy[at(l, first - 1), :] * (src[at(l, first - 1), :] - now[l]) for l in span]

    def step(y, carry):
        now, flux, carry = carry
        nxt, out_flux = [], []
        flux_z = None
        for l in span:
            here = at(l, y)
            u = now[l]
            above = src[at(l, y + 1), :]
            flux_x = gx[here, :] * (u - turn(u, -1))
            flux_y = gy[here, :] * (u - above)
            out = cap[here, :] * u + (flux_x - turn(flux_x, 1)) + (flux_y - flux[l])
            if flux_z is not None:
                out = out - flux_z
            if l + 1 < LAYERS:
                flux_z = gz[here, :] * (u - now[l + 1])
                out = out + flux_z
            nxt.append(above)
            out_flux.append(flux_y)
            carry = emit(l, y, u, out, carry)
        return nxt, out_flux, carry

    return each_row(first, ROWS + 2 * wide, step, (now, flux, carry))[2]


def sweep(src, resid, dst, ops, wide):
    scale = ops[4]

    def emit(l, y, u, out, carry):
        here = at(l, y)
        LATER.put(dst, here, u + scale[here, :] * (resid[here, :] - out))
        return carry

    stencil(src, ops, wide, emit)


def image(src, dst, ops, wide):
    def emit(l, y, u, out, carry):
        LATER.put(dst, at(l, y), out)
        return carry

    stencil(src, ops, wide, emit)


def start_sweep(resid, dst, scale, wide):
    def step(y, carry):
        for l in range(LAYERS):
            here = at(l, y)
            LATER.put(dst, here, scale[here, :] * resid[here, :])
        return carry

    each_row(TOP - wide, ROWS + 2 * wide, step)


def used(tile):
    lane, sub = lanes(tile.shape), subs(tile.shape)
    early = (sub < SPECIES) & (lane >= HALO) & (lane < HALO + SEAM)
    place_in = lane & (HALF - 1)
    late = (sub >= SPECIES) & (place_in >= SEAM - LATE) & (place_in < COLS - LATE)
    late = late & ((sub < 7) | (lane < HALF))
    return jnp.where(early | late, tile, 0.0)


def by_species(tile):
    lane, sub = lanes(tile.shape), subs(tile.shape)
    left = lane < HALF
    out = tile
    out = out + jnp.where((sub == 0) & left, pltpu.roll(tile, 3, 0), 0.0)
    pick = ((sub == 1) & ~left) | ((sub == 2) & left)
    out = out + jnp.where(pick, pltpu.roll(tile, 4, 0), 0.0)
    pick = ((sub == 3) & ~left) | ((sub == 4) & left)
    out = out + jnp.where(pick, pltpu.roll(tile, 5, 0), 0.0)
    return out[:SPECIES]


def keep(acc, group, tile):
    acc[group * SPECIES : (group + 1) * SPECIES, :] = by_species(tile)


def split3(x):
    hi = x.astype(jnp.bfloat16)
    rest = x - hi.astype(F32)
    mid = rest.astype(jnp.bfloat16)
    lo = (rest - mid.astype(F32)).astype(jnp.bfloat16)
    return jnp.concatenate([hi, mid, lo], axis=0)


def exact_dot(x, onehot):
    n = x.shape[0]
    y = jnp.dot(
        jnp.concatenate([split3(x)], axis=0), onehot, preferred_element_type=F32
    )
    return y[:n] + y[n : 2 * n] + y[2 * n :]


def build_scatter(got, onehot):
    for m in range(MATS):
        col = jnp.broadcast_to(got[:, MAP_LANE + m : MAP_LANE + m + 1], (TOTAL, COLS))
        for k in range(4):
            target = (lanes((TOTAL, COLS)) + k * COLS).astype(F32)
            onehot[m * TOTAL : (m + 1) * TOTAL, k * COLS : (k + 1) * COLS] = jnp.where(
                col == target, 1.0, 0.0
            ).astype(jnp.bfloat16)


def build_gather(turned, onehot):
    for m in range(MATS):
        row = jnp.broadcast_to(turned[MAP_LANE + m : MAP_LANE + m + 1, :], (COLS, TOTAL))
        for k in range(4):
            target = (subs((COLS, TOTAL)) + k * COLS).astype(F32)
            onehot[k * COLS : (k + 1) * COLS, m * TOTAL : (m + 1) * TOTAL] = jnp.where(
                row == target, 1.0, 0.0
            ).astype(jnp.bfloat16)


def build_near(got, onehot):
    gx, gy = lax.axis_index("grp"), lax.axis_index("gy")
    lane = lanes((1, COLS))
    row = jnp.full((1, COLS), -1.0, F32)
    for iy in range(3):
        y = lax.rem(gy + (N_GY - 1 + iy), N_GY)
        for ix in range(3):
            x = jnp.clip(gx + (ix - 1), 0, N_GRP - 1)
            region = iy * 3 + ix
            here = got[pl.ds(x * N_GY + y, 1), :]
            inside = (lane >= region * MATS) & (lane < (region + 1) * MATS)
            row = jnp.where(inside, turn(here, region * MATS - MAP_LANE), row)
    for k in range(4):
        target = (subs((COLS, COLS)) + k * COLS).astype(F32)
        onehot[k * COLS : (k + 1) * COLS, :] = jnp.where(
            jnp.broadcast_to(row, (COLS, COLS)) == target, 1.0, 0.0
        ).astype(jnp.bfloat16)


def coarse_solve(sums, turned, scatter):
    res = exact_dot(sums, scatter[...])
    parts = []
    for k in range(4):
        total = None
        for t in range(SPECIES):
            start = INV_LANE + k * SPECIES * SPECIES + t * SPECIES
            term = turned[start : start + 8, :] * res[t : t + 1, k * COLS : (k + 1) * COLS]
            total = term if total is None else total + term
        parts.append(total)
    sol = jnp.concatenate(parts, axis=1)
    return jnp.where(subs(sol.shape) < SPECIES, sol, 0.0)


def local_sums(turned, group):
    x = jnp.concatenate(
        [turned[(group + m) * SPECIES : (group + m) * SPECIES + 8, :] for m in range(MATS)], axis=1
    )
    return jnp.where(subs(x.shape) < SPECIES, x, 0.0)


def spread_values(near, values):
    lane, sub = lanes((8, COLS)), subs((8, COLS))

    def arrange(a, b, c):
        row = lambda s: jnp.broadcast_to(near[s : s + 1, :], (8, COLS))
        out = jnp.where(sub == 5, row(a), near)
        return jnp.where(sub == 7, row(c), jnp.where(sub == 6, row(b), out))

    left, right = arrange(0, 2, 4), arrange(1, 3, 4)
    early = sub < SPECIES
    for iy in range(3):
        for m in range(MATS):
            column = lambda v, ix: jnp.broadcast_to(
                v[:, (iy * 3 + ix) * MATS + m : (iy * 3 + ix) * MATS + m + 1], (8, COLS)
            )
            first = jnp.where(early & (lane < HALO), column(left, 0), column(left, 1))
            first = jnp.where(~early & (lane >= COLS - LATE), column(left, 2), first)
            second = jnp.where(lane >= HALF + COLS - LATE, column(right, 2), column(right, 1))
            values[(iy * MATS + m) * 8 : (iy * MATS + m + 1) * 8, :] = jnp.where(
                early | (lane < HALF), first, second
            )


def coarse_rows(values, mat, wide, emit):
    for iy, first, count in ((0, TOP - wide, wide), (1, TOP, ROWS), (2, TOP + ROWS, wide)):
        if count == 0:
            continue
        v = [values[(iy * MATS + m) * 8 : (iy * MATS + m + 1) * 8, :] for m in range(MATS)]

        def step(y, carry):
            for l in range(LAYERS):
                emit(l, y, coarse_pick(v, mat[at(l, y), :]))
            return carry

        each_row(first, count, step)


def coarse_pick(v, m):
    out = jnp.where(m == 1.0, v[1], v[0])
    out = jnp.where(m == 2.0, v[2], out)
    return jnp.where(m == 3.0, v[3], out)


def table_kernel(
    diff, planes, x_low, x_high, y_low, y_high, acc_in,
    cap_w, mat_w, gy, gx, gz, scale, y0, acc, b_w,
    w, za,
):
    lane, sub = lanes((8, COLS)), subs((8, COLS))
    left = lane < HALF

    pairs = ((0, 1), (2, 3), (4, 4))
    d_late = [
        [jnp.where(left, diff[m, a], diff[m, b]) for m in range(MATS)] for a, b in pairs
    ]

    def choose(v, is1, is2, is3):
        return jnp.where(is3, v[3], jnp.where(is2, v[2], jnp.where(is1, v[1], v[0])))

    def fill(own, low, high, l, row, y):
        rows = pl.ds(row, 8)

        def both(kind):
            v = own[kind * LAYERS + l, rows, :]
            early = jnp.where(lane < HALO, turn(low[l, rows, :], -HALO * kind), turn(v, HALO))
            beyond = turn(high[l, rows, :], COLS - LATE - HALO * kind)
            return early, jnp.where(lane < COLS - LATE, turn(v, -LATE), beyond)

        def put(dst, s, v):
            dst[pl.ds((y + l * TALL) * 8 + s, 8, stride=8), :] = v

        late_b = []
        for s in range(SPECIES):
            early, late = both(s)
            put(b_w, s, early)
            late_b.append(late)
        for i, (a, b) in enumerate(pairs):
            put(b_w, SPECIES + i, jnp.where(left, late_b[a], turn(late_b[b], HALF)))
        for dst, kind in ((cap_w, SPECIES + 1), (mat_w, SPECIES + 2)):
            early, late = both(kind)
            late = jnp.where(left, late, turn(late, HALF))
            for s in range(8):
                put(dst, s, early if s < SPECIES else late)
        m_early, m_late = early, late
        early, late = both(SPECIES)
        late = jnp.where(left, late, turn(late, HALF))
        is_m = [m_early == float(m) for m in (1, 2, 3)]
        down, up = jnp.exp(-0.5 * early), jnp.exp(0.5 * early)
        drift = (down, up, down * down, up * up, down)
        for s in range(SPECIES):
            put(w, s, choose([diff[m, s] for m in range(MATS)], *is_m) * drift[s])
        is_m = [m_late == float(m) for m in (1, 2, 3)]
        down, up = jnp.exp(-0.5 * late), jnp.exp(0.5 * late)
        mixed = jnp.where(left, down, up)
        drift = (mixed, mixed * mixed, down)
        for i in range(3):
            put(w, SPECIES + i, choose(d_late[i], *is_m) * drift[i])

    edge_low = (y_low.at[PLANES : PLANES + GROUPS], y_low.at[PLANES + GROUPS : PLANES + 2 * GROUPS])
    edge_high = (y_high.at[PLANES : PLANES + GROUPS], y_high.at[PLANES + GROUPS : PLANES + 2 * GROUPS])

    @pl.loop(0, LAYERS)
    def _(l):
        for row in range(0, RHALO, 8):
            fill(y_low, *edge_low, l, row, row)

    @pl.loop(0, LAYERS)
    def _(l):
        for row in range(0, ROWS, 8):
            fill(planes, x_low, x_high, l, row, TOP + row)

    @pl.loop(0, LAYERS)
    def _(l):
        for row in range(0, RHALO, 8):
            fill(y_high, *edge_high, l, row, TOP + ROWS + row)

    me_x = lax.axis_index("grp")
    closed = ((sub >= SPECIES) & ((lane & (HALF - 1)) == COLS - 1 - LATE) & (me_x == N_GRP - 1)) | (
        (sub < SPECIES) & (lane == HALO - 1) & (me_x == 0)
    )
    span = range(LAYERS)
    first = TOP - 12

    def edge_step(y, carry):
        now, edge_y = carry
        nxt, out_y = [], []
        ez_below = None
        for l in span:
            here = at(l, y)
            c = now[l]
            above = w[at(l, y + 1), :]
            ey = harmonic(c, above)
            ex = jnp.where(closed, 0.0, harmonic(c, turn(c, -1)))
            LATER.put(gy, here, ey)
            LATER.put(gx, here, ex)
            d = cap_w[here, :] + ey + edge_y[l] + ex + turn(ex, 1)
            if ez_below is not None:
                d = d + ez_below
            if l + 1 < LAYERS:
                ez_below = 0.5 * harmonic(c, now[l + 1])
                LATER.put(gz, here, ez_below)
                d = d + ez_below
            LATER.put(scale, here, DAMPING / d)
            nxt.append(above)
            out_y.append(ey)
        return nxt, out_y

    now = [w[at(l, first), :] for l in span]
    edge_y = [harmonic(w[at(l, first - 1), :], now[l]) for l in span]
    each_row(first, ROWS + 24, edge_step, (now, edge_y))

    ops = (cap_w, gy, gx, gz, scale)
    start_sweep(b_w, za, scale, 12)
    sweep(za, b_w, y0, ops, 10)
    sweep(y0, b_w, za, ops, 10)
    sweep(za, b_w, y0, ops, 8)

    acc[...] = acc_in[...]
    zero = jnp.zeros((8, COLS), F32)
    last = TOP + ROWS - 1
    cy = [zero] * 16
    for l in span:
        code = mat_w[at(l, last), :] * 4.0 + mat_w[at(l, last + 1), :]
        edge = gy[at(l, last), :]
        for i in range(16):
            cy[i] = cy[i] + jnp.where(code == float(i), edge, 0.0)
    for i in range(16):
        keep(acc, G_CY + i, used(cy[i]))

    place_in = lane & (HALF - 1)

    def cross_step(y8, cx):
        side, side_code = zero, zero - 1.0
        for r in range(8):
            for l in span:
                here = at(l, TOP + 8 * y8 + r)
                p = r * LAYERS + l
                m = mat_w[here, :]
                code = m * 4.0 + turn(m, -1)
                target = place_in == COLS - 1 - LATE - p
                side = jnp.where(target, turn(gx[here, :], -p), side)
                side_code = jnp.where(target, turn(code, -p), side_code)
        return [cx[i] + jnp.where(side_code == float(i), side, 0.0) for i in range(16)]

    cx = lax.fori_loop(0, ROWS // 8, cross_step, [zero] * 16)
    valid = (sub >= SPECIES) & ((sub < 7) | left)
    for i in range(16):
        keep(acc, G_CX + i, jnp.where(valid, cx[i], 0.0))


def first_kernel(
    planes, got, cap_w, mat_w, gy, gx, gz, scale, y0, acc_in, b_w,
    second, z0, w0, u_out,
    za, zb, scatter, near_hot, turned, values, acc,
):
    ops = (cap_w, gy, gx, gz, scale)

    turned[...] = got[...].T
    build_scatter(got, scatter)
    build_near(got, near_hot)
    sol = coarse_solve(local_sums(turned, 0), turned, scatter)
    spread_values(exact_dot(sol, near_hot[...]), values)

    def add_coarse(l, y, c):
        LATER.put(z0, at(l, y), y0[at(l, y), :] + c)

    coarse_rows(values, mat_w, 8, add_coarse)
    image(z0, w0, ops, 8)
    start_sweep(w0, za, scale, 8)
    sweep(za, w0, zb, ops, 6)
    sweep(zb, w0, za, ops, 6)
    sweep(za, w0, u_out, ops, 4)

    acc[...] = acc_in[...]

    def emit(l, y, u, au, carry):
        rw, rau, mom = carry
        here = at(l, y)
        m = mat_w[here, :]
        wv, zv, bv = w0[here, :], z0[here, :], b_w[here, :]
        is_m = [m == float(i) for i in range(MATS)]
        rw = [rw[i] + jnp.where(is_m[i], wv, 0.0) for i in range(MATS)]
        rau = [rau[i] + jnp.where(is_m[i], au, 0.0) for i in range(MATS)]
        mom = [mom[0] + bv * zv, mom[1] + zv * wv, mom[2] + wv * u, mom[3] + u * au]
        return rw, rau, mom

    zero = jnp.zeros((8, COLS), F32)
    sums = stencil(u_out, ops, 0, emit, ([zero] * 4, [zero] * 4, [zero] * 4))
    for group, tiles in zip((G_RW, G_RAU, G_MOM), sums):
        for i, v in enumerate(tiles):
            keep(acc, group + i, used(v))

    even = lax.rem(subs((2 * TOTAL, COLS)), 2) == 0
    second[...] = jnp.where(even, place(acc[0:COLS, :]), place(acc[COLS : 2 * COLS, :]))


def next_y(x):
    y = lax.rem(lanes(x.shape), N_GY)
    return jnp.where(y == N_GY - 1, turn(x, N_GY - 1), turn(x, -1))


def prev_y(x):
    y = lax.rem(lanes(x.shape), N_GY)
    return jnp.where(y == 0, turn(x, -(N_GY - 1)), turn(x, 1))


def total_of(x):
    return jnp.sum(jnp.sum(x, axis=0, keepdims=True), axis=1, keepdims=True)


def second_kernel(
    planes, got, got2, cap, mat, gy, gx, gz, scale, z0, w0, u,
    out_x, out_r, out_z,
    v1, w1, za, zb, px, pr, pz, scatter, gather, near_hot, turned, turned2, values, values2,
):
    turned[...] = got[...].T
    turned2[0:COLS, :] = got2[pl.ds(0, TOTAL, stride=2), :].T
    turned2[COLS : 2 * COLS, :] = got2[pl.ds(1, TOTAL, stride=2), :].T
    build_scatter(got, scatter)
    build_gather(turned, gather)
    build_near(got, near_hot)

    sums_w = local_sums(turned2, G_RW)
    sol = coarse_solve(sums_w, turned, scatter)
    spread_values(exact_dot(sol, near_hot[...]), values)
    c_all = exact_dot(sol, gather[...])
    c = [c_all[:, m * TOTAL : (m + 1) * TOTAL] for m in range(MATS)]

    def rows5(group):
        return turned2[group * SPECIES : group * SPECIES + 8, :]

    live = subs((8, TOTAL)) < SPECIES
    bc = [turned2[ROW_CAP + m : ROW_CAP + m + 1, :] * c[m] for m in range(MATS)]
    n = 0
    for i in range(MATS):
        for j in range(i + 1, MATS):
            f = rows5(G_S + n) * (c[i] - c[j])
            bc[i] = bc[i] + f
            bc[j] = bc[j] - f
            n += 1
    c_y = [next_y(v) for v in c]
    c_x = [turn(v, -N_GY) for v in c]
    back_y = [jnp.zeros((8, TOTAL), F32)] * MATS
    back_x = [jnp.zeros((8, TOTAL), F32)] * MATS
    for i in range(MATS):
        for j in range(MATS):
            f = rows5(G_CY + 4 * i + j) * (c[i] - c_y[j])
            bc[i] = bc[i] + f
            back_y[j] = back_y[j] + f
            f = rows5(G_CX + 4 * i + j) * (c[i] - c_x[j])
            bc[i] = bc[i] + f
            back_x[j] = back_x[j] + f
    for j in range(MATS):
        bc[j] = jnp.where(live, bc[j] - prev_y(back_y[j]) - turn(back_x[j], N_GY), 0.0)
    bc_all = jnp.concatenate(bc, axis=1)
    sums_au = local_sums(turned2, G_RAU)
    sol2 = coarse_solve(sums_au + bc_all, turned, scatter)
    spread_values(exact_dot(sol2, near_hot[...]), values2)

    def moment(i):
        return total_of(jnp.where(live, rows5(G_MOM + i), 0.0))

    m0, m1 = moment(0), moment(1)
    m2 = moment(2) + total_of(sums_w * c_all)
    m3 = moment(3) + total_of((2.0 * sums_au + bc_all) * c_all)
    a0 = m0 / m1
    rz1 = m0 - 2.0 * a0 * m1 + a0 * a0 * m2
    g = 1.0 + rz1 / m0
    a1 = rz1 / (g * g * m1 - 2.0 * a0 * g * m2 + a0 * a0 * m3)
    ca = jnp.broadcast_to(a0 + a1 * g, (8, COLS))
    cb = jnp.broadcast_to(a1 * a0, (8, COLS))

    ops = (cap, gy, gx, gz, scale)

    def add_coarse(l, y, c):
        LATER.put(v1, at(l, y), u[at(l, y), :] + c)

    coarse_rows(values, mat, 4, add_coarse)
    image(v1, w1, ops, 4)
    start_sweep(w1, za, scale, 4)
    sweep(za, w1, zb, ops, 2)
    sweep(zb, w1, za, ops, 2)
    own_values = [values2[(MATS + m) * 8 : (MATS + m + 1) * 8, :] for m in range(MATS)]

    def emit(l, y, z, out, carry):
        here = at(l, y)
        w1v, v1v = w1[here, :], v1[here, :]
        z0v, w0v = z0[here, :], w0[here, :]
        v2 = z + scale[here, :] * (w1v - out) + coarse_pick(own_values, mat[here, :])
        LATER.put(px, here, ca * z0v - cb * v1v)
        LATER.put(pr, here, ca * w0v - cb * w1v)
        LATER.put(pz, here, z0v - ca * v1v + cb * v2)
        return carry

    stencil(za, ops, 0, emit)

    lane = lanes((8, COLS))

    def unpacked(src, l, row, s):
        start = (l * TALL + TOP + row) * 8
        early = src[pl.ds(start + s, 8, stride=8), :]
        late = src[pl.ds(start + SPECIES + s // 2, 8, stride=8), :]
        return jnp.where(
            lane < SEAM, turn(early, -HALO), turn(late, LATE - (s % 2) * HALF)
        )

    for s in range(SPECIES):
        for l in range(LAYERS):
            for row in range(0, ROWS, 8):
                k, rows = s * LAYERS + l, slice(row, row + 8)
                out_x[k, rows, :] = unpacked(px, l, row, s)
                out_r[k, rows, :] = planes[k, rows, :] - unpacked(pr, l, row, s)
                out_z[k, rows, :] = unpacked(pz, l, row, s)


def shape(*dims):
    return jax.ShapeDtypeStruct(dims, F32)


VMEM = pl.BlockSpec(memory_space=pltpu.VMEM)
SMEM = pl.BlockSpec(memory_space=pltpu.SMEM)
PARAMS = pltpu.CompilerParams(vmem_limit_bytes=20 * 1024 * 1024)


def run(kernel, outs, scratch, in_specs, cost, *args):
    return pl.pallas_call(
        kernel,
        out_shape=outs,
        in_specs=in_specs,
        out_specs=jax.tree.map(lambda _: VMEM, outs),
        scratch_shapes=scratch,
        compiler_params=PARAMS,
        cost_estimate=pl.CostEstimate(flops=cost, bytes_accessed=1 << 20, transcendentals=0),
    )(*args)


def shifts(axis, count):
    forward = [(i, (i + 1) % count) for i in range(count)]
    backward = [(target, source) for source, target in forward]
    return (functools.partial(lax.ppermute, axis_name=axis, perm=p) for p in (forward, backward))


def to_all(rows):
    got = lax.all_to_all(rows.reshape(TOTAL, -1, COLS), BOTH, 0, 0, tiled=True)
    return got.reshape(rows.shape)


def body(right_side, potential, capacity, diffusivity, material, coarse_map, coarse_inverse):
    b = right_side.reshape(FIELDS, ROWS, COLS)
    right, left = shifts("grp", N_GRP)
    down, up = shifts("gy", N_GY)

    packed = shape(GROUPS, ROWS, COLS)
    planes, to_low, to_high = run(
        pack_kernel,
        (shape(PLANES, ROWS, COLS), packed, packed),
        [],
        [VMEM] * 2,
        1 << 20,
        jnp.concatenate([b, potential, capacity]), material,
    )
    x_low, x_high = right(to_high), left(to_low)
    code = pltpu.VMEM((LAYERS, ROWS, COLS), F32)
    first, acc = run(
        own_kernel,
        (shape(TOTAL, COLS), shape(2 * COLS, COLS)),
        [pltpu.VMEM((FIELDS, ROWS, COLS), F32), code, code, code]
        + [pltpu.VMEM((24, COLS), F32), pltpu.VMEM((8, COLS), jnp.int32)],
        [SMEM] + [VMEM] * 3,
        1 << 20,
        diffusivity.T, planes, coarse_map, jnp.transpose(coarse_inverse, (1, 0, 2)),
    )

    strips = shape(PLANES + 2 * GROUPS, RHALO, COLS)
    to_low, to_high = run(
        rows_kernel, (strips, strips), [], [VMEM] * 3, 1 << 20, planes, x_low, x_high
    )
    first, to_low, to_high = lax.optimization_barrier((first, to_low, to_high))
    y_low, y_high = down(to_high), up(to_low)
    got, y_low, y_high = lax.optimization_barrier((to_all(first), y_low, y_high))

    packed = shape(LAYERS * TALL * 8, COLS)
    field = shape(FIELDS, ROWS, COLS)
    big = pltpu.VMEM(packed.shape, F32)
    hot = pltpu.VMEM((NC, MATS * TOTAL), jnp.bfloat16)
    near = pltpu.VMEM((NC, COLS), jnp.bfloat16)
    square = pltpu.VMEM((COLS, COLS), F32)
    double = pltpu.VMEM((2 * COLS, COLS), F32)
    values = pltpu.VMEM((3 * MATS * 8, COLS), F32)
    cap_w, mat_w, gy, gx, gz, scale, y0, acc, b_w = run(
        table_kernel,
        (packed,) * 7 + (shape(2 * COLS, COLS), packed),
        [big] * 2,
        [SMEM] + [VMEM] * 6,
        1 << 30,
        diffusivity.T, planes, x_low, x_high, y_low, y_high, acc,
    )
    second, z0, w0, u = run(
        first_kernel,
        (shape(2 * TOTAL, COLS), packed, packed, packed),
        [big] * 2 + [hot, near, square, values, double],
        [VMEM] * 11,
        1 << 30,
        planes, got, cap_w, mat_w, gy, gx, gz, scale, y0, acc, b_w,
    )
    got2 = to_all(second)
    out = run(
        second_kernel,
        (field, field, field),
        [big] * 7 + [hot, hot, near, square, double, values, values],
        [VMEM] * 12,
        1 << 30,
        planes, got, got2, cap_w, mat_w, gy, gx, gz, scale, z0, w0, u,
    )
    return tuple(o.reshape(right_side.shape) for o in out)


def solution(mesh):
    placed = (
        P(None, None, "gy", "grp"),
        P(None, "gy", "grp"),
        P(None, "gy", "grp"),
        P(),
        P(None, "gy", "grp"),
        P("gy", "grp", None),
        P(("grp", "gy"), None, None),
    )
    return jax.shard_map(
        body,
        mesh=mesh,
        in_specs=placed,
        out_specs=(P(None, None, "gy", "grp"),) * 3,
        check_vma=False,
    )
```

```python
import functools

import jax
import jax.numpy as jnp
from jax import lax
from jax.experimental import pallas as pl
from jax.experimental.pallas import tpu as pltpu
from jax.sharding import PartitionSpec as P

SPECIES = 5
LAYERS = 4
MATS = 4
FIELDS = SPECIES * LAYERS
PLANES = FIELDS + 3 * LAYERS
POT0, CAP0, MAT0 = FIELDS, FIELDS + LAYERS, FIELDS + 2 * LAYERS
ROWS = 32
COLS = 128
N_GRP = 4
N_GY = 32
TOTAL = N_GRP * N_GY
NC = 512
DAMPING = 2.0 / 3.0
BOTH = ("grp", "gy")

HALO = 12
GROUPS = LAYERS
RHALO = 16
TALL = ROWS + 2 * RHALO
TOP = RHALO
HALF = COLS // 2
LATE = COLS + HALO - HALF
SEAM = 96
F32 = jnp.float32

G_RW, G_RAU, G_S, G_CY, G_CX, G_MOM = 0, 4, 8, 14, 30, 46
ROW_CAP = 250
MAP_LANE = 20
INV_LANE = 24


def lanes(shape):
    return lax.broadcasted_iota(jnp.int32, shape, 1)


def subs(shape):
    return lax.broadcasted_iota(jnp.int32, shape, 0)


def pack_kernel(fields, mat, planes, to_low, to_high):
    planes[0:MAT0] = fields[...]
    planes[MAT0:PLANES] = mat[...].astype(F32)
    lane = lanes((ROWS, COLS))
    for g in range(GROUPS):
        low = jnp.zeros((ROWS, COLS), F32)
        high = jnp.zeros((ROWS, COLS), F32)
        for j in range(PLANES // LAYERS):
            v = planes[j * LAYERS + g]
            inside = (lane >= HALO * j) & (lane < HALO * (j + 1))
            low = jnp.where(inside, turn(v, HALO * j), low)
            high = jnp.where(inside, turn(v, HALO * j + HALO), high)
        to_low[g] = low
        to_high[g] = high


def turn(v, shift):
    shift = shift % v.shape[1]
    return v if shift == 0 else pltpu.roll(v, shift, 1)


def place(rows):
    n = rows.shape[0]
    total = jnp.sum(rows, axis=1, keepdims=True)
    spread = jnp.where(lanes((n, COLS)) == subs((n, COLS)), total, 0.0)
    return jnp.sum(spread, axis=0, keepdims=True)


def fold(v):
    return jnp.sum(v, axis=0, keepdims=True)


def harmonic(a, b):
    return 2.0 * a * b / (a + b)


def after(v, nxt, axis):
    first = lax.broadcasted_iota(jnp.int32, v.shape, axis) == 0
    return pltpu.roll(jnp.where(first, nxt, v), v.shape[axis] - 1, axis)


def power(m):
    p = jnp.where(m == 1.0, 2.0, 1.0)
    p = jnp.where(m == 2.0, 4.0, p)
    return jnp.where(m == 3.0, 8.0, p)


def own_kernel(diff, planes, cmap, inverse, out, acc, w, code_y, code_x, code_z, part, ids):
    part[...] = jnp.zeros(part.shape, F32)
    row = jnp.zeros((1, COLS), F32)
    for s in range(SPECIES):
        part[0:4, 0:SPECIES] = inverse[s]
        for k in range(4):
            row = row + turn(part[k : k + 1, :], INV_LANE + (k * SPECIES + s) * SPECIES)
    part[0:4, :] = jnp.zeros((4, COLS), F32)
    ids[...] = jnp.zeros(ids.shape, jnp.int32)
    ids[0:1, 0:MATS] = cmap[0]
    q = ids[0:1, :]
    row = row + turn(((q & 3) * TOTAL + (q >> 2)).astype(F32), MAP_LANE)
    for s in range(SPECIES):
        for m in range(MATS):
            total = jnp.zeros((ROWS, COLS), F32)
            for l in range(LAYERS):
                total = total + jnp.where(planes[MAT0 + l] == m, planes[s * LAYERS + l], 0.0)
            part[m * SPECIES + s : m * SPECIES + s + 1, :] = fold(total)
    out[...] = jnp.broadcast_to(row + place(part[...]), (TOTAL, COLS))

    acc[...] = jnp.zeros(acc.shape, F32)
    lane, sub = lanes((8, COLS)), subs((8, COLS))
    tiles = [8 * t for t in range(ROWS // 8)]
    for r in tiles:
        here = pl.ds(r, 8)
        for l in range(LAYERS):
            m = planes[MAT0 + l, here, :]
            is1, is2, is3 = m == 1.0, m == 2.0, m == 3.0
            down = jnp.exp(-0.5 * planes[POT0 + l, here, :])
            up = jnp.exp(0.5 * planes[POT0 + l, here, :])
            drift = (down, up, down * down, up * up, down)
            for s in range(SPECIES):
                d = jnp.where(is1, diff[1, s], diff[0, s])
                d = jnp.where(is2, diff[2, s], d)
                d = jnp.where(is3, diff[3, s], d)
                w[s * LAYERS + l, here, :] = d * drift[s]
            p = power(m)
            if r == tiles[-1]:
                code = jnp.where(sub == 7, 0.0, p + power(after(m, m, 0)))
            else:
                code = p + power(after(m, planes[MAT0 + l, pl.ds(r + 8, 8), :], 0))
            code_y[l, here, :] = code
            code_x[l, here, :] = jnp.where(lane == COLS - 1, 0.0, p + power(turn(m, -1)))
            if l + 1 < LAYERS:
                code_z[l, here, :] = p + power(planes[MAT0 + l + 1, here, :])

    @pl.loop(0, SPECIES)
    def _(s):
        pairs = [jnp.zeros((8, COLS), F32)] * 6
        codes = (3.0, 5.0, 9.0, 6.0, 10.0, 12.0)
        for r in tiles:
            here = pl.ds(r, 8)
            for l in range(LAYERS):
                k = s * LAYERS + l
                c = w[k, here, :]
                nxt = c if r == tiles[-1] else w[k, pl.ds(r + 8, 8), :]
                kinds = [
                    (code_y[l, here, :], harmonic(c, after(c, nxt, 0))),
                    (code_x[l, here, :], harmonic(c, turn(c, -1))),
                ]
                if l + 1 < LAYERS:
                    kinds.append((code_z[l, here, :], 0.5 * harmonic(c, w[k + 1, here, :])))
                for code, edge in kinds:
                    for i in range(6):
                        pairs[i] = pairs[i] + jnp.where(code == codes[i], edge, 0.0)
        for i in range(6):
            acc[pl.ds((G_S + i) * SPECIES + s, 1), :] = fold(pairs[i])

    for i in range(MATS):
        total = jnp.zeros((ROWS, COLS), F32)
        for l in range(LAYERS):
            total = total + jnp.where(planes[MAT0 + l] == i, planes[CAP0 + l], 0.0)
        acc[ROW_CAP + i : ROW_CAP + i + 1, :] = fold(total)


def rows_kernel(planes, from_low, from_high, to_low, to_high):
    for k in range(PLANES):
        to_low[k] = planes[k, :RHALO]
        to_high[k] = planes[k, ROWS - RHALO :]
    for g in range(GROUPS):
        for i, part in enumerate((from_low, from_high)):
            k = PLANES + i * GROUPS + g
            to_low[k] = part[g, :RHALO]
            to_high[k] = part[g, ROWS - RHALO :]


def at(l, y):
    if isinstance(y, int):
        return pl.ds((y + l * TALL) * 8, 8)
    return pl.ds(pl.multiple_of((y + l * TALL) * 8, 8), 8)


class Later:
    def __init__(self):
        self.held = []

    def put(self, ref, where, value):
        self.held.append((ref, where, value))

    def flush(self):
        for ref, where, value in self.held:
            ref[where, :] = value
        self.held = []


LATER = Later()
BLOCK = 0


def each_row(first, count, step, carry=()):
    size = BLOCK if BLOCK and count % BLOCK == 0 else 4
    if BLOCK == 0:
        for r in range(count):
            carry = step(first + r, carry)
            LATER.flush()
        return carry

    def block(i, carry):
        for r in range(size):
            carry = step(first + size * i + r, carry)
        LATER.flush()
        return carry

    return lax.fori_loop(0, count // size, block, carry)


def stencil(src, ops, wide, emit, carry=()):
    cap, gy, gx, gz = ops[:4]
    first = TOP - wide
    span = range(LAYERS)
    now = [src[at(l, first), :] for l in span]
    flux = [gy[at(l, first - 1), :] * (src[at(l, first - 1), :] - now[l]) for l in span]

    def step(y, carry):
        now, flux, carry = carry
        nxt, out_flux = [], []
        flux_z = None
        for l in span:
            here = at(l, y)
            u = now[l]
            above = src[at(l, y + 1), :]
            flux_x = gx[here, :] * (u - turn(u, -1))
            flux_y = gy[here, :] * (u - above)
            out = cap[here, :] * u + (flux_x - turn(flux_x, 1)) + (flux_y - flux[l])
            if flux_z is not None:
                out = out - flux_z
            if l + 1 < LAYERS:
                flux_z = gz[here, :] * (u - now[l + 1])
                out = out + flux_z
            nxt.append(above)
            out_flux.append(flux_y)
            carry = emit(l, y, u, out, carry)
        return nxt, out_flux, carry

    return each_row(first, ROWS + 2 * wide, step, (now, flux, carry))[2]


def sweep(src, resid, dst, ops, wide):
    scale = ops[4]

    def emit(l, y, u, out, carry):
        here = at(l, y)
        LATER.put(dst, here, u + scale[here, :] * (resid[here, :] - out))
        return carry

    stencil(src, ops, wide, emit)


def image(src, dst, ops, wide):
    def emit(l, y, u, out, carry):
        LATER.put(dst, at(l, y), out)
        return carry

    stencil(src, ops, wide, emit)


def start_sweep(resid, dst, scale, wide):
    def step(y, carry):
        for l in range(LAYERS):
            here = at(l, y)
            LATER.put(dst, here, scale[here, :] * resid[here, :])
        return carry

    each_row(TOP - wide, ROWS + 2 * wide, step)


def used(tile):
    lane, sub = lanes(tile.shape), subs(tile.shape)
    early = (sub < SPECIES) & (lane >= HALO) & (lane < HALO + SEAM)
    place_in = lane & (HALF - 1)
    late = (sub >= SPECIES) & (place_in >= SEAM - LATE) & (place_in < COLS - LATE)
    late = late & ((sub < 7) | (lane < HALF))
    return jnp.where(early | late, tile, 0.0)


def by_species(tile):
    lane, sub = lanes(tile.shape), subs(tile.shape)
    left = lane < HALF
    out = tile
    out = out + jnp.where((sub == 0) & left, pltpu.roll(tile, 3, 0), 0.0)
    pick = ((sub == 1) & ~left) | ((sub == 2) & left)
    out = out + jnp.where(pick, pltpu.roll(tile, 4, 0), 0.0)
    pick = ((sub == 3) & ~left) | ((sub == 4) & left)
    out = out + jnp.where(pick, pltpu.roll(tile, 5, 0), 0.0)
    return out[:SPECIES]


def keep(acc, group, tile):
    acc[group * SPECIES : (group + 1) * SPECIES, :] = by_species(tile)


def split3(x):
    hi = x.astype(jnp.bfloat16)
    rest = x - hi.astype(F32)
    mid = rest.astype(jnp.bfloat16)
    lo = (rest - mid.astype(F32)).astype(jnp.bfloat16)
    return jnp.concatenate([hi, mid, lo], axis=0)


def exact_dot(x, onehot):
    n = x.shape[0]
    y = jnp.dot(
        jnp.concatenate([split3(x)], axis=0), onehot, preferred_element_type=F32
    )
    return y[:n] + y[n : 2 * n] + y[2 * n :]


def build_scatter(got, onehot):
    for m in range(MATS):
        col = jnp.broadcast_to(got[:, MAP_LANE + m : MAP_LANE + m + 1], (TOTAL, COLS))
        for k in range(4):
            target = (lanes((TOTAL, COLS)) + k * COLS).astype(F32)
            onehot[m * TOTAL : (m + 1) * TOTAL, k * COLS : (k + 1) * COLS] = jnp.where(
                col == target, 1.0, 0.0
            ).astype(jnp.bfloat16)


def build_gather(turned, onehot):
    for m in range(MATS):
        row = jnp.broadcast_to(turned[MAP_LANE + m : MAP_LANE + m + 1, :], (COLS, TOTAL))
        for k in range(4):
            target = (subs((COLS, TOTAL)) + k * COLS).astype(F32)
            onehot[k * COLS : (k + 1) * COLS, m * TOTAL : (m + 1) * TOTAL] = jnp.where(
                row == target, 1.0, 0.0
            ).astype(jnp.bfloat16)


def build_near(got, onehot):
    gx, gy = lax.axis_index("grp"), lax.axis_index("gy")
    lane = lanes((1, COLS))
    row = jnp.full((1, COLS), -1.0, F32)
    for iy in range(3):
        y = lax.rem(gy + (N_GY - 1 + iy), N_GY)
        for ix in range(3):
            x = jnp.clip(gx + (ix - 1), 0, N_GRP - 1)
            region = iy * 3 + ix
            here = got[pl.ds(x * N_GY + y, 1), :]
            inside = (lane >= region * MATS) & (lane < (region + 1) * MATS)
            row = jnp.where(inside, turn(here, region * MATS - MAP_LANE), row)
    for k in range(4):
        target = (subs((COLS, COLS)) + k * COLS).astype(F32)
        onehot[k * COLS : (k + 1) * COLS, :] = jnp.where(
            jnp.broadcast_to(row, (COLS, COLS)) == target, 1.0, 0.0
        ).astype(jnp.bfloat16)


def coarse_solve(sums, turned, scatter):
    res = exact_dot(sums, scatter[...])
    parts = []
    for k in range(4):
        total = None
        for t in range(SPECIES):
            start = INV_LANE + k * SPECIES * SPECIES + t * SPECIES
            term = turned[start : start + 8, :] * res[t : t + 1, k * COLS : (k + 1) * COLS]
            total = term if total is None else total + term
        parts.append(total)
    sol = jnp.concatenate(parts, axis=1)
    return jnp.where(subs(sol.shape) < SPECIES, sol, 0.0)


def local_sums(turned, group):
    x = jnp.concatenate(
        [turned[(group + m) * SPECIES : (group + m) * SPECIES + 8, :] for m in range(MATS)], axis=1
    )
    return jnp.where(subs(x.shape) < SPECIES, x, 0.0)


def spread_values(near, values):
    lane, sub = lanes((8, COLS)), subs((8, COLS))

    def arrange(a, b, c):
        row = lambda s: jnp.broadcast_to(near[s : s + 1, :], (8, COLS))
        out = jnp.where(sub == 5, row(a), near)
        return jnp.where(sub == 7, row(c), jnp.where(sub == 6, row(b), out))

    left, right = arrange(0, 2, 4), arrange(1, 3, 4)
    early = sub < SPECIES
    for iy in range(3):
        for m in range(MATS):
            column = lambda v, ix: jnp.broadcast_to(
                v[:, (iy * 3 + ix) * MATS + m : (iy * 3 + ix) * MATS + m + 1], (8, COLS)
            )
            first = jnp.where(early & (lane < HALO), column(left, 0), column(left, 1))
            first = jnp.where(~early & (lane >= COLS - LATE), column(left, 2), first)
            second = jnp.where(lane >= HALF + COLS - LATE, column(right, 2), column(right, 1))
            values[(iy * MATS + m) * 8 : (iy * MATS + m + 1) * 8, :] = jnp.where(
                early | (lane < HALF), first, second
            )


def coarse_rows(values, mat, wide, emit):
    for iy, first, count in ((0, TOP - wide, wide), (1, TOP, ROWS), (2, TOP + ROWS, wide)):
        if count == 0:
            continue
        v = [values[(iy * MATS + m) * 8 : (iy * MATS + m + 1) * 8, :] for m in range(MATS)]

        def step(y, carry):
            for l in range(LAYERS):
                emit(l, y, coarse_pick(v, mat[at(l, y), :]))
            return carry

        each_row(first, count, step)


def coarse_pick(v, m):
    out = jnp.where(m == 1.0, v[1], v[0])
    out = jnp.where(m == 2.0, v[2], out)
    return jnp.where(m == 3.0, v[3], out)


def table_kernel(
    diff, planes, x_low, x_high, y_low, y_high, acc_in,
    cap_w, mat_w, gy, gx, gz, scale, y0, acc, b_w,
    w, za,
):
    lane, sub = lanes((8, COLS)), subs((8, COLS))
    left = lane < HALF

    pairs = ((0, 1), (2, 3), (4, 4))
    d_late = [
        [jnp.where(left, diff[m, a], diff[m, b]) for m in range(MATS)] for a, b in pairs
    ]

    def choose(v, is1, is2, is3):
        return jnp.where(is3, v[3], jnp.where(is2, v[2], jnp.where(is1, v[1], v[0])))

    def fill(own, low, high, l, row, y):
        rows = pl.ds(row, 8)

        def both(kind):
            v = own[kind * LAYERS + l, rows, :]
            early = jnp.where(lane < HALO, turn(low[l, rows, :], -HALO * kind), turn(v, HALO))
            beyond = turn(high[l, rows, :], COLS - LATE - HALO * kind)
            return early, jnp.where(lane < COLS - LATE, turn(v, -LATE), beyond)

        def put(dst, s, v):
            dst[pl.ds((y + l * TALL) * 8 + s, 8, stride=8), :] = v

        late_b = []
        for s in range(SPECIES):
            early, late = both(s)
            put(b_w, s, early)
            late_b.append(late)
        for i, (a, b) in enumerate(pairs):
            put(b_w, SPECIES + i, jnp.where(left, late_b[a], turn(late_b[b], HALF)))
        for dst, kind in ((cap_w, SPECIES + 1), (mat_w, SPECIES + 2)):
            early, late = both(kind)
            late = jnp.where(left, late, turn(late, HALF))
            for s in range(8):
                put(dst, s, early if s < SPECIES else late)
        m_early, m_late = early, late
        early, late = both(SPECIES)
        late = jnp.where(left, late, turn(late, HALF))
        is_m = [m_early == float(m) for m in (1, 2, 3)]
        down, up = jnp.exp(-0.5 * early), jnp.exp(0.5 * early)
        drift = (down, up, down * down, up * up, down)
        for s in range(SPECIES):
            put(w, s, choose([diff[m, s] for m in range(MATS)], *is_m) * drift[s])
        is_m = [m_late == float(m) for m in (1, 2, 3)]
        down, up = jnp.exp(-0.5 * late), jnp.exp(0.5 * late)
        mixed = jnp.where(left, down, up)
        drift = (mixed, mixed * mixed, down)
        for i in range(3):
            put(w, SPECIES + i, choose(d_late[i], *is_m) * drift[i])

    edge_low = (y_low.at[PLANES : PLANES + GROUPS], y_low.at[PLANES + GROUPS : PLANES + 2 * GROUPS])
    edge_high = (y_high.at[PLANES : PLANES + GROUPS], y_high.at[PLANES + GROUPS : PLANES + 2 * GROUPS])

    @pl.loop(0, LAYERS)
    def _(l):
        for row in range(0, RHALO, 8):
            fill(y_low, *edge_low, l, row, row)

    @pl.loop(0, LAYERS)
    def _(l):
        for row in range(0, ROWS, 8):
            fill(planes, x_low, x_high, l, row, TOP + row)

    @pl.loop(0, LAYERS)
    def _(l):
        for row in range(0, RHALO, 8):
            fill(y_high, *edge_high, l, row, TOP + ROWS + row)

    me_x = lax.axis_index("grp")
    closed = ((sub >= SPECIES) & ((lane & (HALF - 1)) == COLS - 1 - LATE) & (me_x == N_GRP - 1)) | (
        (sub < SPECIES) & (lane == HALO - 1) & (me_x == 0)
    )
    span = range(LAYERS)
    first = TOP - 12

    def edge_step(y, carry):
        now, edge_y = carry
        nxt, out_y = [], []
        ez_below = None
        for l in span:
            here = at(l, y)
            c = now[l]
            above = w[at(l, y + 1), :]
            ey = harmonic(c, above)
            ex = jnp.where(closed, 0.0, harmonic(c, turn(c, -1)))
            LATER.put(gy, here, ey)
            LATER.put(gx, here, ex)
            d = cap_w[here, :] + ey + edge_y[l] + ex + turn(ex, 1)
            if ez_below is not None:
                d = d + ez_below
            if l + 1 < LAYERS:
                ez_below = 0.5 * harmonic(c, now[l + 1])
                LATER.put(gz, here, ez_below)
                d = d + ez_below
            LATER.put(scale, here, DAMPING / d)
            nxt.append(above)
            out_y.append(ey)
        return nxt, out_y

    now = [w[at(l, first), :] for l in span]
    edge_y = [harmonic(w[at(l, first - 1), :], now[l]) for l in span]
    each_row(first, ROWS + 24, edge_step, (now, edge_y))

    ops = (cap_w, gy, gx, gz, scale)
    start_sweep(b_w, za, scale, 12)
    sweep(za, b_w, y0, ops, 10)
    sweep(y0, b_w, za, ops, 10)
    sweep(za, b_w, y0, ops, 8)

    acc[...] = acc_in[...]
    zero = jnp.zeros((8, COLS), F32)
    last = TOP + ROWS - 1
    cy = [zero] * 16
    for l in span:
        code = mat_w[at(l, last), :] * 4.0 + mat_w[at(l, last + 1), :]
        edge = gy[at(l, last), :]
        for i in range(16):
            cy[i] = cy[i] + jnp.where(code == float(i), edge, 0.0)
    for i in range(16):
        keep(acc, G_CY + i, used(cy[i]))

    place_in = lane & (HALF - 1)

    def cross_step(y8, cx):
        side, side_code = zero, zero - 1.0
        for r in range(8):
            for l in span:
                here = at(l, TOP + 8 * y8 + r)
                p = r * LAYERS + l
                m = mat_w[here, :]
                code = m * 4.0 + turn(m, -1)
                target = place_in == COLS - 1 - LATE - p
                side = jnp.where(target, turn(gx[here, :], -p), side)
                side_code = jnp.where(target, turn(code, -p), side_code)
        return [cx[i] + jnp.where(side_code == float(i), side, 0.0) for i in range(16)]

    cx = lax.fori_loop(0, ROWS // 8, cross_step, [zero] * 16)
    valid = (sub >= SPECIES) & ((sub < 7) | left)
    for i in range(16):
        keep(acc, G_CX + i, jnp.where(valid, cx[i], 0.0))


def first_kernel(
    planes, got, cap_w, mat_w, gy, gx, gz, scale, y0, acc_in, b_w,
    second, z0, w0, u_out, scatter, near_hot, turned,
    za, zb, values, acc,
):
    ops = (cap_w, gy, gx, gz, scale)

    turned[...] = got[...].T
    build_scatter(got, scatter)
    build_near(got, near_hot)
    sol = coarse_solve(local_sums(turned, 0), turned, scatter)
    spread_values(exact_dot(sol, near_hot[...]), values)

    def add_coarse(l, y, c):
        LATER.put(z0, at(l, y), y0[at(l, y), :] + c)

    coarse_rows(values, mat_w, 8, add_coarse)
    image(z0, w0, ops, 8)
    start_sweep(w0, za, scale, 8)
    sweep(za, w0, zb, ops, 6)
    sweep(zb, w0, za, ops, 6)
    sweep(za, w0, u_out, ops, 4)

    acc[...] = acc_in[...]

    def emit(l, y, u, au, carry):
        rw, rau, mom = carry
        here = at(l, y)
        m = mat_w[here, :]
        wv, zv, bv = w0[here, :], z0[here, :], b_w[here, :]
        is_m = [m == float(i) for i in range(MATS)]
        rw = [rw[i] + jnp.where(is_m[i], wv, 0.0) for i in range(MATS)]
        rau = [rau[i] + jnp.where(is_m[i], au, 0.0) for i in range(MATS)]
        mom = [mom[0] + bv * zv, mom[1] + zv * wv, mom[2] + wv * u, mom[3] + u * au]
        return rw, rau, mom

    zero = jnp.zeros((8, COLS), F32)
    sums = stencil(u_out, ops, 0, emit, ([zero] * 4, [zero] * 4, [zero] * 4))
    for group, tiles in zip((G_RW, G_RAU, G_MOM), sums):
        for i, v in enumerate(tiles):
            keep(acc, group + i, used(v))

    even = lax.rem(subs((2 * TOTAL, COLS)), 2) == 0
    second[...] = jnp.where(even, place(acc[0:COLS, :]), place(acc[COLS : 2 * COLS, :]))


def next_y(x):
    y = lax.rem(lanes(x.shape), N_GY)
    return jnp.where(y == N_GY - 1, turn(x, N_GY - 1), turn(x, -1))


def prev_y(x):
    y = lax.rem(lanes(x.shape), N_GY)
    return jnp.where(y == 0, turn(x, -(N_GY - 1)), turn(x, 1))


def total_of(x):
    return jnp.sum(jnp.sum(x, axis=0, keepdims=True), axis=1, keepdims=True)


def second_kernel(
    planes, scatter, near_hot, turned, got2, cap, mat, gy, gx, gz, scale, z0, w0, u,
    out_x, out_r, out_z,
    v1, w1, za, zb, px, pr, pz, gather, turned2, values, values2,
):
    turned2[0:COLS, :] = got2[pl.ds(0, TOTAL, stride=2), :].T
    turned2[COLS : 2 * COLS, :] = got2[pl.ds(1, TOTAL, stride=2), :].T
    build_gather(turned, gather)

    sums_w = local_sums(turned2, G_RW)
    sol = coarse_solve(sums_w, turned, scatter)
    spread_values(exact_dot(sol, near_hot[...]), values)
    c_all = exact_dot(sol, gather[...])
    c = [c_all[:, m * TOTAL : (m + 1) * TOTAL] for m in range(MATS)]

    def rows5(group):
        return turned2[group * SPECIES : group * SPECIES + 8, :]

    live = subs((8, TOTAL)) < SPECIES
    bc = [turned2[ROW_CAP + m : ROW_CAP + m + 1, :] * c[m] for m in range(MATS)]
    n = 0
    for i in range(MATS):
        for j in range(i + 1, MATS):
            f = rows5(G_S + n) * (c[i] - c[j])
            bc[i] = bc[i] + f
            bc[j] = bc[j] - f
            n += 1
    c_y = [next_y(v) for v in c]
    c_x = [turn(v, -N_GY) for v in c]
    back_y = [jnp.zeros((8, TOTAL), F32)] * MATS
    back_x = [jnp.zeros((8, TOTAL), F32)] * MATS
    for i in range(MATS):
        for j in range(MATS):
            f = rows5(G_CY + 4 * i + j) * (c[i] - c_y[j])
            bc[i] = bc[i] + f
            back_y[j] = back_y[j] + f
            f = rows5(G_CX + 4 * i + j) * (c[i] - c_x[j])
            bc[i] = bc[i] + f
            back_x[j] = back_x[j] + f
    for j in range(MATS):
        bc[j] = jnp.where(live, bc[j] - prev_y(back_y[j]) - turn(back_x[j], N_GY), 0.0)
    bc_all = jnp.concatenate(bc, axis=1)
    sums_au = local_sums(turned2, G_RAU)
    sol2 = coarse_solve(sums_au + bc_all, turned, scatter)
    spread_values(exact_dot(sol2, near_hot[...]), values2)

    def moment(i):
        return total_of(jnp.where(live, rows5(G_MOM + i), 0.0))

    m0, m1 = moment(0), moment(1)
    m2 = moment(2) + total_of(sums_w * c_all)
    m3 = moment(3) + total_of((2.0 * sums_au + bc_all) * c_all)
    a0 = m0 / m1
    rz1 = m0 - 2.0 * a0 * m1 + a0 * a0 * m2
    g = 1.0 + rz1 / m0
    a1 = rz1 / (g * g * m1 - 2.0 * a0 * g * m2 + a0 * a0 * m3)
    ca = jnp.broadcast_to(a0 + a1 * g, (8, COLS))
    cb = jnp.broadcast_to(a1 * a0, (8, COLS))

    ops = (cap, gy, gx, gz, scale)

    def add_coarse(l, y, c):
        LATER.put(v1, at(l, y), u[at(l, y), :] + c)

    coarse_rows(values, mat, 4, add_coarse)
    image(v1, w1, ops, 4)
    start_sweep(w1, za, scale, 4)
    sweep(za, w1, zb, ops, 2)
    sweep(zb, w1, za, ops, 2)
    own_values = [values2[(MATS + m) * 8 : (MATS + m + 1) * 8, :] for m in range(MATS)]

    def emit(l, y, z, out, carry):
        here = at(l, y)
        w1v, v1v = w1[here, :], v1[here, :]
        z0v, w0v = z0[here, :], w0[here, :]
        v2 = z + scale[here, :] * (w1v - out) + coarse_pick(own_values, mat[here, :])
        LATER.put(px, here, ca * z0v - cb * v1v)
        LATER.put(pr, here, ca * w0v - cb * w1v)
        LATER.put(pz, here, z0v - ca * v1v + cb * v2)
        return carry

    stencil(za, ops, 0, emit)

    lane = lanes((8, COLS))

    def unpacked(src, l, row, s):
        start = (l * TALL + TOP + row) * 8
        early = src[pl.ds(start + s, 8, stride=8), :]
        late = src[pl.ds(start + SPECIES + s // 2, 8, stride=8), :]
        return jnp.where(
            lane < SEAM, turn(early, -HALO), turn(late, LATE - (s % 2) * HALF)
        )

    for s in range(SPECIES):
        for l in range(LAYERS):
            for row in range(0, ROWS, 8):
                k, rows = s * LAYERS + l, slice(row, row + 8)
                out_x[k, rows, :] = unpacked(px, l, row, s)
                out_r[k, rows, :] = planes[k, rows, :] - unpacked(pr, l, row, s)
                out_z[k, rows, :] = unpacked(pz, l, row, s)


def shape(*dims):
    return jax.ShapeDtypeStruct(dims, F32)


VMEM = pl.BlockSpec(memory_space=pltpu.VMEM)
SMEM = pl.BlockSpec(memory_space=pltpu.SMEM)
PARAMS = pltpu.CompilerParams(vmem_limit_bytes=20 * 1024 * 1024)


def run(kernel, outs, scratch, in_specs, cost, *args):
    return pl.pallas_call(
        kernel,
        out_shape=outs,
        in_specs=in_specs,
        out_specs=jax.tree.map(lambda _: VMEM, outs),
        scratch_shapes=scratch,
        compiler_params=PARAMS,
        cost_estimate=pl.CostEstimate(flops=cost, bytes_accessed=1 << 20, transcendentals=0),
    )(*args)


def shifts(axis, count):
    forward = [(i, (i + 1) % count) for i in range(count)]
    backward = [(target, source) for source, target in forward]
    return (functools.partial(lax.ppermute, axis_name=axis, perm=p) for p in (forward, backward))


def to_all(rows):
    got = lax.all_to_all(rows.reshape(TOTAL, -1, COLS), BOTH, 0, 0, tiled=True)
    return got.reshape(rows.shape)


def body(right_side, potential, capacity, diffusivity, material, coarse_map, coarse_inverse):
    b = right_side.reshape(FIELDS, ROWS, COLS)
    right, left = shifts("grp", N_GRP)
    down, up = shifts("gy", N_GY)

    packed = shape(GROUPS, ROWS, COLS)
    planes, to_low, to_high = run(
        pack_kernel,
        (shape(PLANES, ROWS, COLS), packed, packed),
        [],
        [VMEM] * 2,
        1 << 20,
        jnp.concatenate([b, potential, capacity]), material,
    )
    x_low, x_high = right(to_high), left(to_low)
    code = pltpu.VMEM((LAYERS, ROWS, COLS), F32)
    first, acc = run(
        own_kernel,
        (shape(TOTAL, COLS), shape(2 * COLS, COLS)),
        [pltpu.VMEM((FIELDS, ROWS, COLS), F32), code, code, code]
        + [pltpu.VMEM((24, COLS), F32), pltpu.VMEM((8, COLS), jnp.int32)],
        [SMEM] + [VMEM] * 3,
        1 << 20,
        diffusivity.T, planes, coarse_map, jnp.transpose(coarse_inverse, (1, 0, 2)),
    )

    strips = shape(PLANES + 2 * GROUPS, RHALO, COLS)
    to_low, to_high = run(
        rows_kernel, (strips, strips), [], [VMEM] * 3, 1 << 20, planes, x_low, x_high
    )
    first, to_low, to_high = lax.optimization_barrier((first, to_low, to_high))
    y_low, y_high = down(to_high), up(to_low)
    got, y_low, y_high = lax.optimization_barrier((to_all(first), y_low, y_high))

    packed = shape(LAYERS * TALL * 8, COLS)
    field = shape(FIELDS, ROWS, COLS)
    big = pltpu.VMEM(packed.shape, F32)
    hot = pltpu.VMEM((NC, MATS * TOTAL), jnp.bfloat16)
    double = pltpu.VMEM((2 * COLS, COLS), F32)
    values = pltpu.VMEM((3 * MATS * 8, COLS), F32)
    cap_w, mat_w, gy, gx, gz, scale, y0, acc, b_w = run(
        table_kernel,
        (packed,) * 7 + (shape(2 * COLS, COLS), packed),
        [big] * 2,
        [SMEM] + [VMEM] * 6,
        1 << 30,
        diffusivity.T, planes, x_low, x_high, y_low, y_high, acc,
    )
    hot_shape = jax.ShapeDtypeStruct((NC, MATS * TOTAL), jnp.bfloat16)
    near_shape = jax.ShapeDtypeStruct((NC, COLS), jnp.bfloat16)
    second, z0, w0, u, scatter, near_hot, turned = run(
        first_kernel,
        (shape(2 * TOTAL, COLS), packed, packed, packed, hot_shape, near_shape, shape(COLS, COLS)),
        [big] * 2 + [values, double],
        [VMEM] * 11,
        1 << 30,
        planes, got, cap_w, mat_w, gy, gx, gz, scale, y0, acc, b_w,
    )
    got2 = to_all(second)
    out = run(
        second_kernel,
        (field, field, field),
        [big] * 7 + [hot, double, values, values],
        [VMEM] * 14,
        1 << 30,
        planes, scatter, near_hot, turned, got2, cap_w, mat_w, gy, gx, gz, scale, z0, w0, u,
    )
    return tuple(o.reshape(right_side.shape) for o in out)


def solution(mesh):
    placed = (
        P(None, None, "gy", "grp"),
        P(None, "gy", "grp"),
        P(None, "gy", "grp"),
        P(),
        P(None, "gy", "grp"),
        P("gy", "grp", None),
        P(("grp", "gy"), None, None),
    )
    return jax.shard_map(
        body,
        mesh=mesh,
        in_specs=placed,
        out_specs=(P(None, None, "gy", "grp"),) * 3,
        check_vma=False,
    )
```

```python
import functools

import jax
import jax.numpy as jnp
from jax import lax
from jax.experimental import pallas as pl
from jax.experimental.pallas import tpu as pltpu
from jax.sharding import PartitionSpec as P

SPECIES = 5
LAYERS = 4
MATS = 4
FIELDS = SPECIES * LAYERS
PLANES = FIELDS + 3 * LAYERS
POT0, CAP0, MAT0 = FIELDS, FIELDS + LAYERS, FIELDS + 2 * LAYERS
ROWS = 32
COLS = 128
N_GRP = 4
N_GY = 32
TOTAL = N_GRP * N_GY
NC = 512
DAMPING = 2.0 / 3.0
BOTH = ("grp", "gy")

HALO = 12
GROUPS = LAYERS
RHALO = 16
TALL = ROWS + 2 * RHALO
TOP = RHALO
HALF = COLS // 2
LATE = COLS + HALO - HALF
SEAM = 96
F32 = jnp.float32

G_RW, G_RAU, G_S, G_CY, G_CX, G_MOM = 0, 4, 8, 14, 30, 46
ROW_CAP = 250
MAP_LANE = 20
INV_LANE = 24


def lanes(shape):
    return lax.broadcasted_iota(jnp.int32, shape, 1)


def subs(shape):
    return lax.broadcasted_iota(jnp.int32, shape, 0)


def pack_kernel(fields, mat, planes, to_low, to_high):
    planes[0:MAT0] = fields[...]
    planes[MAT0:PLANES] = mat[...].astype(F32)
    lane = lanes((ROWS, COLS))
    for g in range(GROUPS):
        low = jnp.zeros((ROWS, COLS), F32)
        high = jnp.zeros((ROWS, COLS), F32)
        for j in range(PLANES // LAYERS):
            v = planes[j * LAYERS + g]
            inside = (lane >= HALO * j) & (lane < HALO * (j + 1))
            low = jnp.where(inside, turn(v, HALO * j), low)
            high = jnp.where(inside, turn(v, HALO * j + HALO), high)
        to_low[g] = low
        to_high[g] = high


def turn(v, shift):
    shift = shift % v.shape[1]
    return v if shift == 0 else pltpu.roll(v, shift, 1)


def place(rows):
    n = rows.shape[0]
    total = jnp.sum(rows, axis=1, keepdims=True)
    spread = jnp.where(lanes((n, COLS)) == subs((n, COLS)), total, 0.0)
    return jnp.sum(spread, axis=0, keepdims=True)


def fold(v):
    return jnp.sum(v, axis=0, keepdims=True)


def harmonic(a, b):
    return 2.0 * a * b / (a + b)


def after(v, nxt, axis):
    first = lax.broadcasted_iota(jnp.int32, v.shape, axis) == 0
    return pltpu.roll(jnp.where(first, nxt, v), v.shape[axis] - 1, axis)


def power(m):
    p = jnp.where(m == 1.0, 2.0, 1.0)
    p = jnp.where(m == 2.0, 4.0, p)
    return jnp.where(m == 3.0, 8.0, p)


def own_kernel(diff, planes, cmap, inverse, out, acc, w, code_y, code_x, code_z, part, ids):
    part[...] = jnp.zeros(part.shape, F32)
    row = jnp.zeros((1, COLS), F32)
    for s in range(SPECIES):
        part[0:4, 0:SPECIES] = inverse[s]
        for k in range(4):
            row = row + turn(part[k : k + 1, :], INV_LANE + (k * SPECIES + s) * SPECIES)
    part[0:4, :] = jnp.zeros((4, COLS), F32)
    ids[...] = jnp.zeros(ids.shape, jnp.int32)
    ids[0:1, 0:MATS] = cmap[0]
    q = ids[0:1, :]
    row = row + turn(((q & 3) * TOTAL + (q >> 2)).astype(F32), MAP_LANE)
    for s in range(SPECIES):
        for m in range(MATS):
            total = jnp.zeros((ROWS, COLS), F32)
            for l in range(LAYERS):
                total = total + jnp.where(planes[MAT0 + l] == m, planes[s * LAYERS + l], 0.0)
            part[m * SPECIES + s : m * SPECIES + s + 1, :] = fold(total)
    out[...] = jnp.broadcast_to(row + place(part[...]), (TOTAL, COLS))

    acc[...] = jnp.zeros(acc.shape, F32)
    lane, sub = lanes((8, COLS)), subs((8, COLS))
    tiles = [8 * t for t in range(ROWS // 8)]
    for r in tiles:
        here = pl.ds(r, 8)
        for l in range(LAYERS):
            m = planes[MAT0 + l, here, :]
            is1, is2, is3 = m == 1.0, m == 2.0, m == 3.0
            down = jnp.exp(-0.5 * planes[POT0 + l, here, :])
            up = jnp.exp(0.5 * planes[POT0 + l, here, :])
            drift = (down, up, down * down, up * up, down)
            for s in range(SPECIES):
                d = jnp.where(is1, diff[1, s], diff[0, s])
                d = jnp.where(is2, diff[2, s], d)
                d = jnp.where(is3, diff[3, s], d)
                w[s * LAYERS + l, here, :] = d * drift[s]
            p = power(m)
            if r == tiles[-1]:
                code = jnp.where(sub == 7, 0.0, p + power(after(m, m, 0)))
            else:
                code = p + power(after(m, planes[MAT0 + l, pl.ds(r + 8, 8), :], 0))
            code_y[l, here, :] = code
            code_x[l, here, :] = jnp.where(lane == COLS - 1, 0.0, p + power(turn(m, -1)))
            if l + 1 < LAYERS:
                code_z[l, here, :] = p + power(planes[MAT0 + l + 1, here, :])

    @pl.loop(0, SPECIES)
    def _(s):
        pairs = [jnp.zeros((8, COLS), F32)] * 6
        codes = (3.0, 5.0, 9.0, 6.0, 10.0, 12.0)
        for r in tiles:
            here = pl.ds(r, 8)
            for l in range(LAYERS):
                k = s * LAYERS + l
                c = w[k, here, :]
                nxt = c if r == tiles[-1] else w[k, pl.ds(r + 8, 8), :]
                kinds = [
                    (code_y[l, here, :], harmonic(c, after(c, nxt, 0))),
                    (code_x[l, here, :], harmonic(c, turn(c, -1))),
                ]
                if l + 1 < LAYERS:
                    kinds.append((code_z[l, here, :], 0.5 * harmonic(c, w[k + 1, here, :])))
                for code, edge in kinds:
                    for i in range(6):
                        pairs[i] = pairs[i] + jnp.where(code == codes[i], edge, 0.0)
        for i in range(6):
            acc[pl.ds((G_S + i) * SPECIES + s, 1), :] = fold(pairs[i])

    for i in range(MATS):
        total = jnp.zeros((ROWS, COLS), F32)
        for l in range(LAYERS):
            total = total + jnp.where(planes[MAT0 + l] == i, planes[CAP0 + l], 0.0)
        acc[ROW_CAP + i : ROW_CAP + i + 1, :] = fold(total)


def rows_kernel(planes, from_low, from_high, to_low, to_high):
    for k in range(PLANES):
        to_low[k] = planes[k, :RHALO]
        to_high[k] = planes[k, ROWS - RHALO :]
    for g in range(GROUPS):
        for i, part in enumerate((from_low, from_high)):
            k = PLANES + i * GROUPS + g
            to_low[k] = part[g, :RHALO]
            to_high[k] = part[g, ROWS - RHALO :]


def at(l, y):
    if isinstance(y, int):
        return pl.ds((y + l * TALL) * 8, 8)
    return pl.ds(pl.multiple_of((y + l * TALL) * 8, 8), 8)


class Later:
    def __init__(self):
        self.held = []

    def put(self, ref, where, value):
        self.held.append((ref, where, value))

    def flush(self):
        for ref, where, value in self.held:
            ref[where, :] = value
        self.held = []


LATER = Later()
BLOCK = 0


def each_row(first, count, step, carry=()):
    size = BLOCK if BLOCK and count % BLOCK == 0 else 4
    if BLOCK == 0:
        for r in range(count):
            carry = step(first + r, carry)
            LATER.flush()
        return carry

    def block(i, carry):
        for r in range(size):
            carry = step(first + size * i + r, carry)
        LATER.flush()
        return carry

    return lax.fori_loop(0, count // size, block, carry)


def stencil(src, ops, wide, emit, carry=()):
    cap, gy, gx, gz = ops[:4]
    first = TOP - wide
    span = range(LAYERS)
    now = [src[at(l, first), :] for l in span]
    flux = [gy[at(l, first - 1), :] * (src[at(l, first - 1), :] - now[l]) for l in span]

    def step(y, carry):
        now, flux, carry = carry
        nxt, out_flux = [], []
        flux_z = None
        for l in span:
            here = at(l, y)
            u = now[l]
            above = src[at(l, y + 1), :]
            flux_x = gx[here, :] * (u - turn(u, -1))
            flux_y = gy[here, :] * (u - above)
            out = cap[here, :] * u + (flux_x - turn(flux_x, 1)) + (flux_y - flux[l])
            if flux_z is not None:
                out = out - flux_z
            if l + 1 < LAYERS:
                flux_z = gz[here, :] * (u - now[l + 1])
                out = out + flux_z
            nxt.append(above)
            out_flux.append(flux_y)
            carry = emit(l, y, u, out, carry)
        return nxt, out_flux, carry

    return each_row(first, ROWS + 2 * wide, step, (now, flux, carry))[2]


def sweep(src, resid, dst, ops, wide):
    scale = ops[4]

    def emit(l, y, u, out, carry):
        here = at(l, y)
        LATER.put(dst, here, u + scale[here, :] * (resid[here, :] - out))
        return carry

    stencil(src, ops, wide, emit)


def image(src, dst, ops, wide):
    def emit(l, y, u, out, carry):
        LATER.put(dst, at(l, y), out)
        return carry

    stencil(src, ops, wide, emit)


def start_sweep(resid, dst, scale, wide):
    def step(y, carry):
        for l in range(LAYERS):
            here = at(l, y)
            LATER.put(dst, here, scale[here, :] * resid[here, :])
        return carry

    each_row(TOP - wide, ROWS + 2 * wide, step)


def used(tile):
    lane, sub = lanes(tile.shape), subs(tile.shape)
    early = (sub < SPECIES) & (lane >= HALO) & (lane < HALO + SEAM)
    place_in = lane & (HALF - 1)
    late = (sub >= SPECIES) & (place_in >= SEAM - LATE) & (place_in < COLS - LATE)
    late = late & ((sub < 7) | (lane < HALF))
    return jnp.where(early | late, tile, 0.0)


def by_species(tile):
    lane, sub = lanes(tile.shape), subs(tile.shape)
    left = lane < HALF
    out = tile
    out = out + jnp.where((sub == 0) & left, pltpu.roll(tile, 3, 0), 0.0)
    pick = ((sub == 1) & ~left) | ((sub == 2) & left)
    out = out + jnp.where(pick, pltpu.roll(tile, 4, 0), 0.0)
    pick = ((sub == 3) & ~left) | ((sub == 4) & left)
    out = out + jnp.where(pick, pltpu.roll(tile, 5, 0), 0.0)
    return out[:SPECIES]


def keep(acc, group, tile):
    acc[group * SPECIES : (group + 1) * SPECIES, :] = by_species(tile)


def split3(x):
    hi = x.astype(jnp.bfloat16)
    rest = x - hi.astype(F32)
    mid = rest.astype(jnp.bfloat16)
    lo = (rest - mid.astype(F32)).astype(jnp.bfloat16)
    return jnp.concatenate([hi, mid, lo], axis=0)


def exact_dot(x, onehot):
    n = x.shape[0]
    y = jnp.dot(
        jnp.concatenate([split3(x)], axis=0), onehot, preferred_element_type=F32
    )
    return y[:n] + y[n : 2 * n] + y[2 * n :]


def build_scatter(got, onehot):
    for m in range(MATS):
        col = jnp.broadcast_to(got[:, MAP_LANE + m : MAP_LANE + m + 1], (TOTAL, COLS))
        for k in range(4):
            target = (lanes((TOTAL, COLS)) + k * COLS).astype(F32)
            onehot[m * TOTAL : (m + 1) * TOTAL, k * COLS : (k + 1) * COLS] = jnp.where(
                col == target, 1.0, 0.0
            ).astype(jnp.bfloat16)


def build_gather(turned, onehot):
    for m in range(MATS):
        row = jnp.broadcast_to(turned[MAP_LANE + m : MAP_LANE + m + 1, :], (COLS, TOTAL))
        for k in range(4):
            target = (subs((COLS, TOTAL)) + k * COLS).astype(F32)
            onehot[k * COLS : (k + 1) * COLS, m * TOTAL : (m + 1) * TOTAL] = jnp.where(
                row == target, 1.0, 0.0
            ).astype(jnp.bfloat16)


def build_near(got, onehot):
    gx, gy = lax.axis_index("grp"), lax.axis_index("gy")
    lane = lanes((1, COLS))
    row = jnp.full((1, COLS), -1.0, F32)
    for iy in range(3):
        y = lax.rem(gy + (N_GY - 1 + iy), N_GY)
        for ix in range(3):
            x = jnp.clip(gx + (ix - 1), 0, N_GRP - 1)
            region = iy * 3 + ix
            here = got[pl.ds(x * N_GY + y, 1), :]
            inside = (lane >= region * MATS) & (lane < (region + 1) * MATS)
            row = jnp.where(inside, turn(here, region * MATS - MAP_LANE), row)
    for k in range(4):
        target = (subs((COLS, COLS)) + k * COLS).astype(F32)
        onehot[k * COLS : (k + 1) * COLS, :] = jnp.where(
            jnp.broadcast_to(row, (COLS, COLS)) == target, 1.0, 0.0
        ).astype(jnp.bfloat16)


def coarse_solve(sums, turned, scatter):
    res = exact_dot(sums, scatter[...])
    parts = []
    for k in range(4):
        total = None
        for t in range(SPECIES):
            start = INV_LANE + k * SPECIES * SPECIES + t * SPECIES
            term = turned[start : start + 8, :] * res[t : t + 1, k * COLS : (k + 1) * COLS]
            total = term if total is None else total + term
        parts.append(total)
    sol = jnp.concatenate(parts, axis=1)
    return jnp.where(subs(sol.shape) < SPECIES, sol, 0.0)


def local_sums(turned, group):
    x = jnp.concatenate(
        [turned[(group + m) * SPECIES : (group + m) * SPECIES + 8, :] for m in range(MATS)], axis=1
    )
    return jnp.where(subs(x.shape) < SPECIES, x, 0.0)


def spread_values(near, values):
    lane, sub = lanes((8, COLS)), subs((8, COLS))

    def arrange(a, b, c):
        row = lambda s: jnp.broadcast_to(near[s : s + 1, :], (8, COLS))
        out = jnp.where(sub == 5, row(a), near)
        return jnp.where(sub == 7, row(c), jnp.where(sub == 6, row(b), out))

    left, right = arrange(0, 2, 4), arrange(1, 3, 4)
    early = sub < SPECIES
    for iy in range(3):
        for m in range(MATS):
            column = lambda v, ix: jnp.broadcast_to(
                v[:, (iy * 3 + ix) * MATS + m : (iy * 3 + ix) * MATS + m + 1], (8, COLS)
            )
            first = jnp.where(early & (lane < HALO), column(left, 0), column(left, 1))
            first = jnp.where(~early & (lane >= COLS - LATE), column(left, 2), first)
            second = jnp.where(lane >= HALF + COLS - LATE, column(right, 2), column(right, 1))
            values[(iy * MATS + m) * 8 : (iy * MATS + m + 1) * 8, :] = jnp.where(
                early | (lane < HALF), first, second
            )


def coarse_rows(values, mat, wide, emit):
    for iy, first, count in ((0, TOP - wide, wide), (1, TOP, ROWS), (2, TOP + ROWS, wide)):
        if count == 0:
            continue
        v = [values[(iy * MATS + m) * 8 : (iy * MATS + m + 1) * 8, :] for m in range(MATS)]

        def step(y, carry):
            for l in range(LAYERS):
                emit(l, y, coarse_pick(v, mat[at(l, y), :]))
            return carry

        each_row(first, count, step)


def coarse_pick(v, m):
    out = jnp.where(m == 1.0, v[1], v[0])
    out = jnp.where(m == 2.0, v[2], out)
    return jnp.where(m == 3.0, v[3], out)


def table_kernel(
    diff, planes, x_low, x_high, y_low, y_high, acc_in,
    cap_w, mat_w, gy, gx, gz, scale, y0, acc, b_w,
    w, za,
):
    lane, sub = lanes((8, COLS)), subs((8, COLS))
    left = lane < HALF

    pairs = ((0, 1), (2, 3), (4, 4))
    d_late = [
        [jnp.where(left, diff[m, a], diff[m, b]) for m in range(MATS)] for a, b in pairs
    ]

    def choose(v, is1, is2, is3):
        return jnp.where(is3, v[3], jnp.where(is2, v[2], jnp.where(is1, v[1], v[0])))

    def fill(own, low, high, l, row, y):
        rows = pl.ds(row, 8)

        def both(kind):
            v = own[kind * LAYERS + l, rows, :]
            early = jnp.where(lane < HALO, turn(low[l, rows, :], -HALO * kind), turn(v, HALO))
            beyond = turn(high[l, rows, :], COLS - LATE - HALO * kind)
            return early, jnp.where(lane < COLS - LATE, turn(v, -LATE), beyond)

        def put(dst, s, v):
            dst[pl.ds((y + l * TALL) * 8 + s, 8, stride=8), :] = v

        late_b = []
        for s in range(SPECIES):
            early, late = both(s)
            put(b_w, s, early)
            late_b.append(late)
        for i, (a, b) in enumerate(pairs):
            put(b_w, SPECIES + i, jnp.where(left, late_b[a], turn(late_b[b], HALF)))
        for dst, kind in ((cap_w, SPECIES + 1), (mat_w, SPECIES + 2)):
            early, late = both(kind)
            late = jnp.where(left, late, turn(late, HALF))
            for s in range(8):
                put(dst, s, early if s < SPECIES else late)
        m_early, m_late = early, late
        early, late = both(SPECIES)
        late = jnp.where(left, late, turn(late, HALF))
        is_m = [m_early == float(m) for m in (1, 2, 3)]
        down, up = jnp.exp(-0.5 * early), jnp.exp(0.5 * early)
        drift = (down, up, down * down, up * up, down)
        for s in range(SPECIES):
            put(w, s, choose([diff[m, s] for m in range(MATS)], *is_m) * drift[s])
        is_m = [m_late == float(m) for m in (1, 2, 3)]
        down, up = jnp.exp(-0.5 * late), jnp.exp(0.5 * late)
        mixed = jnp.where(left, down, up)
        drift = (mixed, mixed * mixed, down)
        for i in range(3):
            put(w, SPECIES + i, choose(d_late[i], *is_m) * drift[i])

    edge_low = (y_low.at[PLANES : PLANES + GROUPS], y_low.at[PLANES + GROUPS : PLANES + 2 * GROUPS])
    edge_high = (y_high.at[PLANES : PLANES + GROUPS], y_high.at[PLANES + GROUPS : PLANES + 2 * GROUPS])

    @pl.loop(0, LAYERS)
    def _(l):
        for row in range(0, RHALO, 8):
            fill(y_low, *edge_low, l, row, row)

    @pl.loop(0, LAYERS)
    def _(l):
        for row in range(0, ROWS, 8):
            fill(planes, x_low, x_high, l, row, TOP + row)

    @pl.loop(0, LAYERS)
    def _(l):
        for row in range(0, RHALO, 8):
            fill(y_high, *edge_high, l, row, TOP + ROWS + row)

    me_x = lax.axis_index("grp")
    closed = ((sub >= SPECIES) & ((lane & (HALF - 1)) == COLS - 1 - LATE) & (me_x == N_GRP - 1)) | (
        (sub < SPECIES) & (lane == HALO - 1) & (me_x == 0)
    )
    span = range(LAYERS)
    first = TOP - 12

    def edge_step(y, carry):
        now, edge_y = carry
        nxt, out_y = [], []
        ez_below = None
        for l in span:
            here = at(l, y)
            c = now[l]
            above = w[at(l, y + 1), :]
            ey = harmonic(c, above)
            ex = jnp.where(closed, 0.0, harmonic(c, turn(c, -1)))
            LATER.put(gy, here, ey)
            LATER.put(gx, here, ex)
            d = cap_w[here, :] + ey + edge_y[l] + ex + turn(ex, 1)
            if ez_below is not None:
                d = d + ez_below
            if l + 1 < LAYERS:
                ez_below = 0.5 * harmonic(c, now[l + 1])
                LATER.put(gz, here, ez_below)
                d = d + ez_below
            LATER.put(scale, here, DAMPING / d)
            nxt.append(above)
            out_y.append(ey)
        return nxt, out_y

    now = [w[at(l, first), :] for l in span]
    edge_y = [harmonic(w[at(l, first - 1), :], now[l]) for l in span]
    each_row(first, ROWS + 24, edge_step, (now, edge_y))

    ops = (cap_w, gy, gx, gz, scale)
    start_sweep(b_w, za, scale, 12)
    sweep(za, b_w, y0, ops, 10)
    sweep(y0, b_w, za, ops, 10)
    sweep(za, b_w, y0, ops, 8)

    acc[...] = acc_in[...]
    zero = jnp.zeros((8, COLS), F32)
    last = TOP + ROWS - 1
    cy = [zero] * 16
    for l in span:
        code = mat_w[at(l, last), :] * 4.0 + mat_w[at(l, last + 1), :]
        edge = gy[at(l, last), :]
        for i in range(16):
            cy[i] = cy[i] + jnp.where(code == float(i), edge, 0.0)
    for i in range(16):
        keep(acc, G_CY + i, used(cy[i]))

    place_in = lane & (HALF - 1)

    targets = [place_in == COLS - 1 - LATE - l for l in span]
    cross = []
    for row in range(TOP, TOP + ROWS, 8):
        def strip(ref, s, change):
            tile = zero - 1.0
            for l in span:
                v = change(ref[pl.ds((l * TALL + row) * 8 + s, 8, stride=8), :])
                tile = jnp.where(targets[l], turn(v, -l), tile)
            return tile

        code = strip(mat_w, SPECIES, lambda m: m * 4.0 + turn(m, -1))
        cross.append((code, [strip(gx, SPECIES + i, lambda v: v) for i in range(3)]))
    for k in range(16):
        for i, (a, b) in enumerate(pairs):
            total = zero
            for code, sides in cross:
                total = total + jnp.where(code == float(k), sides[i], 0.0)
            total = fold(total)
            r = (G_CX + k) * SPECIES
            acc[r + a : r + a + 1, :] = jnp.where(left[0:1], total, 0.0)
            if b != a:
                acc[r + b : r + b + 1, :] = jnp.where(left[0:1], 0.0, total)


def first_kernel(
    planes, got, cap_w, mat_w, gy, gx, gz, scale, y0, acc_in, b_w,
    second, z0, w0, u_out, scatter, near_hot, turned,
    za, zb, values, acc,
):
    ops = (cap_w, gy, gx, gz, scale)

    turned[...] = got[...].T
    build_scatter(got, scatter)
    build_near(got, near_hot)
    sol = coarse_solve(local_sums(turned, 0), turned, scatter)
    spread_values(exact_dot(sol, near_hot[...]), values)

    def add_coarse(l, y, c):
        LATER.put(z0, at(l, y), y0[at(l, y), :] + c)

    coarse_rows(values, mat_w, 8, add_coarse)
    image(z0, w0, ops, 8)
    start_sweep(w0, za, scale, 8)
    sweep(za, w0, zb, ops, 6)
    sweep(zb, w0, za, ops, 6)
    sweep(za, w0, u_out, ops, 4)

    acc[...] = acc_in[...]

    def emit(l, y, u, au, carry):
        rw, rau, mom = carry
        here = at(l, y)
        m = mat_w[here, :]
        wv, zv, bv = w0[here, :], z0[here, :], b_w[here, :]
        is_m = [m == float(i) for i in range(MATS)]
        rw = [rw[i] + jnp.where(is_m[i], wv, 0.0) for i in range(MATS)]
        rau = [rau[i] + jnp.where(is_m[i], au, 0.0) for i in range(MATS)]
        mom = [mom[0] + bv * zv, mom[1] + zv * wv, mom[2] + wv * u, mom[3] + u * au]
        return rw, rau, mom

    zero = jnp.zeros((8, COLS), F32)
    sums = stencil(u_out, ops, 0, emit, ([zero] * 4, [zero] * 4, [zero] * 4))
    for group, tiles in zip((G_RW, G_RAU, G_MOM), sums):
        for i, v in enumerate(tiles):
            keep(acc, group + i, used(v))

    even = lax.rem(subs((2 * TOTAL, COLS)), 2) == 0
    second[...] = jnp.where(even, place(acc[0:COLS, :]), place(acc[COLS : 2 * COLS, :]))


def next_y(x):
    y = lax.rem(lanes(x.shape), N_GY)
    return jnp.where(y == N_GY - 1, turn(x, N_GY - 1), turn(x, -1))


def prev_y(x):
    y = lax.rem(lanes(x.shape), N_GY)
    return jnp.where(y == 0, turn(x, -(N_GY - 1)), turn(x, 1))


def total_of(x):
    return jnp.sum(jnp.sum(x, axis=0, keepdims=True), axis=1, keepdims=True)


def second_kernel(
    planes, scatter, near_hot, turned, got2, cap, mat, gy, gx, gz, scale, z0, w0, u,
    out_x, out_r, out_z,
    v1, w1, za, zb, px, pr, pz, gather, turned2, values, values2,
):
    turned2[0:COLS, :] = got2[pl.ds(0, TOTAL, stride=2), :].T
    turned2[COLS : 2 * COLS, :] = got2[pl.ds(1, TOTAL, stride=2), :].T
    build_gather(turned, gather)

    sums_w = local_sums(turned2, G_RW)
    sol = coarse_solve(sums_w, turned, scatter)
    spread_values(exact_dot(sol, near_hot[...]), values)
    c_all = exact_dot(sol, gather[...])
    c = [c_all[:, m * TOTAL : (m + 1) * TOTAL] for m in range(MATS)]

    def rows5(group):
        return turned2[group * SPECIES : group * SPECIES + 8, :]

    live = subs((8, TOTAL)) < SPECIES
    bc = [turned2[ROW_CAP + m : ROW_CAP + m + 1, :] * c[m] for m in range(MATS)]
    n = 0
    for i in range(MATS):
        for j in range(i + 1, MATS):
            f = rows5(G_S + n) * (c[i] - c[j])
            bc[i] = bc[i] + f
            bc[j] = bc[j] - f
            n += 1
    c_y = [next_y(v) for v in c]
    c_x = [turn(v, -N_GY) for v in c]
    back_y = [jnp.zeros((8, TOTAL), F32)] * MATS
    back_x = [jnp.zeros((8, TOTAL), F32)] * MATS
    for i in range(MATS):
        for j in range(MATS):
            f = rows5(G_CY + 4 * i + j) * (c[i] - c_y[j])
            bc[i] = bc[i] + f
            back_y[j] = back_y[j] + f
            f = rows5(G_CX + 4 * i + j) * (c[i] - c_x[j])
            bc[i] = bc[i] + f
            back_x[j] = back_x[j] + f
    for j in range(MATS):
        bc[j] = jnp.where(live, bc[j] - prev_y(back_y[j]) - turn(back_x[j], N_GY), 0.0)
    bc_all = jnp.concatenate(bc, axis=1)
    sums_au = local_sums(turned2, G_RAU)
    sol2 = coarse_solve(sums_au + bc_all, turned, scatter)
    spread_values(exact_dot(sol2, near_hot[...]), values2)

    def moment(i):
        return total_of(jnp.where(live, rows5(G_MOM + i), 0.0))

    m0, m1 = moment(0), moment(1)
    m2 = moment(2) + total_of(sums_w * c_all)
    m3 = moment(3) + total_of((2.0 * sums_au + bc_all) * c_all)
    a0 = m0 / m1
    rz1 = m0 - 2.0 * a0 * m1 + a0 * a0 * m2
    g = 1.0 + rz1 / m0
    a1 = rz1 / (g * g * m1 - 2.0 * a0 * g * m2 + a0 * a0 * m3)
    ca = jnp.broadcast_to(a0 + a1 * g, (8, COLS))
    cb = jnp.broadcast_to(a1 * a0, (8, COLS))

    ops = (cap, gy, gx, gz, scale)

    def add_coarse(l, y, c):
        LATER.put(v1, at(l, y), u[at(l, y), :] + c)

    coarse_rows(values, mat, 4, add_coarse)
    image(v1, w1, ops, 4)
    start_sweep(w1, za, scale, 4)
    sweep(za, w1, zb, ops, 2)
    sweep(zb, w1, za, ops, 2)
    own_values = [values2[(MATS + m) * 8 : (MATS + m + 1) * 8, :] for m in range(MATS)]

    def emit(l, y, z, out, carry):
        here = at(l, y)
        w1v, v1v = w1[here, :], v1[here, :]
        z0v, w0v = z0[here, :], w0[here, :]
        v2 = z + scale[here, :] * (w1v - out) + coarse_pick(own_values, mat[here, :])
        LATER.put(px, here, ca * z0v - cb * v1v)
        LATER.put(pr, here, ca * w0v - cb * w1v)
        LATER.put(pz, here, z0v - ca * v1v + cb * v2)
        return carry

    stencil(za, ops, 0, emit)

    lane = lanes((8, COLS))

    def unpacked(src, l, row, s):
        start = (l * TALL + TOP + row) * 8
        early = src[pl.ds(start + s, 8, stride=8), :]
        late = src[pl.ds(start + SPECIES + s // 2, 8, stride=8), :]
        return jnp.where(
            lane < SEAM, turn(early, -HALO), turn(late, LATE - (s % 2) * HALF)
        )

    for s in range(SPECIES):
        for l in range(LAYERS):
            for row in range(0, ROWS, 8):
                k, rows = s * LAYERS + l, slice(row, row + 8)
                out_x[k, rows, :] = unpacked(px, l, row, s)
                out_r[k, rows, :] = planes[k, rows, :] - unpacked(pr, l, row, s)
                out_z[k, rows, :] = unpacked(pz, l, row, s)


def shape(*dims):
    return jax.ShapeDtypeStruct(dims, F32)


VMEM = pl.BlockSpec(memory_space=pltpu.VMEM)
SMEM = pl.BlockSpec(memory_space=pltpu.SMEM)
PARAMS = pltpu.CompilerParams(vmem_limit_bytes=20 * 1024 * 1024)


def run(kernel, outs, scratch, in_specs, cost, *args):
    return pl.pallas_call(
        kernel,
        out_shape=outs,
        in_specs=in_specs,
        out_specs=jax.tree.map(lambda _: VMEM, outs),
        scratch_shapes=scratch,
        compiler_params=PARAMS,
        cost_estimate=pl.CostEstimate(flops=cost, bytes_accessed=1 << 20, transcendentals=0),
    )(*args)


def shifts(axis, count):
    forward = [(i, (i + 1) % count) for i in range(count)]
    backward = [(target, source) for source, target in forward]
    return (functools.partial(lax.ppermute, axis_name=axis, perm=p) for p in (forward, backward))


def to_all(rows):
    got = lax.all_to_all(rows.reshape(TOTAL, -1, COLS), BOTH, 0, 0, tiled=True)
    return got.reshape(rows.shape)


def body(right_side, potential, capacity, diffusivity, material, coarse_map, coarse_inverse):
    b = right_side.reshape(FIELDS, ROWS, COLS)
    right, left = shifts("grp", N_GRP)
    down, up = shifts("gy", N_GY)

    packed = shape(GROUPS, ROWS, COLS)
    planes, to_low, to_high = run(
        pack_kernel,
        (shape(PLANES, ROWS, COLS), packed, packed),
        [],
        [VMEM] * 2,
        1 << 20,
        jnp.concatenate([b, potential, capacity]), material,
    )
    x_low, x_high = right(to_high), left(to_low)
    code = pltpu.VMEM((LAYERS, ROWS, COLS), F32)
    first, acc = run(
        own_kernel,
        (shape(TOTAL, COLS), shape(2 * COLS, COLS)),
        [pltpu.VMEM((FIELDS, ROWS, COLS), F32), code, code, code]
        + [pltpu.VMEM((24, COLS), F32), pltpu.VMEM((8, COLS), jnp.int32)],
        [SMEM] + [VMEM] * 3,
        1 << 20,
        diffusivity.T, planes, coarse_map, jnp.transpose(coarse_inverse, (1, 0, 2)),
    )

    strips = shape(PLANES + 2 * GROUPS, RHALO, COLS)
    to_low, to_high = run(
        rows_kernel, (strips, strips), [], [VMEM] * 3, 1 << 20, planes, x_low, x_high
    )
    first, to_low, to_high = lax.optimization_barrier((first, to_low, to_high))
    y_low, y_high = down(to_high), up(to_low)
    got, y_low, y_high = lax.optimization_barrier((to_all(first), y_low, y_high))

    packed = shape(LAYERS * TALL * 8, COLS)
    field = shape(FIELDS, ROWS, COLS)
    big = pltpu.VMEM(packed.shape, F32)
    hot = pltpu.VMEM((NC, MATS * TOTAL), jnp.bfloat16)
    double = pltpu.VMEM((2 * COLS, COLS), F32)
    values = pltpu.VMEM((3 * MATS * 8, COLS), F32)
    cap_w, mat_w, gy, gx, gz, scale, y0, acc, b_w = run(
        table_kernel,
        (packed,) * 7 + (shape(2 * COLS, COLS), packed),
        [big] * 2,
        [SMEM] + [VMEM] * 6,
        1 << 30,
        diffusivity.T, planes, x_low, x_high, y_low, y_high, acc,
    )
    hot_shape = jax.ShapeDtypeStruct((NC, MATS * TOTAL), jnp.bfloat16)
    near_shape = jax.ShapeDtypeStruct((NC, COLS), jnp.bfloat16)
    second, z0, w0, u, scatter, near_hot, turned = run(
        first_kernel,
        (shape(2 * TOTAL, COLS), packed, packed, packed, hot_shape, near_shape, shape(COLS, COLS)),
        [big] * 2 + [values, double],
        [VMEM] * 11,
        1 << 30,
        planes, got, cap_w, mat_w, gy, gx, gz, scale, y0, acc, b_w,
    )
    got2 = to_all(second)
    out = run(
        second_kernel,
        (field, field, field),
        [big] * 7 + [hot, double, values, values],
        [VMEM] * 14,
        1 << 30,
        planes, scatter, near_hot, turned, got2, cap_w, mat_w, gy, gx, gz, scale, z0, w0, u,
    )
    return tuple(o.reshape(right_side.shape) for o in out)


def solution(mesh):
    placed = (
        P(None, None, "gy", "grp"),
        P(None, "gy", "grp"),
        P(None, "gy", "grp"),
        P(),
        P(None, "gy", "grp"),
        P("gy", "grp", None),
        P(("grp", "gy"), None, None),
    )
    return jax.shard_map(
        body,
        mesh=mesh,
        in_specs=placed,
        out_specs=(P(None, None, "gy", "grp"),) * 3,
        check_vma=False,
    )
```
